128 devices in a mesh: rows: 16 (over z, x_hi, core), lat: 8 (over y, x_lo).
Axes of the slice: x: 4 (x_hi: 2, x_lo: 2; x = x_hi * 2 + x_lo), y: 4, z: 4, core: 2. Of those that a mesh axis runs over, the one named last changes fastest.
Arguments:
- batch: bfloat16 [6144, 4608], P('rows'), may hold values from -6 to 6
- next_acts: bfloat16 [6144, 4608], P(('rows', 'lat')), may hold values from -6 to 6
- row_source: int32 [6144], replicated, may hold values from 0 to 6143, as said below
- enc_weight: bfloat16 [4608, 4096], P('rows', 'lat'), may hold values from -0.09375 to 0.09375
- dec_weight: bfloat16 [4096, 4608], P('lat', 'rows'), may hold values from -0.09375 to 0.09375
- enc_bias: float32 [4096], P('lat'), may hold values from -0.8 to 0.2
- dec_bias: float32 [4608], replicated, may hold values from -3 to 3
- enc_first: bfloat16 [4608, 4096], P('rows', 'lat'), may hold values from -0.011962891 to 0.011962891
- enc_second: bfloat16 [4608, 4096], P('rows', 'lat'), may hold values from 4.9825758e-08 to 4.991889e-07
- dec_first: bfloat16 [4096, 4608], P('lat', 'rows'), may hold values from -0.011962891 to 0.011962891
- dec_second: bfloat16 [4096, 4608], P('lat', 'rows'), may hold values from 4.9825758e-08 to 4.991889e-07
Outputs:
- next_batch: bfloat16 [6144, 4608], P('rows')
- latent_codes: bfloat16 [6144, 4096], P('rows', 'lat')
- recon_error: bfloat16 [6144, 4608], P('rows', 'lat')
- new_enc_first: bfloat16 [4608, 4096], P('rows', 'lat')
- new_enc_second: bfloat16 [4608, 4096], P('rows', 'lat')
- enc_update: bfloat16 [4608, 4096], P('rows', 'lat')
- new_dec_first: bfloat16 [4096, 4608], P('lat', 'rows')
- new_dec_second: bfloat16 [4096, 4608], P('lat', 'rows')
- dec_update: bfloat16 [4096, 4608], P('lat', 'rows')
The draws below stay inside these ranges and needn't reach their ends.
Inputs may be any that keep to these rules, and one draw needn't show every extreme that they name: row_source is a permutation of the 6144 rows. Of the 48 rows of next_acts that one device holds, exactly 3 go to each group of 384 consecutive rows of next_batch.
All inputs are finite; a program needn't handle non-finite values.
Results may differ from the reference program's by a relative error of at most 0.035.
Values may be sent and summed in bfloat16 or wider, within the bound.
A program may use at most 128 MiB of HBM per device.

```python
import math
import jax
import jax.numpy as jnp
from jax import lax

D = 4608
R_DEV = 384
LATENTS = 4096
TOKENS = 6144
SRC_DEV = 48
PER_PEER = 3
N_ROWS = 16


def draw_row_source(key, part):
    key = jax.random.fold_in(key, 7)
    groups = TOKENS // R_DEV
    devices = TOKENS // SRC_DEV
    slot_keys = jax.random.split(jax.random.fold_in(key, 1), groups)
    slot_table = jax.vmap(lambda sub_key: jax.random.permutation(sub_key, R_DEV))(slot_keys)
    owners = slot_table // PER_PEER
    rank_within = slot_table % PER_PEER
    local_keys = jax.random.split(jax.random.fold_in(key, 2), devices)
    local_table = jax.vmap(lambda sub_key: jax.random.permutation(sub_key, SRC_DEV))(local_keys)
    group_ids = jnp.arange(groups, dtype=jnp.int32)[:, None]
    chosen = local_table[owners, group_ids * PER_PEER + rank_within]
    return (owners * SRC_DEV + chosen).reshape(TOKENS).astype(jnp.int32)


def raised(result, key, source, target, shards_of, factor):
    def block_of(position):
        return (jnp.arange(result.shape[position]) // (result.shape[position] // shards_of)).reshape((-1,) + (1,) * (result.ndim - 1 - position))

    one_side = jax.random.permutation(key, shards_of)[block_of(target)]
    other_side = (block_of(target) + shards_of // 2) % shards_of
    return jnp.where((block_of(source) == one_side) | (block_of(source) == other_side), factor * result, result)


def level_of(rng, extent, shards, low, high):
    factor_of = 1.0
    for dim, blocks in shards:
        steps = jax.random.uniform(jax.random.fold_in(jax.random.fold_in(rng, 6), dim), (blocks,), jnp.float32, low / len(shards), high / len(shards))
        factor_of = factor_of * jnp.repeat(jnp.exp(steps), extent[dim] // blocks).reshape((-1,) + (1,) * (len(extent) - 1 - dim))
    return factor_of


def bell_draw(own_key, extent, deviation, limit, shards=(), kind=jnp.bfloat16):
    drawn = jax.random.normal(own_key, extent, jnp.float32) * deviation
    if len(shards) > 0:
        drawn = level_of(own_key, extent, shards, -0.22, 0.18) * drawn
    return jnp.clip(drawn, min=-limit, max=limit).astype(kind)


def noise_with(key, dims, width, limit, shards, heavy, kind=jnp.bfloat16):
    result = width * jax.random.normal(key, dims, jnp.float32)
    if shards:
        result = result * level_of(key, dims, shards, -0.22, 0.18)
    return jnp.clip(raised(result, jax.random.fold_in(key, 3), *heavy), -limit, limit).astype(kind)


def setup_inputs(seed: int = 0) -> dict:
    arg_keys = jax.random.split(jax.random.key(seed), 12)
    batch = noise_with(arg_keys[0], (TOKENS, D), 1.0, 6.0, ((0, 16),), (0, 1, 16, 2.0))
    next_acts = bell_draw(arg_keys[1], (TOKENS, D), 1.0, 6.0, ((0, 128),))
    row_source = draw_row_source(jax.random.fold_in(arg_keys[11], 71), 0)
    enc_weight = bell_draw(arg_keys[3], (D, LATENTS), D ** -0.5, 0.09375, ((0, 16), (1, 8)))
    dec_weight = bell_draw(arg_keys[4], (LATENTS, D), LATENTS ** -0.5, 0.09375, ((0, 8), (1, 16)))
    enc_bias = jnp.clip(-0.8 + 1 * jax.random.uniform(arg_keys[5], (LATENTS,), jnp.float32) ** level_of(arg_keys[5], (LATENTS,), ((0, 8),), -0.2, 0.2), -0.8, 0.2)
    dec_bias = bell_draw(arg_keys[6], (D,), 0.5, 3.0, (), jnp.float32)
    enc_first = bell_draw(arg_keys[7], (D, LATENTS), 0.002, 0.011962891, ((0, 16), (1, 8)))
    enc_second = jnp.clip(jnp.exp(math.log(4.991888999938965e-07) - 2.3044525 * jax.random.uniform(arg_keys[8], (D, LATENTS), jnp.float32) ** level_of(arg_keys[8], (D, LATENTS), ((0, 16), (1, 8)), -0.2, 0.2)), 4.98257577419281e-08, 4.991888999938965e-07).astype(jnp.bfloat16)
    dec_first = bell_draw(arg_keys[9], (LATENTS, D), 0.002, 0.011962891, ((0, 8), (1, 16)))
    dec_second = jnp.clip(jnp.exp(math.log(4.991888999938965e-07) - 2.3044525 * jax.random.uniform(arg_keys[10], (LATENTS, D), jnp.float32) ** level_of(arg_keys[10], (LATENTS, D), ((0, 8), (1, 16)), -0.2, 0.2)), 4.98257577419281e-08, 4.991888999938965e-07).astype(jnp.bfloat16)
    return {"batch": batch, "next_acts": next_acts, "row_source": row_source, "enc_weight": enc_weight, "dec_weight": dec_weight, "enc_bias": enc_bias, "dec_bias": dec_bias, "enc_first": enc_first, "enc_second": enc_second, "dec_first": dec_first, "dec_second": dec_second}


beta_one = 0.9
beta_two = 0.999
correction_one = 1.0 - 0.9 ** 3
correction_two = 1.0 - 0.999 ** 3
eps_adam = 1e-08
sparsity_weight = 0.2

def adam_update(gradient, first, second):
    first_new = beta_one * first.astype(jnp.float32) + (1.0 - beta_one) * gradient
    second_new = beta_two * second.astype(jnp.float32) + (1.0 - beta_two) * gradient * gradient
    direction = first_new / correction_one / (jnp.sqrt(second_new / correction_two) + eps_adam)
    return (first_new.astype(jnp.bfloat16), second_new.astype(jnp.bfloat16), direction.astype(jnp.bfloat16))

def grouped_sum(left, right, scale_factor, shape):
    left_blocks = left.reshape(N_ROWS, R_DEV, left.shape[1])
    right_blocks = right.reshape(N_ROWS, R_DEV, right.shape[1])

    def add_block(running, pair):
        left_part, right_part = pair
        term = jnp.dot(left_part.T, right_part, preferred_element_type=jnp.float32) * scale_factor
        rounded = lax.optimization_barrier(term.astype(jnp.bfloat16)).astype(jnp.float32)
        return (running + rounded, None)
    summed, _ = lax.scan(add_block, jnp.zeros(shape, jnp.float32), (left_blocks, right_blocks))
    return summed

def reference(batch, next_acts, row_source, enc_weight, dec_weight, enc_bias, dec_bias, enc_first, enc_second, dec_first, dec_second):
    next_batch = jnp.take(next_acts, row_source, axis=0)
    inv_tokens = 1.0 / TOKENS
    centered = (batch.astype(jnp.float32) - dec_bias).astype(jnp.bfloat16)
    pre = jnp.dot(centered, enc_weight, preferred_element_type=jnp.float32) + enc_bias
    latent_codes = jnp.maximum(pre, 0.0).astype(jnp.bfloat16)
    recon = jnp.dot(latent_codes, dec_weight, preferred_element_type=jnp.float32)
    recon_error = (recon + dec_bias - batch.astype(jnp.float32)).astype(jnp.bfloat16)
    grad_codes = jnp.dot(recon_error, dec_weight.T, preferred_element_type=jnp.float32)
    code_grad = jnp.where(pre > 0, (grad_codes + sparsity_weight) * inv_tokens, 0.0).astype(jnp.bfloat16)
    enc_grad = grouped_sum(centered, code_grad, 1.0, (D, LATENTS))
    dec_grad = grouped_sum(latent_codes, recon_error, inv_tokens, (LATENTS, D))
    new_enc_first, new_enc_second, enc_update = adam_update(enc_grad, enc_first, enc_second)
    new_dec_first, new_dec_second, dec_update = adam_update(dec_grad, dec_first, dec_second)
    return (next_batch, latent_codes, recon_error, new_enc_first, new_enc_second, enc_update, new_dec_first, new_dec_second, dec_update)
```

```python
import functools

import jax
import jax.numpy as jnp
from jax import lax
from jax.experimental import pallas as pl
from jax.experimental.pallas import tpu as pltpu
from jax.sharding import PartitionSpec as P

beta_one = 0.9
beta_two = 0.999
correction_one = 1.0 - 0.9**3
correction_two = 1.0 - 0.999**3
eps_adam = 1e-08
sparsity_weight = 0.2

MESH = pl.DeviceIdType.MESH
BF = jnp.bfloat16
F32 = jnp.float32
D = 4608
ROWS = 384
LAT = 512
SH = 288
CH = 576
NT = (((1,), (1,)), ((), ()))
TN = (((0,), (0,)), ((), ()))


def adam_update(gradient, first, second):
    first_new = beta_one * first.astype(F32) + (1.0 - beta_one) * gradient
    second_new = beta_two * second.astype(F32) + (1.0 - beta_two) * gradient * gradient
    direction = first_new / correction_one / (jnp.sqrt(second_new / correction_two) + eps_adam)
    return first_new.astype(BF), second_new.astype(BF), direction.astype(BF)


def step_kernel(
    inv_tokens,
    batch_h, encw, decw, enc_bias, dec_bias, ef, es, df, ds,
    codes, err_out, nef, nes, eup, ndf, nds, dup,
    batch, cent, cent_t, neg_t, encf, decf, pre,
    rs_send, rs_recv, recon, err, gcodes, cgrad,
    dsib_s, dsib_r, dsend, drecv, down,
    esib_s, esib_r, esend, erecv, eown,
    loc, enc_s, enc_r, encx_s, encx_r, dec_s, dec_r, decx_s, decx_r,
    sum_s, sum_r, err_s, err_r, dx_s, dx_r, dg_s, dg_r, ex_s, ex_r, eg_s, eg_r,
):
    r = lax.axis_index("rows")
    l = lax.axis_index("lat")
    c = r % 2
    q = r // 2
    sib = (q * 2 + 1 - c, l)

    def chip(k):
        return (q + k) % 8

    def rows_dev(p):
        return (p * 2 + c, l)

    def lat_dev(k):
        return (r, (l + k) % 8)

    def remote(src, dst, ssem, rsem, device):
        return pltpu.make_async_remote_copy(
            src_ref=src, dst_ref=dst, send_sem=ssem, recv_sem=rsem,
            device_id=device, device_id_type=MESH,
        )

    def shard(p, core):
        return pl.ds(pl.multiple_of((p * 2 + core) * SH, 32), SH)

    def chunk(p):
        return pl.ds(pl.multiple_of(p * CH, 64), CH)

    barrier = pltpu.get_barrier_semaphore()
    for k in range(1, 8):
        pl.semaphore_signal(barrier, inc=1, device_id=rows_dev(chip(k)), device_id_type=MESH)
        pl.semaphore_signal(barrier, inc=1, device_id=lat_dev(k), device_id_type=MESH)
    pl.semaphore_signal(barrier, inc=1, device_id=sib, device_id_type=MESH)
    batch_cp = pltpu.make_async_copy(batch_h, batch, loc.at[0])
    batch_cp.start()
    enc_cp = pltpu.make_async_copy(encw, encf.at[shard(q, c)], loc.at[1])
    enc_cp.start()
    dec_cp = pltpu.make_async_copy(decw, decf.at[shard(q, c)], loc.at[2])
    dec_cp.start()
    pl.semaphore_wait(barrier, 15)

    def to_chip(w, full, ssem, rsem, k):
        return remote(w, full.at[shard(q, c)], ssem.at[k], rsem.at[k], rows_dev(chip(k)))

    def from_chip(w, full, ssem, rsem, k):
        return remote(w, full.at[shard(chip(8 - k), c)], ssem.at[k], rsem.at[k], rows_dev(chip(k)))

    def to_sib(full, ssem, rsem, k):
        part = full.at[shard(chip(8 - k), c)]
        return remote(part, part, ssem.at[k], rsem.at[k], sib)

    def from_sib(full, ssem, rsem, k):
        part = full.at[shard(chip(8 - k), 1 - c)]
        return remote(part, part, ssem.at[k], rsem.at[k], sib)

    def send_shards(w, full, ssem, rsem):
        def send(k, _):
            to_chip(w, full, ssem, rsem, k).start()
            return 0

        lax.fori_loop(1, 8, send, 0)

    def collect(w, full, ssem, rsem, xs, xr):
        def forward(k, _):
            from_chip(w, full, ssem, rsem, k).wait_recv()
            to_sib(full, xs, xr, k).start()
            return 0

        lax.fori_loop(1, 8, forward, 0)

    def settle(full, xs, xr):
        def take(k, _):
            from_sib(full, xs, xr, k).wait_recv()
            return 0

        lax.fori_loop(0, 8, take, 0)

    send_shards(encw, encf, enc_s, enc_r)
    enc_cp.wait()
    to_sib(encf, encx_s, encx_r, 0).start()
    dec_cp.wait()
    to_sib(decf, decx_s, decx_r, 0).start()

    batch_cp.wait()

    def center(j, _):
        cols = pl.ds(pl.multiple_of(j * 128, 128), 128)
        x = batch[:, cols].astype(F32) - dec_bias[:, cols]
        cent[:, cols] = x.astype(BF)
        xt = x.T
        cent_t[pl.ds(pl.multiple_of(j * 128, 128), 128), :] = xt.astype(BF)
        for half in range(2):
            h = j * 2 + half

            @pl.when(h // 9 == l)
            def _():
                neg_t[pl.ds(pl.multiple_of((h % 9) * 64, 64), 64), :] = xt[64 * half : 64 * half + 64]

        return 0

    lax.fori_loop(0, 36, center, 0)

    collect(encw, encf, enc_s, enc_r, encx_s, encx_r)
    send_shards(decw, decf, dec_s, dec_r)
    settle(encf, encx_s, encx_r)

    pre[...] = jnp.broadcast_to(enc_bias[...], (ROWS, LAT))

    def encode(j, _):
        part = pl.ds(pl.multiple_of(j * 1152, 128), 1152)
        pre[...] += jnp.dot(cent[:, part], encf[part, :], preferred_element_type=F32)
        return 0

    lax.fori_loop(0, 4, encode, 0)
    codes[...] = jnp.maximum(pre[...], 0.0).astype(BF)

    collect(decw, decf, dec_s, dec_r, decx_s, decx_r)
    settle(decf, decx_s, decx_r)

    def hop(i):
        return 1 + (i + q) % 7

    def sum_copy(k):
        return remote(rs_send.at[k - 1], rs_recv.at[k - 1], sum_s.at[k - 1], sum_r.at[k - 1], lat_dev(k))

    def decode(i, _):
        k = hop(i)
        part = lax.dot_general(decf[chunk((l + k) % 8), :], codes[...], NT, preferred_element_type=F32)
        rs_send[k - 1] = part.astype(BF)
        sum_copy(k).start()
        return 0

    lax.fori_loop(0, 7, decode, 0)
    recon[...] = (
        lax.dot_general(decf[chunk(l), :], codes[...], NT, preferred_element_type=F32) - neg_t[...]
    )

    def add_share(i, _):
        k = hop(i)
        sum_copy(k).wait_recv()
        recon[...] += rs_recv[k - 1].astype(F32)
        return 0

    lax.fori_loop(0, 7, add_share, 0)
    err[chunk(l), :] = recon[...].astype(BF)
    err_out[...] = err[chunk(l), :]

    def err_to(k):
        return remote(err.at[chunk(l)], err.at[chunk(l)], err_s.at[k - 1], err_r.at[k - 1], lat_dev(k))

    def err_from(k):
        part = err.at[chunk((l + 8 - k) % 8)]
        return remote(part, part, err_s.at[k - 1], err_r.at[k - 1], lat_dev(k))

    def send_err(i, _):
        err_to(hop(i)).start()
        return 0

    lax.fori_loop(0, 7, send_err, 0)
    gcodes[...] = jnp.full((ROWS, LAT), sparsity_weight, F32)

    def grad_block(lhs, rhs, p, scale, sib_s, sib_r, send, recv, own, xs, xr, gs, gr):
        other = jnp.dot(lhs[shard(p, 1 - c), :], rhs[...], preferred_element_type=F32)
        sib_s[p] = (other * scale).astype(BF)
        cross = remote(sib_s.at[p], sib_r.at[p], xs.at[p], xr.at[p], sib)
        cross.start()
        mine = jnp.dot(lhs[shard(p, c), :], rhs[...], preferred_element_type=F32) * scale
        cross.wait_recv()
        total = mine + sib_r[p].astype(F32)
        k = (p + 8 - q) % 8

        @pl.when(k == 0)
        def _():
            own[...] = total

        @pl.when(k > 0)
        def _():
            send[k - 1] = total.astype(BF)
            remote(send.at[k - 1], recv.at[k - 1], gs.at[k - 1], gr.at[k - 1], rows_dev(p)).start()

    def error_chunk(p):
        gcodes[...] += lax.dot_general(
            err[chunk(p), :], decf[chunk(p), :], TN, preferred_element_type=F32
        )
        grad_block(err, codes, p, inv_tokens, dsib_s, dsib_r, dsend, drecv, down, dx_s, dx_r, dg_s, dg_r)

    error_chunk(l)

    def error_step(i, _):
        k = hop(i)
        err_from(k).wait_recv()
        error_chunk((l + 8 - k) % 8)
        return 0

    lax.fori_loop(0, 7, error_step, 0)
    cgrad[...] = jnp.where(pre[...] > 0, gcodes[...] * inv_tokens, 0.0).astype(BF)

    def enc_step(i, _):
        grad_block(
            cent_t, cgrad, (q + 1 + i) % 8, 1.0, esib_s, esib_r, esend, erecv, eown, ex_s, ex_r, eg_s, eg_r
        )
        return 0

    lax.fori_loop(0, 8, enc_step, 0)

    def finish(send, recv, own, gs, gr, first, second, outs):
        def add(k, _):
            remote(send.at[k], recv.at[k], gs.at[k], gr.at[k], rows_dev(chip(k + 1))).wait_recv()
            own[...] += recv[k].astype(F32)
            return 0

        lax.fori_loop(0, 7, add, 0)
        new = adam_update(own[...], first[...], second[...])
        for out, value in zip(outs, new):
            out[...] = value

    finish(dsend, drecv, down, dg_s, dg_r, df, ds, (ndf, nds, dup))
    finish(esend, erecv, eown, eg_s, eg_r, ef, es, (nef, nes, eup))

    def drain(i, _):
        k = i + 1
        to_chip(encw, encf, enc_s, enc_r, k).wait_send()
        to_chip(decw, decf, dec_s, dec_r, k).wait_send()
        sum_copy(k).wait_send()
        err_to(k).wait_send()
        remote(dsend.at[i], drecv.at[i], dg_s.at[i], dg_r.at[i], rows_dev(chip(k))).wait_send()
        remote(esend.at[i], erecv.at[i], eg_s.at[i], eg_r.at[i], rows_dev(chip(k))).wait_send()
        return 0

    lax.fori_loop(0, 7, drain, 0)

    def drain_sib(k, _):
        to_sib(encf, encx_s, encx_r, k).wait_send()
        to_sib(decf, decx_s, decx_r, k).wait_send()
        remote(dsib_s.at[k], dsib_r.at[k], dx_s.at[k], dx_r.at[k], sib).wait_send()
        remote(esib_s.at[k], esib_r.at[k], ex_s.at[k], ex_r.at[k], sib).wait_send()
        return 0

    lax.fori_loop(0, 8, drain_sib, 0)


def train_step(batch, encw, decw_t, enc_bias, dec_bias, ef, es, df_t, ds_t, inv_tokens):
    any_space = pl.BlockSpec(memory_space=pl.ANY)
    vmem = pl.BlockSpec(memory_space=pltpu.VMEM)
    dma = pltpu.SemaphoreType.DMA
    grads = [
        pltpu.VMEM((8, SH, LAT), BF),
        pltpu.VMEM((8, SH, LAT), BF),
        pltpu.VMEM((7, SH, LAT), BF),
        pltpu.VMEM((7, SH, LAT), BF),
        pltpu.VMEM((SH, LAT), F32),
    ]
    shard = jax.ShapeDtypeStruct((SH, LAT), BF)
    return pl.pallas_call(
        functools.partial(step_kernel, inv_tokens),
        out_shape=(
            jax.ShapeDtypeStruct((ROWS, LAT), BF),
            jax.ShapeDtypeStruct((CH, ROWS), BF),
            *([shard] * 6),
        ),
        in_specs=[any_space] * 3 + [vmem] * 6,
        out_specs=[vmem] * 8,
        scratch_shapes=[
            pltpu.VMEM((ROWS, D), BF),
            pltpu.VMEM((ROWS, D), BF),
            pltpu.VMEM((D, ROWS), BF),
            pltpu.VMEM((CH, ROWS), F32),
            pltpu.VMEM((D, LAT), BF),
            pltpu.VMEM((D, LAT), BF),
            pltpu.VMEM((ROWS, LAT), F32),
            pltpu.VMEM((7, CH, ROWS), BF),
            pltpu.VMEM((7, CH, ROWS), BF),
            pltpu.VMEM((CH, ROWS), F32),
            pltpu.VMEM((D, ROWS), BF),
            pltpu.VMEM((ROWS, LAT), F32),
            pltpu.VMEM((ROWS, LAT), BF),
            *grads,
            *grads,
            dma((3,)),
            *([dma((8,))] * 8),
            *([dma((7,))] * 4),
            dma((8,)), dma((8,)), dma((7,)), dma((7,)),
            dma((8,)), dma((8,)), dma((7,)), dma((7,)),
        ],
        compiler_params=pltpu.CompilerParams(
            collective_id=0, has_side_effects=True, vmem_limit_bytes=63 * 2**20
        ),
        cost_estimate=pl.CostEstimate(
            flops=5 * 2 * ROWS * LAT * D, bytes_accessed=16 * 2**20, transcendentals=0
        ),
    )(batch, encw, decw_t, enc_bias, dec_bias, ef, es, df_t, ds_t)


def relayout(next_acts, row_source):
    rows_index = lax.axis_index("rows")
    lat_index = lax.axis_index("lat")
    per_device = next_acts.shape[0]
    total_rows = row_source.shape[0]
    mine = (rows_index * 8 + lat_index) * per_device + jnp.arange(per_device, dtype=jnp.int32)
    matches = row_source[None, :] == mine[:, None]
    dest_of = jnp.sum(
        jnp.where(matches, jnp.arange(total_rows, dtype=jnp.int32)[None, :], 0), axis=1
    )
    slot = jnp.sum(dest_of[:, None] > dest_of[None, :], axis=1, dtype=jnp.int32)
    pick = (slot[None, :] == jnp.arange(per_device, dtype=jnp.int32)[:, None]).astype(BF)
    outgoing = jnp.dot(pick, next_acts, preferred_element_type=F32).astype(BF)
    arrived = lax.all_to_all(
        outgoing.reshape(16, 3, D), "rows", split_axis=0, concat_axis=0, tiled=True
    ).reshape(per_device, D)
    everything = lax.all_gather(arrived, "lat", axis=0, tiled=True)
    wanted = lax.dynamic_slice_in_dim(row_source, rows_index * ROWS, ROWS)
    owners = wanted // per_device
    place = jnp.arange(ROWS, dtype=jnp.int32)
    same = jnp.logical_and(owners[:, None] == owners[None, :], place[:, None] > place[None, :])
    rank = jnp.sum(same, axis=1, dtype=jnp.int32)
    position = (owners % 8) * per_device + (owners // 8) * 3 + rank
    put = (position[:, None] == place[None, :]).astype(BF)
    return everything, put


def on_device(
    batch, next_acts, row_source, enc_weight, dec_weight, enc_bias, dec_bias,
    enc_first, enc_second, dec_first, dec_second,
):
    inv_tokens = 1.0 / (batch.shape[0] * 16)
    everything, put = relayout(next_acts, row_source)
    codes, err_t, nef, nes, eup, ndf, nds, dup = train_step(
        batch, enc_weight, dec_weight.T, enc_bias.reshape(1, LAT), dec_bias.reshape(1, D),
        enc_first, enc_second, dec_first.T, dec_second.T, inv_tokens,
    )
    next_batch = jnp.dot(put, everything, preferred_element_type=F32).astype(BF)
    return next_batch, codes, err_t.T, nef, nes, eup, ndf.T, nds.T, dup.T


def solution(mesh):
    return jax.shard_map(
        on_device,
        mesh=mesh,
        in_specs=(
            P("rows", None),
            P(("rows", "lat"), None),
            P(),
            P("rows", "lat"),
            P("lat", "rows"),
            P("lat"),
            P(),
            P("rows", "lat"),
            P("rows", "lat"),
            P("lat", "rows"),
            P("lat", "rows"),
        ),
        out_specs=(
            P("rows", None),
            P("rows", "lat"),
            P("rows", "lat"),
            P("rows", "lat"),
            P("rows", "lat"),
            P("rows", "lat"),
            P("lat", "rows"),
            P("lat", "rows"),
            P("lat", "rows"),
        ),
        check_vma=False,
    )
```

```python
import functools

import jax
import jax.numpy as jnp
from jax import lax
from jax.experimental import pallas as pl
from jax.experimental.pallas import tpu as pltpu
from jax.sharding import PartitionSpec as P

beta_one = 0.9
beta_two = 0.999
correction_one = 1.0 - 0.9**3
correction_two = 1.0 - 0.999**3
eps_adam = 1e-08
sparsity_weight = 0.2

MESH = pl.DeviceIdType.MESH
BF = jnp.bfloat16
F32 = jnp.float32
D = 4608
ROWS = 384
LAT = 512
SH = 288
CH = 576
CH_A = 224
SH_A = 112
NT = (((1,), (1,)), ((), ()))
TN = (((0,), (0,)), ((), ()))


def adam_update(gradient, first, second):
    first_new = beta_one * first.astype(F32) + (1.0 - beta_one) * gradient
    second_new = beta_two * second.astype(F32) + (1.0 - beta_two) * gradient * gradient
    direction = first_new / correction_one / (jnp.sqrt(second_new / correction_two) + eps_adam)
    return first_new.astype(BF), second_new.astype(BF), direction.astype(BF)


def step_kernel(
    inv_tokens,
    batch_h, next_h, encw, decw, source, enc_bias, dec_bias, ef, es, df, ds,
    next_out, codes, err_out, nef, nes, eup, ndf, nds, dup,
    batch, cent, cent_t, neg_t, encf, decf, pre, recon, err, gcodes, cgrad,
    lpart, lrec_a, lrec_y, lrec_b, lrec_p,
    sib_s, dsib_r, esib_r,
    dpart, drec_a, drec_y, drec_b, drec_p, down,
    epart, erec_a, erec_y, erec_b, erec_p, eown,
    nacts, tmp, out3, in3, rows48,
    loc, enc_s, enc_r, encx_s, encx_r, dec_s, dec_r, decx_s, decx_r,
    ls_s, ls_r, err_s, err_r, dx_s, dx_r, dg_s, dg_r, ex_s, ex_r, eg_s, eg_r,
    a2a_s, a2a_r, n_s, n_r,
):
    r = lax.axis_index("rows")
    l = lax.axis_index("lat")
    c = r % 2
    q = r // 2
    sib = (q * 2 + 1 - c, l)

    def remote(src, dst, ssem, rsem, device):
        return pltpu.make_async_remote_copy(
            src_ref=src, dst_ref=dst, send_sem=ssem, recv_sem=rsem,
            device_id=device, device_id_type=MESH,
        )

    def member(g, dm, db):
        return (g // 2 + dm) % 4 * 2 + (g + db) % 2

    def rows_dev(g):
        return (g * 2 + c, l)

    def lat_dev(g):
        return (r, g)

    def shard_at(g):
        return pl.multiple_of((g * 2 + c) * SH, 32)

    def shard(g, core):
        return pl.ds(pl.multiple_of((g * 2 + core) * SH, 32), SH)

    def chunk_at(g):
        return pl.multiple_of(g * CH, 64)

    def chunk(g):
        return pl.ds(chunk_at(g), CH)

    barrier = pltpu.get_barrier_semaphore()
    for k in range(1, 16):
        pl.semaphore_signal(barrier, inc=1, device_id=((r + k) % 16, l), device_id_type=MESH)
    for dm, db in ((0, 1), (1, 0), (2, 0), (3, 0)):
        pl.semaphore_signal(barrier, inc=1, device_id=lat_dev(member(l, dm, db)), device_id_type=MESH)
    batch_cp = pltpu.make_async_copy(batch_h, batch, loc.at[0])
    enc_cp = pltpu.make_async_copy(encw, encf.at[shard(q, c)], loc.at[1])
    dec_cp = pltpu.make_async_copy(decw, decf.at[shard(q, c)], loc.at[2])
    next_cp = pltpu.make_async_copy(next_h, nacts, loc.at[3])
    next_cp.start()
    enc_cp.start()
    batch_cp.start()
    dec_cp.start()
    pl.semaphore_wait(barrier, 19)

    class Gather:
        def __init__(self, full, at, g, dev, ssem, rsem, size, size_a):
            self.full, self.at, self.g, self.dev, self.s, self.r = full, at, g, dev, ssem, rsem
            self.size, self.size_a = size, size_a

        def part(self, g, which):
            if which == "a":
                return self.full.at[pl.ds(self.at(g), self.size_a)]
            return self.full.at[pl.ds(self.at(g) + self.size_a, self.size - self.size_a)]

        def copy(self, g, which, slot, to):
            part = self.part(g, which)
            return remote(part, part, self.s.at[slot], self.r.at[slot], self.dev(to))

        def own(self, dm, db, which):
            slot = dm if which == "a" else 4 + dm
            return self.copy(self.g, which, slot, member(self.g, dm, db))

        def came(self, dm, db, which):
            slot = dm if which == "a" else 4 + dm
            return self.copy(member(self.g, 4 - dm, db), which, slot, self.g)

        def on_a(self, j):
            return self.copy(member(self.g, 0, 1), "a", 8 + j, member(self.g, j, 0))

        def on_b(self, j):
            return self.copy(member(self.g, 4 - j, 0), "b", 12 + j, member(self.g, 0, 1))

        def diag_a(self, j):
            return self.copy(member(self.g, 4 - j, 1), "a", 8 + j, self.g)

        def diag_b(self, j):
            return self.copy(member(self.g, 4 - j, 1), "b", 12 + j, self.g)

        def start(self):
            self.own(0, 1, "a").start()
            for j in (1, 3, 2):
                self.own(j, 0, "b").start()
            self.own(0, 1, "b").start()
            for j in (1, 3, 2):
                self.own(j, 0, "a").start()

        def forward_a(self):
            self.came(0, 1, "a").wait_recv()
            for j in (2, 1, 3):
                self.on_a(j).start()

        def forward_b(self, j):
            self.came(j, 0, "b").wait_recv()
            self.on_b(j).start()

        def take_pair(self):
            self.came(0, 1, "b").wait_recv()

        def take_ring(self, j):
            self.came(j, 0, "a").wait_recv()

        def take_diag(self, j):
            self.diag_a(j).wait_recv()
            self.diag_b(j).wait_recv()

        def drain(self):
            for dm, db in ((0, 1), (1, 0), (2, 0), (3, 0)):
                self.own(dm, db, "a").wait_send()
                self.own(dm, db, "b").wait_send()
            for j in (1, 2, 3):
                self.on_a(j).wait_send()
                self.on_b(j).wait_send()

    class Scatter:
        def __init__(self, part, rec_a, rec_y, rec_b, rec_p, g, dev, ssem, rsem, size, size_a):
            self.p, self.ra, self.ry, self.rb, self.rp = part, rec_a, rec_y, rec_b, rec_p
            self.g, self.dev, self.s, self.r = g, dev, ssem, rsem
            self.a, self.b = pl.ds(0, size_a), pl.ds(size_a, size - size_a)

        def copy(self, src, dst, slot, to):
            return remote(src, dst, self.s.at[slot], self.r.at[slot], self.dev(to))

        def diag_a(self, j):
            src = self.p.at[member(self.g, j, 1), self.a]
            return self.copy(src, self.ra.at[j - 1], j, member(self.g, j, 0))

        def diag_b(self, j):
            src = self.p.at[member(self.g, j, 1), self.b]
            return self.copy(src, self.ry.at[j], 4 + j, member(self.g, 0, 1))

        def ring_a(self, j):
            src = self.p.at[member(self.g, j, 0), self.a]
            return self.copy(src, self.ra.at[2 + j], 8 + j, member(self.g, j, 0))

        def ring_b(self, j):
            src = self.p.at[member(self.g, j, 0), self.b]
            return self.copy(src, self.rb.at[j - 1], 12 + j, member(self.g, j, 0))

        def pair_b(self):
            src = self.p.at[member(self.g, 0, 1), self.b]
            return self.copy(src, self.ry.at[0], 4, member(self.g, 0, 1))

        def pair_a(self):
            src = self.p.at[member(self.g, 0, 1), self.a]
            return self.copy(src, self.rp, 8, member(self.g, 0, 1))

        def emit(self, p):
            dm = (p // 2 + 4 - self.g // 2) % 4
            db = (p + self.g) % 2

            @pl.when(jnp.logical_and(db == 1, dm > 0))
            def _():
                self.diag_b(dm).start()
                self.diag_a(dm).start()

            @pl.when(jnp.logical_and(db == 0, dm > 0))
            def _():
                self.ring_a(dm).start()

            @pl.when(jnp.logical_and(db == 1, dm == 0))
            def _():
                self.pair_b().start()

        def pass_on(self):
            for j in (2, 3, 1):
                self.diag_b(j).wait_recv()
                block = self.p.at[member(self.g, j, 0), self.b]
                block[...] = (block[...].astype(F32) + self.ry[j].astype(F32)).astype(BF)
                self.ring_b(j).start()
            block = self.p.at[member(self.g, 0, 1), self.a]
            total = block[...].astype(F32)
            for j in (2, 3, 1):
                self.diag_a(j).wait_recv()
                total = total + self.ra[j - 1].astype(F32)
            block[...] = total.astype(BF)
            self.pair_a().start()

        def finish(self, own):
            for j in (1, 2, 3):
                self.ring_a(j).wait_recv()
            total = own[self.a, :]
            for j in (1, 2, 3):
                total = total + self.ra[2 + j].astype(F32)
            self.pair_b().wait_recv()
            rest = own[self.b, :] + self.ry[0].astype(F32)
            for j in (2, 3, 1):
                self.ring_b(j).wait_recv()
                rest = rest + self.rb[j - 1].astype(F32)
            own[self.b, :] = rest
            self.pair_a().wait_recv()
            own[self.a, :] = total + self.rp[...].astype(F32)

        def drain(self):
            for j in (1, 2, 3):
                self.diag_a(j).wait_send()
                self.diag_b(j).wait_send()
                self.ring_a(j).wait_send()
                self.ring_b(j).wait_send()
            self.pair_a().wait_send()
            self.pair_b().wait_send()

    class Weights(Gather):
        def __init__(self, full, ssem, rsem, xs, xr):
            super().__init__(full, shard_at, q, rows_dev, ssem, rsem, SH, SH_A)
            self.xs, self.xr = xs, xr

        def cross(self, dm, db):
            part = self.full.at[shard(member(q, 4 - dm, db), c)]
            return remote(part, part, self.xs.at[dm * 2 + db], self.xr.at[dm * 2 + db], sib)

        def crossed(self, dm, db):
            part = self.full.at[shard(member(q, 4 - dm, db), 1 - c)]
            return remote(part, part, self.xs.at[dm * 2 + db], self.xr.at[dm * 2 + db], sib)

        def collect(self):
            for j in (1, 3, 2):
                self.forward_b(j)
            self.take_pair()
            self.cross(0, 1).start()
            for j in (1, 3, 2):
                self.take_ring(j)
                self.cross(j, 0).start()

        def settle(self):
            for j in (1, 3, 2):
                self.take_diag(j)
                self.cross(j, 1).start()
            for i in range(8):
                self.crossed(i // 2, i % 2).wait_recv()

        def drain(self):
            super().drain()
            for i in range(8):
                self.cross(i // 2, i % 2).wait_send()

    enc_g = Weights(encf, enc_s, enc_r, encx_s, encx_r)
    dec_g = Weights(decf, dec_s, dec_r, decx_s, decx_r)
    enc_cp.wait()
    enc_g.start()
    enc_g.cross(0, 0).start()

    next_cp.wait()
    lane48 = lax.broadcasted_iota(jnp.int32, (48, 48), 1)
    sub48 = lax.broadcasted_iota(jnp.int32, (48, 48), 0)
    mine = (r * 8 + l) * 48

    def find(j, dest):
        cols = pl.ds(pl.multiple_of(j * 512, 512), 512)
        ids = jnp.broadcast_to(source[:, cols], (48, 512))
        sub = lax.broadcasted_iota(jnp.int32, (48, 512), 0)
        lane = lax.broadcasted_iota(jnp.int32, (48, 512), 1)
        hit = jnp.where(ids == sub + mine, lane + j * 512, 0)
        return dest + jnp.sum(hit.astype(F32), axis=1, keepdims=True)

    dest = lax.fori_loop(0, 12, find, jnp.zeros((48, 1), F32))
    dest_row = jnp.sum(jnp.where(lane48 == sub48, dest, 0.0), axis=0, keepdims=True)
    slot = jnp.sum(jnp.where(dest < dest_row, 1.0, 0.0), axis=0, keepdims=True)
    pick = jnp.where(slot == sub48.astype(F32), 1.0, 0.0).astype(BF)
    tmp[...] = jnp.dot(pick, nacts[...], preferred_element_type=F32)
    for g in range(16):
        out3[g, 0:3, :] = tmp[3 * g : 3 * g + 3, :].astype(BF)

    def to_group(k):
        return remote(
            out3.at[(r + k) % 16], in3.at[r], a2a_s.at[k - 1], a2a_r.at[k - 1], ((r + k) % 16, l)
        )

    def from_group(k):
        part = in3.at[(r + 16 - k) % 16]
        return remote(part, part, a2a_s.at[k - 1], a2a_r.at[k - 1], (r, l))

    def send_group(k, _):
        to_group(k).start()
        return 0

    lax.fori_loop(1, 16, send_group, 0)
    in3[r] = out3[r]

    dec_cp.wait()
    dec_g.cross(0, 0).start()
    enc_g.forward_a()

    batch_cp.wait()

    def center(j, _):
        cols = pl.ds(pl.multiple_of(j * 128, 128), 128)
        x = batch[:, cols].astype(F32) - dec_bias[:, cols]
        cent[:, cols] = x.astype(BF)
        xt = x.T
        cent_t[pl.ds(pl.multiple_of(j * 128, 128), 128), :] = xt.astype(BF)
        for half in range(2):
            h = j * 2 + half

            @pl.when(h // 9 == l)
            def _():
                neg_t[pl.ds(pl.multiple_of((h % 9) * 64, 64), 64), :] = xt[64 * half : 64 * half + 64]

        return 0

    lax.fori_loop(0, 36, center, 0)

    enc_g.collect()
    dec_g.start()

    def arrive(k, _):
        from_group(k).wait_recv()
        return 0

    lax.fori_loop(1, 16, arrive, 0)
    for g in range(16):
        tmp[3 * g : 3 * g + 3, :] = in3[g, 0:3, :].astype(F32)
    rows48[pl.ds(pl.multiple_of(l * 48, 16), 48), :] = tmp[...].astype(BF)

    def next_copy(g, slot, to):
        part = rows48.at[pl.ds(pl.multiple_of(g * 48, 16), 48)]
        return remote(part, part, n_s.at[slot], n_r.at[slot], lat_dev(to))

    def next_own(j):
        return next_copy(l, j, member(l, j, 0) if j else member(l, 0, 1))

    def next_came(j):
        return next_copy(member(l, 4 - j, 0) if j else member(l, 0, 1), j, l)

    def next_on(j):
        return next_copy(member(l, 0, 1), 3 + j, member(l, j, 0))

    def next_diag(j):
        return next_copy(member(l, 4 - j, 1), 3 + j, l)

    for j in range(4):
        next_own(j).start()

    enc_g.settle()
    pre[...] = jnp.broadcast_to(enc_bias[...], (ROWS, LAT))
    dec_g.forward_a()

    def encode(j, _):
        part = pl.ds(pl.multiple_of(j * 1152, 128), 1152)
        pre[...] += jnp.dot(cent[:, part], encf[part, :], preferred_element_type=F32)
        return 0

    lax.fori_loop(0, 4, encode, 0)
    codes[...] = jnp.maximum(pre[...], 0.0).astype(BF)
    dec_g.collect()
    dec_g.settle()

    lat_sum = Scatter(lpart, lrec_a, lrec_y, lrec_b, lrec_p, l, lat_dev, ls_s, ls_r, CH, CH_A)

    def order(g, i):
        return member(g, (i + 2) % 4, 1 - i // 4)

    def decode(i, _):
        p = order(l, i)
        part = lax.dot_general(decf[chunk(p), :], codes[...], NT, preferred_element_type=F32)
        lpart[p] = part.astype(BF)
        lat_sum.emit(p)

        @pl.when(i == 6)
        def _():
            recon[...] = part - neg_t[...]

        return 0

    lax.fori_loop(0, 8, decode, 0)
    lat_sum.pass_on()
    lat_sum.finish(recon)
    err[chunk(l), :] = recon[...].astype(BF)
    err_out[...] = err[chunk(l), :]

    err_g = Gather(err, chunk_at, l, lat_dev, err_s, err_r, CH, CH_A)
    err_g.start()
    gcodes[...] = jnp.full((ROWS, LAT), sparsity_weight, F32)

    def grad_block(lhs, rhs, p, scale, sib_r, own, scatter, xs, xr):
        other = jnp.dot(lhs[shard(p, 1 - c), :], rhs[...], preferred_element_type=F32)
        sib_s[p] = (other * scale).astype(BF)
        cross = remote(sib_s.at[p], sib_r.at[p], xs.at[p], xr.at[p], sib)
        cross.start()
        mine = jnp.dot(lhs[shard(p, c), :], rhs[...], preferred_element_type=F32) * scale
        cross.wait_recv()
        total = mine + sib_r[p].astype(F32)
        scatter.p[p] = total.astype(BF)
        scatter.emit(p)

        @pl.when(p == q)
        def _():
            own[...] = total

    dec_sum = Scatter(dpart, drec_a, drec_y, drec_b, drec_p, q, rows_dev, dg_s, dg_r, SH, SH_A)
    enc_sum = Scatter(epart, erec_a, erec_y, erec_b, erec_p, q, rows_dev, eg_s, eg_r, SH, SH_A)

    def error_block(p):
        gcodes[...] += lax.dot_general(
            err[chunk(p), :], decf[chunk(p), :], TN, preferred_element_type=F32
        )
        grad_block(err, codes, p, inv_tokens, dsib_r, down, dec_sum, dx_s, dx_r)

    error_block(l)
    err_g.forward_a()
    for j in (1, 3, 2):
        err_g.forward_b(j)
    err_g.take_pair()
    error_block(member(l, 0, 1))

    def error_ring(i, _):
        j = (7 - i) % 4
        err_g.take_ring(j)
        error_block(member(l, 4 - j, 0))
        return 0

    lax.fori_loop(0, 3, error_ring, 0)

    def error_diag(i, _):
        j = (7 - i) % 4
        err_g.take_diag(j)
        error_block(member(l, 4 - j, 1))
        return 0

    lax.fori_loop(0, 3, error_diag, 0)
    next_came(0).wait_recv()
    for j in (1, 3, 2):
        next_on(j).start()
    cgrad[...] = jnp.where(pre[...] > 0, gcodes[...] * inv_tokens, 0.0).astype(BF)
    dec_sum.pass_on()

    def drain_cross(p, _):
        remote(sib_s.at[p], dsib_r.at[p], dx_s.at[p], dx_r.at[p], sib).wait_send()
        return 0

    lax.fori_loop(0, 8, drain_cross, 0)

    def enc_step(i, _):
        grad_block(cent_t, cgrad, order(q, i), 1.0, esib_r, eown, enc_sum, ex_s, ex_r)
        return 0

    lax.fori_loop(0, 8, enc_step, 0)
    enc_sum.pass_on()

    place_l = lax.broadcasted_iota(jnp.int32, (ROWS, ROWS), 1)
    place_s = lax.broadcasted_iota(jnp.int32, (ROWS, ROWS), 0)
    wanted = source[:, pl.ds(pl.multiple_of(r * ROWS, 128), ROWS)]
    owner = jnp.right_shift(wanted * 43691, 21).astype(F32)
    owner_col = jnp.sum(jnp.where(place_l == place_s, owner, 0.0), axis=1, keepdims=True)
    earlier = jnp.logical_and(owner == owner_col, place_l < place_s)
    rank = jnp.sum(jnp.where(earlier, 1.0, 0.0), axis=1, keepdims=True)
    owner_i = owner_col.astype(jnp.int32)
    position = jnp.bitwise_and(owner_i, 7) * 48 + jnp.right_shift(owner_i, 3) * 3 + rank.astype(jnp.int32)
    put = jnp.where(position == place_l, 1.0, 0.0).astype(BF)
    for j in (1, 3, 2):
        next_came(j).wait_recv()
    for j in (1, 3, 2):
        next_diag(j).wait_recv()
    cgrad[:, 0:ROWS] = put

    def permute(j, _):
        cols = pl.ds(pl.multiple_of(j * 512, 512), 512)
        batch[:, cols] = jnp.dot(
            cgrad[:, 0:ROWS], rows48[:, cols], preferred_element_type=F32
        ).astype(BF)
        return 0

    lax.fori_loop(0, 9, permute, 0)
    out_cp = pltpu.make_async_copy(batch, next_out, loc.at[4])
    out_cp.start()

    def update(scatter, own, first, second, outs):
        scatter.finish(own)
        for out, value in zip(outs, adam_update(own[...], first[...], second[...])):
            out[...] = value

    update(dec_sum, down, df, ds, (ndf, nds, dup))
    update(enc_sum, eown, ef, es, (nef, nes, eup))

    enc_g.drain()
    dec_g.drain()
    err_g.drain()
    lat_sum.drain()
    dec_sum.drain()
    enc_sum.drain()

    def drain_group(k, _):
        to_group(k).wait_send()
        return 0

    lax.fori_loop(1, 16, drain_group, 0)
    for j in range(4):
        next_own(j).wait_send()
    for j in (1, 2, 3):
        next_on(j).wait_send()

    def drain_cross2(p, _):
        remote(sib_s.at[p], esib_r.at[p], ex_s.at[p], ex_r.at[p], sib).wait_send()
        return 0

    lax.fori_loop(0, 8, drain_cross2, 0)
    out_cp.wait()


def train_step(
    batch, next_acts, encw, decw_t, source, enc_bias, dec_bias, ef, es, df_t, ds_t, inv_tokens
):
    any_space = pl.BlockSpec(memory_space=pl.ANY)
    vmem = pl.BlockSpec(memory_space=pltpu.VMEM)
    dma = pltpu.SemaphoreType.DMA

    def received(size, size_a, width):
        return [
            pltpu.VMEM((8, size, width), BF),
            pltpu.VMEM((6, size_a, width), BF),
            pltpu.VMEM((4, size - size_a, width), BF),
            pltpu.VMEM((3, size - size_a, width), BF),
            pltpu.VMEM((size_a, width), BF),
        ]

    shard = jax.ShapeDtypeStruct((SH, LAT), BF)
    return pl.pallas_call(
        functools.partial(step_kernel, inv_tokens),
        out_shape=(
            jax.ShapeDtypeStruct((ROWS, D), BF),
            jax.ShapeDtypeStruct((ROWS, LAT), BF),
            jax.ShapeDtypeStruct((CH, ROWS), BF),
            *([shard] * 6),
        ),
        in_specs=[any_space] * 4 + [vmem] * 7,
        out_specs=[any_space] + [vmem] * 8,
        scratch_shapes=[
            pltpu.VMEM((ROWS, D), BF),
            pltpu.VMEM((ROWS, D), BF),
            pltpu.VMEM((D, ROWS), BF),
            pltpu.VMEM((CH, ROWS), F32),
            pltpu.VMEM((D, LAT), BF),
            pltpu.VMEM((D, LAT), BF),
            pltpu.VMEM((ROWS, LAT), F32),
            pltpu.VMEM((CH, ROWS), F32),
            pltpu.VMEM((D, ROWS), BF),
            pltpu.VMEM((ROWS, LAT), F32),
            pltpu.VMEM((ROWS, LAT), BF),
            *received(CH, CH_A, ROWS),
            *([pltpu.VMEM((8, SH, LAT), BF)] * 3),
            *received(SH, SH_A, LAT),
            pltpu.VMEM((SH, LAT), F32),
            *received(SH, SH_A, LAT),
            pltpu.VMEM((SH, LAT), F32),
            pltpu.VMEM((48, D), BF),
            pltpu.VMEM((48, D), F32),
            pltpu.VMEM((16, 4, D), BF),
            pltpu.VMEM((16, 4, D), BF),
            pltpu.VMEM((ROWS, D), BF),
            dma((5,)),
            dma((16,)), dma((16,)), dma((8,)), dma((8,)),
            dma((16,)), dma((16,)), dma((8,)), dma((8,)),
            dma((16,)), dma((16,)), dma((16,)), dma((16,)),
            dma((8,)), dma((8,)), dma((16,)), dma((16,)),
            dma((8,)), dma((8,)), dma((16,)), dma((16,)),
            dma((15,)), dma((15,)), dma((7,)), dma((7,)),
        ],
        compiler_params=pltpu.CompilerParams(
            collective_id=0, has_side_effects=True, vmem_limit_bytes=63 * 2**20
        ),
        cost_estimate=pl.CostEstimate(
            flops=5 * 2 * ROWS * LAT * D, bytes_accessed=16 * 2**20, transcendentals=0
        ),
    )(batch, next_acts, encw, decw_t, source, enc_bias, dec_bias, ef, es, df_t, ds_t)


def on_device(
    batch, next_acts, row_source, enc_weight, dec_weight, enc_bias, dec_bias,
    enc_first, enc_second, dec_first, dec_second,
):
    inv_tokens = 1.0 / (batch.shape[0] * 16)
    next_batch, codes, err_t, nef, nes, eup, ndf, nds, dup = train_step(
        batch, next_acts, enc_weight, dec_weight.T, row_source.reshape(1, -1),
        enc_bias.reshape(1, LAT), dec_bias.reshape(1, D),
        enc_first, enc_second, dec_first.T, dec_second.T, inv_tokens,
    )
    return next_batch, codes, err_t.T, nef, nes, eup, ndf.T, nds.T, dup.T


def solution(mesh):
    return jax.shard_map(
        on_device,
        mesh=mesh,
        in_specs=(
            P("rows", None),
            P(("rows", "lat"), None),
            P(),
            P("rows", "lat"),
            P("lat", "rows"),
            P("lat"),
            P(),
            P("rows", "lat"),
            P("rows", "lat"),
            P("lat", "rows"),
            P("lat", "rows"),
        ),
        out_specs=(
            P("rows", None),
            P("rows", "lat"),
            P("rows", "lat"),
            P("rows", "lat"),
            P("rows", "lat"),
            P("rows", "lat"),
            P("lat", "rows"),
            P("lat", "rows"),
            P("lat", "rows"),
        ),
        check_vma=False,
    )
```

```python
import functools

import jax
import jax.numpy as jnp
from jax import lax
from jax.experimental import pallas as pl
from jax.experimental.pallas import tpu as pltpu
from jax.sharding import PartitionSpec as P

beta_one = 0.9
beta_two = 0.999
correction_one = 1.0 - 0.9**3
correction_two = 1.0 - 0.999**3
eps_adam = 1e-08
sparsity_weight = 0.2

MESH = pl.DeviceIdType.MESH
BF = jnp.bfloat16
F32 = jnp.float32
D = 4608
ROWS = 384
LAT = 512
SH = 288
CH = 576
CH_A = 224
SH_A = 112
NT = (((1,), (1,)), ((), ()))
TN = (((0,), (0,)), ((), ()))


def adam_update(gradient, first, second):
    first_new = beta_one * first.astype(F32) + (1.0 - beta_one) * gradient
    second_new = beta_two * second.astype(F32) + (1.0 - beta_two) * gradient * gradient
    direction = first_new / correction_one / (jnp.sqrt(second_new / correction_two) + eps_adam)
    return first_new.astype(BF), second_new.astype(BF), direction.astype(BF)


def step_kernel(
    inv_tokens,
    batch_h, next_h, encw, decw, source, enc_bias, dec_bias, ef, es, df, ds,
    next_out, codes, err_out, nef, nes, eup, ndf, nds, dup,
    batch, cent, cent_t, neg_t, encf, decf, pre, recon, err, gcodes, cgrad,
    lpart, lrec_a, lrec_y, lrec_b, lrec_p,
    sib_s, dsib_r, esib_r,
    dpart, drec_a, drec_y, drec_b, drec_p, down,
    epart, erec_a, erec_y, erec_b, erec_p, eown,
    nacts, tmp, out3, in3, rows48,
    loc, enc_s, enc_r, encx_s, encx_r, dec_s, dec_r, decx_s, decx_r,
    ls_s, ls_r, err_s, err_r, dx_s, dx_r, dg_s, dg_r, ex_s, ex_r, eg_s, eg_r,
    a2a_s, a2a_r, n_s, n_r,
):
    r = lax.axis_index("rows")
    l = lax.axis_index("lat")
    c = r % 2
    q = r // 2
    sib = (q * 2 + 1 - c, l)

    def remote(src, dst, ssem, rsem, device):
        return pltpu.make_async_remote_copy(
            src_ref=src, dst_ref=dst, send_sem=ssem, recv_sem=rsem,
            device_id=device, device_id_type=MESH,
        )

    def member(g, dm, db):
        return (g // 2 + dm) % 4 * 2 + (g + db) % 2

    def rows_dev(g):
        return (g * 2 + c, l)

    def lat_dev(g):
        return (r, g)

    def shard_at(g):
        return pl.multiple_of((g * 2 + c) * SH, 32)

    def shard(g, core):
        return pl.ds(pl.multiple_of((g * 2 + core) * SH, 32), SH)

    def chunk_at(g):
        return pl.multiple_of(g * CH, 64)

    def chunk(g):
        return pl.ds(chunk_at(g), CH)

    barrier = pltpu.get_barrier_semaphore()
    for k in range(1, 16):
        pl.semaphore_signal(barrier, inc=1, device_id=((r + k) % 16, l), device_id_type=MESH)
    for dm, db in ((0, 1), (1, 0), (2, 0), (3, 0)):
        pl.semaphore_signal(barrier, inc=1, device_id=lat_dev(member(l, dm, db)), device_id_type=MESH)
    batch_cp = pltpu.make_async_copy(batch_h, batch, loc.at[0])
    enc_cp = pltpu.make_async_copy(encw, encf.at[shard(q, c)], loc.at[1])
    dec_cp = pltpu.make_async_copy(decw, decf.at[shard(q, c)], loc.at[2])
    next_cp = pltpu.make_async_copy(next_h, nacts, loc.at[3])
    next_cp.start()
    enc_cp.start()
    batch_cp.start()
    dec_cp.start()
    with jax.named_scope("barrier"):
        pl.semaphore_wait(barrier, 19)

    class Gather:
        def __init__(self, full, at, g, dev, ssem, rsem, size, size_a):
            self.full, self.at, self.g, self.dev, self.s, self.r = full, at, g, dev, ssem, rsem
            self.size, self.size_a = size, size_a

        def part(self, g, which):
            if which == "a":
                return self.full.at[pl.ds(self.at(g), self.size_a)]
            return self.full.at[pl.ds(self.at(g) + self.size_a, self.size - self.size_a)]

        def copy(self, g, which, slot, to):
            part = self.part(g, which)
            return remote(part, part, self.s.at[slot], self.r.at[slot], self.dev(to))

        def own(self, dm, db, which):
            slot = dm if which == "a" else 4 + dm
            return self.copy(self.g, which, slot, member(self.g, dm, db))

        def came(self, dm, db, which):
            slot = dm if which == "a" else 4 + dm
            return self.copy(member(self.g, 4 - dm, db), which, slot, self.g)

        def on_a(self, j):
            return self.copy(member(self.g, 0, 1), "a", 8 + j, member(self.g, j, 0))

        def on_b(self, j):
            return self.copy(member(self.g, 4 - j, 0), "b", 12 + j, member(self.g, 0, 1))

        def diag_a(self, j):
            return self.copy(member(self.g, 4 - j, 1), "a", 8 + j, self.g)

        def diag_b(self, j):
            return self.copy(member(self.g, 4 - j, 1), "b", 12 + j, self.g)

        def start(self):
            self.own(0, 1, "a").start()
            for j in (1, 3, 2):
                self.own(j, 0, "b").start()
            self.own(0, 1, "b").start()
            for j in (1, 3, 2):
                self.own(j, 0, "a").start()

        def forward_a(self):
            self.came(0, 1, "a").wait_recv()
            for j in (2, 1, 3):
                self.on_a(j).start()

        def forward_b(self, j):
            self.came(j, 0, "b").wait_recv()
            self.on_b(j).start()

        def take_pair(self):
            self.came(0, 1, "b").wait_recv()

        def take_ring(self, j):
            self.came(j, 0, "a").wait_recv()

        def take_diag(self, j):
            self.diag_a(j).wait_recv()
            self.diag_b(j).wait_recv()

        def drain(self):
            for dm, db in ((0, 1), (1, 0), (2, 0), (3, 0)):
                self.own(dm, db, "a").wait_send()
                self.own(dm, db, "b").wait_send()
            for j in (1, 2, 3):
                self.on_a(j).wait_send()
                self.on_b(j).wait_send()

    class Scatter:
        def __init__(self, part, rec_a, rec_y, rec_b, rec_p, g, dev, ssem, rsem, size, size_a):
            self.p, self.ra, self.ry, self.rb, self.rp = part, rec_a, rec_y, rec_b, rec_p
            self.g, self.dev, self.s, self.r = g, dev, ssem, rsem
            self.a, self.b = pl.ds(0, size_a), pl.ds(size_a, size - size_a)

        def copy(self, src, dst, slot, to):
            return remote(src, dst, self.s.at[slot], self.r.at[slot], self.dev(to))

        def diag_a(self, j):
            src = self.p.at[member(self.g, j, 1), self.a]
            return self.copy(src, self.ra.at[j - 1], j, member(self.g, j, 0))

        def diag_b(self, j):
            src = self.p.at[member(self.g, j, 1), self.b]
            return self.copy(src, self.ry.at[j], 4 + j, member(self.g, 0, 1))

        def ring_a(self, j):
            src = self.p.at[member(self.g, j, 0), self.a]
            return self.copy(src, self.ra.at[2 + j], 8 + j, member(self.g, j, 0))

        def ring_b(self, j):
            src = self.p.at[member(self.g, j, 0), self.b]
            return self.copy(src, self.rb.at[j - 1], 12 + j, member(self.g, j, 0))

        def pair_b(self):
            src = self.p.at[member(self.g, 0, 1), self.b]
            return self.copy(src, self.ry.at[0], 4, member(self.g, 0, 1))

        def pair_a(self):
            src = self.p.at[member(self.g, 0, 1), self.a]
            return self.copy(src, self.rp, 8, member(self.g, 0, 1))

        def emit(self, p):
            dm = (p // 2 + 4 - self.g // 2) % 4
            db = (p + self.g) % 2

            @pl.when(jnp.logical_and(db == 1, dm > 0))
            def _():
                self.diag_b(dm).start()
                self.diag_a(dm).start()

            @pl.when(jnp.logical_and(db == 0, dm > 0))
            def _():
                self.ring_a(dm).start()

            @pl.when(jnp.logical_and(db == 1, dm == 0))
            def _():
                self.pair_b().start()

        def pass_on(self):
            for j in (2, 3, 1):
                self.diag_b(j).wait_recv()
                block = self.p.at[member(self.g, j, 0), self.b]
                block[...] = (block[...].astype(F32) + self.ry[j].astype(F32)).astype(BF)
                self.ring_b(j).start()
            block = self.p.at[member(self.g, 0, 1), self.a]
            total = block[...].astype(F32)
            for j in (2, 3, 1):
                self.diag_a(j).wait_recv()
                total = total + self.ra[j - 1].astype(F32)
            block[...] = total.astype(BF)
            self.pair_a().start()

        def finish(self, own):
            for j in (1, 2, 3):
                self.ring_a(j).wait_recv()
            total = own[self.a, :]
            for j in (1, 2, 3):
                total = total + self.ra[2 + j].astype(F32)
            self.pair_b().wait_recv()
            rest = own[self.b, :] + self.ry[0].astype(F32)
            for j in (2, 3, 1):
                self.ring_b(j).wait_recv()
                rest = rest + self.rb[j - 1].astype(F32)
            own[self.b, :] = rest
            self.pair_a().wait_recv()
            own[self.a, :] = total + self.rp[...].astype(F32)

        def drain(self):
            for j in (1, 2, 3):
                self.diag_a(j).wait_send()
                self.diag_b(j).wait_send()
                self.ring_a(j).wait_send()
                self.ring_b(j).wait_send()
            self.pair_a().wait_send()
            self.pair_b().wait_send()

    class Weights(Gather):
        def __init__(self, full, ssem, rsem, xs, xr):
            super().__init__(full, shard_at, q, rows_dev, ssem, rsem, SH, SH_A)
            self.xs, self.xr = xs, xr

        def cross(self, dm, db):
            part = self.full.at[shard(member(q, 4 - dm, db), c)]
            return remote(part, part, self.xs.at[dm * 2 + db], self.xr.at[dm * 2 + db], sib)

        def crossed(self, dm, db):
            part = self.full.at[shard(member(q, 4 - dm, db), 1 - c)]
            return remote(part, part, self.xs.at[dm * 2 + db], self.xr.at[dm * 2 + db], sib)

        def collect(self):
            for j in (1, 3, 2):
                self.forward_b(j)
            self.take_pair()
            self.cross(0, 1).start()
            for j in (1, 3, 2):
                self.take_ring(j)
                self.cross(j, 0).start()

        def settle(self):
            for j in (1, 3, 2):
                self.take_diag(j)
                self.cross(j, 1).start()
            for i in range(8):
                self.crossed(i // 2, i % 2).wait_recv()

        def drain(self):
            super().drain()
            for i in range(8):
                self.cross(i // 2, i % 2).wait_send()

    enc_g = Weights(encf, enc_s, enc_r, encx_s, encx_r)
    dec_g = Weights(decf, dec_s, dec_r, decx_s, decx_r)
    enc_cp.wait()
    enc_g.start()
    enc_g.cross(0, 0).start()

    with jax.named_scope("next_cp"):
        next_cp.wait()
    lane48 = lax.broadcasted_iota(jnp.int32, (48, 48), 1)
    sub48 = lax.broadcasted_iota(jnp.int32, (48, 48), 0)
    mine = (r * 8 + l) * 48

    def find(j, dest):
        cols = pl.ds(pl.multiple_of(j * 512, 512), 512)
        ids = jnp.broadcast_to(source[:, cols], (48, 512))
        sub = lax.broadcasted_iota(jnp.int32, (48, 512), 0)
        lane = lax.broadcasted_iota(jnp.int32, (48, 512), 1)
        hit = jnp.where(ids == sub + mine, lane + j * 512, 0)
        return dest + jnp.sum(hit.astype(F32), axis=1, keepdims=True)

    dest = lax.fori_loop(0, 12, find, jnp.zeros((48, 1), F32))
    dest_row = jnp.sum(jnp.where(lane48 == sub48, dest, 0.0), axis=0, keepdims=True)
    slot = jnp.sum(jnp.where(dest < dest_row, 1.0, 0.0), axis=0, keepdims=True)
    pick = jnp.where(slot == sub48.astype(F32), 1.0, 0.0).astype(BF)
    tmp[...] = jnp.dot(pick, nacts[...], preferred_element_type=F32)
    for g in range(16):
        out3[g, 0:3, :] = tmp[3 * g : 3 * g + 3, :].astype(BF)

    def to_group(k):
        return remote(
            out3.at[(r + k) % 16], in3.at[r], a2a_s.at[k - 1], a2a_r.at[k - 1], ((r + k) % 16, l)
        )

    def from_group(k):
        part = in3.at[(r + 16 - k) % 16]
        return remote(part, part, a2a_s.at[k - 1], a2a_r.at[k - 1], (r, l))

    def send_group(k, _):
        to_group(k).start()
        return 0

    with jax.named_scope("send_group"):
        lax.fori_loop(1, 16, send_group, 0)
    in3[r] = out3[r]

    dec_cp.wait()
    dec_g.cross(0, 0).start()
    with jax.named_scope("enc_fwd_a"):
        enc_g.forward_a()

    batch_cp.wait()

    def center(j, _):
        cols = pl.ds(pl.multiple_of(j * 128, 128), 128)
        x = batch[:, cols].astype(F32) - dec_bias[pl.ds(j, 1), :]
        cent[:, cols] = x.astype(BF)
        xt = x.T
        cent_t[pl.ds(pl.multiple_of(j * 128, 128), 128), :] = xt.astype(BF)
        for half in range(2):
            h = j * 2 + half

            @pl.when(h // 9 == l)
            def _():
                neg_t[pl.ds(pl.multiple_of((h % 9) * 64, 64), 64), :] = xt[64 * half : 64 * half + 64]

        return 0

    with jax.named_scope("center"):
        lax.fori_loop(0, 36, center, 0)

    with jax.named_scope("enc_collect"):
        enc_g.collect()
    dec_g.start()

    def arrive(k, _):
        from_group(k).wait_recv()
        return 0

    with jax.named_scope("a2a_arrive"):
        lax.fori_loop(1, 16, arrive, 0)
    for g in range(16):
        tmp[3 * g : 3 * g + 3, :] = in3[g, 0:3, :].astype(F32)
    rows48[pl.ds(pl.multiple_of(l * 48, 16), 48), :] = tmp[...].astype(BF)

    def next_copy(g, slot, to):
        part = rows48.at[pl.ds(pl.multiple_of(g * 48, 16), 48)]
        return remote(part, part, n_s.at[slot], n_r.at[slot], lat_dev(to))

    def next_own(j):
        return next_copy(l, j, member(l, j, 0) if j else member(l, 0, 1))

    def next_came(j):
        return next_copy(member(l, 4 - j, 0) if j else member(l, 0, 1), j, l)

    def next_on(j):
        return next_copy(member(l, 0, 1), 3 + j, member(l, j, 0))

    def next_diag(j):
        return next_copy(member(l, 4 - j, 1), 3 + j, l)

    for j in range(4):
        next_own(j).start()

    with jax.named_scope("enc_settle"):
        enc_g.settle()
    pre[...] = jnp.broadcast_to(enc_bias[...], (ROWS, LAT))
    with jax.named_scope("dec_fwd_a"):
        dec_g.forward_a()

    def encode(j, _):
        part = pl.ds(pl.multiple_of(j * 1152, 128), 1152)
        pre[...] += jnp.dot(cent[:, part], encf[part, :], preferred_element_type=F32)
        return 0

    with jax.named_scope("encode"):
        lax.fori_loop(0, 4, encode, 0)
    codes[...] = jnp.maximum(pre[...], 0.0).astype(BF)
    with jax.named_scope("dec_collect"):
        dec_g.collect()
    with jax.named_scope("dec_settle"):
        dec_g.settle()

    lat_sum = Scatter(lpart, lrec_a, lrec_y, lrec_b, lrec_p, l, lat_dev, ls_s, ls_r, CH, CH_A)

    def order(g, i):
        return member(g, (i + 2) % 4, 1 - i // 4)

    def decode(i, _):
        p = order(l, i)
        part = lax.dot_general(decf[chunk(p), :], codes[...], NT, preferred_element_type=F32)
        lpart[p] = part.astype(BF)
        lat_sum.emit(p)

        @pl.when(i == 6)
        def _():
            recon[...] = part - neg_t[...]

        return 0

    with jax.named_scope("decode"):
        lax.fori_loop(0, 8, decode, 0)
    with jax.named_scope("lat_pass"):
        lat_sum.pass_on()
    with jax.named_scope("lat_finish"):
        lat_sum.finish(recon)
    err[chunk(l), :] = recon[...].astype(BF)
    err_out[...] = err[chunk(l), :]

    err_g = Gather(err, chunk_at, l, lat_dev, err_s, err_r, CH, CH_A)
    err_g.start()
    gcodes[...] = jnp.full((ROWS, LAT), sparsity_weight, F32)

    def grad_block(lhs, rhs, p, scale, sib_r, own, scatter, xs, xr):
        other = jnp.dot(lhs[shard(p, 1 - c), :], rhs[...], preferred_element_type=F32)
        sib_s[p] = (other * scale).astype(BF)
        cross = remote(sib_s.at[p], sib_r.at[p], xs.at[p], xr.at[p], sib)
        cross.start()
        mine = jnp.dot(lhs[shard(p, c), :], rhs[...], preferred_element_type=F32) * scale
        cross.wait_recv()
        total = mine + sib_r[p].astype(F32)
        scatter.p[p] = total.astype(BF)
        scatter.emit(p)

        @pl.when(p == q)
        def _():
            own[...] = total

    dec_sum = Scatter(dpart, drec_a, drec_y, drec_b, drec_p, q, rows_dev, dg_s, dg_r, SH, SH_A)
    enc_sum = Scatter(epart, erec_a, erec_y, erec_b, erec_p, q, rows_dev, eg_s, eg_r, SH, SH_A)

    def error_block(p):
        gcodes[...] += lax.dot_general(
            err[chunk(p), :], decf[chunk(p), :], TN, preferred_element_type=F32
        )
        grad_block(err, codes, p, inv_tokens, dsib_r, down, dec_sum, dx_s, dx_r)

    with jax.named_scope("err_own"):
        error_block(l)
    with jax.named_scope("err_fwd_a"):
        err_g.forward_a()
    for j in (1, 3, 2):
        err_g.forward_b(j)
    with jax.named_scope("err_take_pair"):
        err_g.take_pair()
    with jax.named_scope("err_pair"):
        error_block(member(l, 0, 1))

    def error_ring(i, _):
        j = (7 - i) % 4
        err_g.take_ring(j)
        error_block(member(l, 4 - j, 0))
        return 0

    with jax.named_scope("err_ring"):
        lax.fori_loop(0, 3, error_ring, 0)

    def error_diag(i, _):
        j = (7 - i) % 4
        err_g.take_diag(j)
        error_block(member(l, 4 - j, 1))
        return 0

    with jax.named_scope("err_diag"):
        lax.fori_loop(0, 3, error_diag, 0)
    with jax.named_scope("next_came"):
        next_came(0).wait_recv()
    for j in (1, 3, 2):
        next_on(j).start()
    cgrad[...] = jnp.where(pre[...] > 0, gcodes[...] * inv_tokens, 0.0).astype(BF)
    with jax.named_scope("dec_pass"):
        dec_sum.pass_on()

    def drain_cross(p, _):
        remote(sib_s.at[p], dsib_r.at[p], dx_s.at[p], dx_r.at[p], sib).wait_send()
        return 0

    with jax.named_scope("drain_cross"):
        lax.fori_loop(0, 8, drain_cross, 0)

    def enc_step(i, _):
        grad_block(cent_t, cgrad, order(q, i), 1.0, esib_r, eown, enc_sum, ex_s, ex_r)
        return 0

    with jax.named_scope("enc_step"):
        lax.fori_loop(0, 8, enc_step, 0)
    with jax.named_scope("enc_pass"):
        enc_sum.pass_on()

    place_l = lax.broadcasted_iota(jnp.int32, (ROWS, ROWS), 1)
    place_s = lax.broadcasted_iota(jnp.int32, (ROWS, ROWS), 0)
    wanted = source[:, pl.ds(pl.multiple_of(r * ROWS, 128), ROWS)]
    owner = jnp.right_shift(wanted * 43691, 21).astype(F32)
    owner_col = jnp.sum(jnp.where(place_l == place_s, owner, 0.0), axis=1, keepdims=True)
    earlier = jnp.logical_and(owner == owner_col, place_l < place_s)
    rank = jnp.sum(jnp.where(earlier, 1.0, 0.0), axis=1, keepdims=True)
    owner_i = owner_col.astype(jnp.int32)
    position = jnp.bitwise_and(owner_i, 7) * 48 + jnp.right_shift(owner_i, 3) * 3 + rank.astype(jnp.int32)
    put = jnp.where(position == place_l, 1.0, 0.0).astype(BF)
    for j in (1, 3, 2):
        next_came(j).wait_recv()
    for j in (1, 3, 2):
        next_diag(j).wait_recv()
    cgrad[:, 0:ROWS] = put

    def permute(j, _):
        cols = pl.ds(pl.multiple_of(j * 512, 512), 512)
        batch[:, cols] = jnp.dot(
            cgrad[:, 0:ROWS], rows48[:, cols], preferred_element_type=F32
        ).astype(BF)
        return 0

    with jax.named_scope("permute"):
        lax.fori_loop(0, 9, permute, 0)
    out_cp = pltpu.make_async_copy(batch, next_out, loc.at[4])
    out_cp.start()

    def update(scatter, own, first, second, outs):
        scatter.finish(own)
        for out, value in zip(outs, adam_update(own[...], first[...], second[...])):
            out[...] = value

    with jax.named_scope("upd_dec"):
        update(dec_sum, down, df, ds, (ndf, nds, dup))
    with jax.named_scope("upd_enc"):
        update(enc_sum, eown, ef, es, (nef, nes, eup))

    with jax.named_scope("drain"):
        enc_g.drain()
    dec_g.drain()
    err_g.drain()
    lat_sum.drain()
    dec_sum.drain()
    enc_sum.drain()

    def drain_group(k, _):
        to_group(k).wait_send()
        return 0

    lax.fori_loop(1, 16, drain_group, 0)
    for j in range(4):
        next_own(j).wait_send()
    for j in (1, 2, 3):
        next_on(j).wait_send()

    def drain_cross2(p, _):
        remote(sib_s.at[p], esib_r.at[p], ex_s.at[p], ex_r.at[p], sib).wait_send()
        return 0

    lax.fori_loop(0, 8, drain_cross2, 0)
    with jax.named_scope("out_wait"):
        out_cp.wait()


def train_step(
    batch, next_acts, encw, decw_t, source, enc_bias, dec_bias, ef, es, df_t, ds_t, inv_tokens
):
    any_space = pl.BlockSpec(memory_space=pl.ANY)
    vmem = pl.BlockSpec(memory_space=pltpu.VMEM)
    dma = pltpu.SemaphoreType.DMA

    def received(size, size_a, width):
        return [
            pltpu.VMEM((8, size, width), BF),
            pltpu.VMEM((6, size_a, width), BF),
            pltpu.VMEM((4, size - size_a, width), BF),
            pltpu.VMEM((3, size - size_a, width), BF),
            pltpu.VMEM((size_a, width), BF),
        ]

    shard = jax.ShapeDtypeStruct((SH, LAT), BF)
    return pl.pallas_call(
        functools.partial(step_kernel, inv_tokens),
        out_shape=(
            jax.ShapeDtypeStruct((ROWS, D), BF),
            jax.ShapeDtypeStruct((ROWS, LAT), BF),
            jax.ShapeDtypeStruct((CH, ROWS), BF),
            *([shard] * 6),
        ),
        in_specs=[any_space] * 4 + [vmem] * 7,
        out_specs=[any_space] + [vmem] * 8,
        scratch_shapes=[
            pltpu.VMEM((ROWS, D), BF),
            pltpu.VMEM((ROWS, D), BF),
            pltpu.VMEM((D, ROWS), BF),
            pltpu.VMEM((CH, ROWS), F32),
            pltpu.VMEM((D, LAT), BF),
            pltpu.VMEM((D, LAT), BF),
            pltpu.VMEM((ROWS, LAT), F32),
            pltpu.VMEM((CH, ROWS), F32),
            pltpu.VMEM((D, ROWS), BF),
            pltpu.VMEM((ROWS, LAT), F32),
            pltpu.VMEM((ROWS, LAT), BF),
            *received(CH, CH_A, ROWS),
            *([pltpu.VMEM((8, SH, LAT), BF)] * 3),
            *received(SH, SH_A, LAT),
            pltpu.VMEM((SH, LAT), F32),
            *received(SH, SH_A, LAT),
            pltpu.VMEM((SH, LAT), F32),
            pltpu.VMEM((48, D), BF),
            pltpu.VMEM((48, D), F32),
            pltpu.VMEM((16, 4, D), BF),
            pltpu.VMEM((16, 4, D), BF),
            pltpu.VMEM((ROWS, D), BF),
            dma((5,)),
            dma((16,)), dma((16,)), dma((8,)), dma((8,)),
            dma((16,)), dma((16,)), dma((8,)), dma((8,)),
            dma((16,)), dma((16,)), dma((16,)), dma((16,)),
            dma((8,)), dma((8,)), dma((16,)), dma((16,)),
            dma((8,)), dma((8,)), dma((16,)), dma((16,)),
            dma((15,)), dma((15,)), dma((7,)), dma((7,)),
        ],
        compiler_params=pltpu.CompilerParams(
            collective_id=0, has_side_effects=True, vmem_limit_bytes=63 * 2**20
        ),
        cost_estimate=pl.CostEstimate(
            flops=5 * 2 * ROWS * LAT * D, bytes_accessed=16 * 2**20, transcendentals=0
        ),
    )(batch, next_acts, encw, decw_t, source, enc_bias, dec_bias, ef, es, df_t, ds_t)


def publish(*arrays):
    n = len(arrays)
    pieces = []
    for i, a in enumerate(arrays):
        step = a.shape[0] // 4 if a.size > 2**20 else a.shape[0]
        pieces += [(i, row, step) for row in range(0, a.shape[0], step)]

    def kernel(*refs):
        held, into, out_of = refs[2 * n : 3 * n], refs[3 * n], refs[3 * n + 1]

        def read(k):
            i, row, rows = pieces[k]
            part = pl.ds(row, rows)
            return pltpu.make_async_copy(refs[i].at[part], held[i].at[part], into.at[k])

        def write(k):
            i, row, rows = pieces[k]
            part = pl.ds(row, rows)
            return pltpu.make_async_copy(held[i].at[part], refs[n + i].at[part], out_of.at[k])

        for k in range(len(pieces)):
            read(k).start()
        for k in range(len(pieces)):
            read(k).wait()
            write(k).start()
        for k in range(len(pieces)):
            write(k).wait()

    any_space = pl.BlockSpec(memory_space=pl.ANY)
    return pl.pallas_call(
        kernel,
        out_shape=tuple(jax.ShapeDtypeStruct(a.shape, a.dtype) for a in arrays),
        in_specs=[any_space] * n,
        out_specs=[any_space] * n,
        scratch_shapes=[
            *[pltpu.VMEM(a.shape, a.dtype) for a in arrays],
            pltpu.SemaphoreType.DMA((len(pieces),)),
            pltpu.SemaphoreType.DMA((len(pieces),)),
        ],
        compiler_params=pltpu.CompilerParams(vmem_limit_bytes=63 * 2**20),
    )(*arrays)


def on_device(
    batch, next_acts, row_source, enc_weight, dec_weight, enc_bias, dec_bias,
    enc_first, enc_second, dec_first, dec_second,
):
    inv_tokens = 1.0 / (batch.shape[0] * 16)
    results = train_step(
        batch, next_acts, enc_weight, dec_weight.T, row_source.reshape(1, -1),
        enc_bias.reshape(1, LAT), dec_bias.reshape(D // 128, 128),
        enc_first, enc_second, dec_first.T, dec_second.T, inv_tokens,
    )
    next_batch, codes, err_t, nef, nes, eup, ndf, nds, dup = publish(*results)
    return next_batch, codes, err_t.T, nef, nes, eup, ndf.T, nds.T, dup.T


def solution(mesh):
    return jax.shard_map(
        on_device,
        mesh=mesh,
        in_specs=(
            P("rows", None),
            P(("rows", "lat"), None),
            P(),
            P("rows", "lat"),
            P("lat", "rows"),
            P("lat"),
            P(),
            P("rows", "lat"),
            P("rows", "lat"),
            P("lat", "rows"),
            P("lat", "rows"),
        ),
        out_specs=(
            P("rows", None),
            P("rows", "lat"),
            P("rows", "lat"),
            P("rows", "lat"),
            P("rows", "lat"),
            P("rows", "lat"),
            P("lat", "rows"),
            P("lat", "rows"),
            P("lat", "rows"),
        ),
        check_vma=False,
    )
```

```python
import functools

import jax
import jax.numpy as jnp
from jax import lax
from jax.experimental import pallas as pl
from jax.experimental.pallas import tpu as pltpu
from jax.sharding import PartitionSpec as P

beta_one = 0.9
beta_two = 0.999
correction_one = 1.0 - 0.9**3
correction_two = 1.0 - 0.999**3
eps_adam = 1e-08
sparsity_weight = 0.2

MESH = pl.DeviceIdType.MESH
BF = jnp.bfloat16
F32 = jnp.float32
D = 4608
ROWS = 384
LAT = 512
SH = 288
CH = 576
CH_A = 224
SH_A = 112
NT = (((1,), (1,)), ((), ()))
TN = (((0,), (0,)), ((), ()))


def adam_update(gradient, first, second):
    first_new = beta_one * first.astype(F32) + (1.0 - beta_one) * gradient
    second_new = beta_two * second.astype(F32) + (1.0 - beta_two) * gradient * gradient
    direction = first_new / correction_one / (jnp.sqrt(second_new / correction_two) + eps_adam)
    return first_new.astype(BF), second_new.astype(BF), direction.astype(BF)


def step_kernel(
    inv_tokens,
    batch_h, next_h, encw, decw, source, enc_bias, dec_bias, ef, es, df, ds,
    next_out, codes, err_out, nef, nes, eup, ndf, nds, dup,
    batch, cent, cent_t, neg_t, encf, decf, pre, recon, err, gcodes, cgrad,
    lpart, lrec_a, lrec_y, lrec_b, lrec_p,
    sib_s, dsib_r, esib_r, kept,
    dpart, drec_a, drec_y, drec_b, drec_p, down,
    epart, erec_a, erec_y, erec_b, erec_p, eown,
    nacts, tmp, out3, in3, rows48,
    loc, enc_s, enc_r, encx_s, encx_r, dec_s, dec_r, decx_s, decx_r,
    ls_s, ls_r, err_s, err_r, dx_s, dx_r, dg_s, dg_r, ex_s, ex_r, eg_s, eg_r,
    a2a_s, a2a_r, n_s, n_r,
):
    r = lax.axis_index("rows")
    l = lax.axis_index("lat")
    c = r % 2
    q = r // 2
    sib = (q * 2 + 1 - c, l)

    def remote(src, dst, ssem, rsem, device):
        return pltpu.make_async_remote_copy(
            src_ref=src, dst_ref=dst, send_sem=ssem, recv_sem=rsem,
            device_id=device, device_id_type=MESH,
        )

    def member(g, dm, db):
        return (g // 2 + dm) % 4 * 2 + (g + db) % 2

    def rows_dev(g):
        return (g * 2 + c, l)

    def lat_dev(g):
        return (r, g)

    def shard_at(g):
        return pl.multiple_of((g * 2 + c) * SH, 32)

    def shard(g, core):
        return pl.ds(pl.multiple_of((g * 2 + core) * SH, 32), SH)

    def chunk_at(g):
        return pl.multiple_of(g * CH, 64)

    def chunk(g):
        return pl.ds(chunk_at(g), CH)

    barrier = pltpu.get_barrier_semaphore()
    for k in range(1, 16):
        pl.semaphore_signal(barrier, inc=1, device_id=((r + k) % 16, l), device_id_type=MESH)
    for dm, db in ((0, 1), (1, 0), (2, 0), (3, 0)):
        pl.semaphore_signal(barrier, inc=1, device_id=lat_dev(member(l, dm, db)), device_id_type=MESH)
    batch_cp = pltpu.make_async_copy(batch_h, batch, loc.at[0])
    enc_cp = pltpu.make_async_copy(encw, encf.at[shard(q, c)], loc.at[1])
    dec_cp = pltpu.make_async_copy(decw, decf.at[shard(q, c)], loc.at[2])
    next_cp = pltpu.make_async_copy(next_h, nacts, loc.at[3])
    next_cp.start()
    enc_cp.start()
    batch_cp.start()
    dec_cp.start()
    pl.semaphore_wait(barrier, 19)

    class Gather:
        def __init__(self, full, at, g, dev, ssem, rsem, size, size_a):
            self.full, self.at, self.g, self.dev, self.s, self.r = full, at, g, dev, ssem, rsem
            self.size, self.size_a = size, size_a

        def part(self, g, which):
            if which == "a":
                return self.full.at[pl.ds(self.at(g), self.size_a)]
            return self.full.at[pl.ds(self.at(g) + self.size_a, self.size - self.size_a)]

        def copy(self, g, which, slot, to):
            part = self.part(g, which)
            return remote(part, part, self.s.at[slot], self.r.at[slot], self.dev(to))

        def own(self, dm, db, which):
            slot = dm if which == "a" else 4 + dm
            return self.copy(self.g, which, slot, member(self.g, dm, db))

        def came(self, dm, db, which):
            slot = dm if which == "a" else 4 + dm
            return self.copy(member(self.g, 4 - dm, db), which, slot, self.g)

        def on_a(self, j):
            return self.copy(member(self.g, 0, 1), "a", 8 + j, member(self.g, j, 0))

        def on_b(self, j):
            return self.copy(member(self.g, 4 - j, 0), "b", 12 + j, member(self.g, 0, 1))

        def diag_a(self, j):
            return self.copy(member(self.g, 4 - j, 1), "a", 8 + j, self.g)

        def diag_b(self, j):
            return self.copy(member(self.g, 4 - j, 1), "b", 12 + j, self.g)

        def start(self):
            self.own(0, 1, "a").start()
            for j in (1, 3, 2):
                self.own(j, 0, "b").start()
            self.own(0, 1, "b").start()
            for j in (1, 3, 2):
                self.own(j, 0, "a").start()

        def forward_a(self):
            self.came(0, 1, "a").wait_recv()
            for j in (2, 1, 3):
                self.on_a(j).start()

        def forward_b(self, j):
            self.came(j, 0, "b").wait_recv()
            self.on_b(j).start()

        def take_pair(self):
            self.came(0, 1, "b").wait_recv()

        def take_ring(self, j):
            self.came(j, 0, "a").wait_recv()

        def take_diag(self, j):
            self.diag_a(j).wait_recv()
            self.diag_b(j).wait_recv()

        def drain(self):
            for dm, db in ((0, 1), (1, 0), (2, 0), (3, 0)):
                self.own(dm, db, "a").wait_send()
                self.own(dm, db, "b").wait_send()
            for j in (1, 2, 3):
                self.on_a(j).wait_send()
                self.on_b(j).wait_send()

    class Scatter:
        def __init__(self, part, rec_a, rec_y, rec_b, rec_p, g, dev, ssem, rsem, size, size_a):
            self.p, self.ra, self.ry, self.rb, self.rp = part, rec_a, rec_y, rec_b, rec_p
            self.g, self.dev, self.s, self.r = g, dev, ssem, rsem
            self.a, self.b = pl.ds(0, size_a), pl.ds(size_a, size - size_a)

        def copy(self, src, dst, slot, to):
            return remote(src, dst, self.s.at[slot], self.r.at[slot], self.dev(to))

        def diag_a(self, j):
            src = self.p.at[member(self.g, j, 1), self.a]
            return self.copy(src, self.ra.at[j - 1], j, member(self.g, j, 0))

        def diag_b(self, j):
            src = self.p.at[member(self.g, j, 1), self.b]
            return self.copy(src, self.ry.at[j], 4 + j, member(self.g, 0, 1))

        def ring_a(self, j):
            src = self.p.at[member(self.g, j, 0), self.a]
            return self.copy(src, self.ra.at[2 + j], 8 + j, member(self.g, j, 0))

        def ring_b(self, j):
            src = self.p.at[member(self.g, j, 0), self.b]
            return self.copy(src, self.rb.at[j - 1], 12 + j, member(self.g, j, 0))

        def pair_b(self):
            src = self.p.at[member(self.g, 0, 1), self.b]
            return self.copy(src, self.ry.at[0], 4, member(self.g, 0, 1))

        def pair_a(self):
            src = self.p.at[member(self.g, 0, 1), self.a]
            return self.copy(src, self.rp, 8, member(self.g, 0, 1))

        def emit(self, p):
            dm = (p // 2 + 4 - self.g // 2) % 4
            db = (p + self.g) % 2

            @pl.when(jnp.logical_and(db == 1, dm > 0))
            def _():
                self.diag_b(dm).start()
                self.diag_a(dm).start()

            @pl.when(jnp.logical_and(db == 0, dm > 0))
            def _():
                self.ring_a(dm).start()

            @pl.when(jnp.logical_and(db == 1, dm == 0))
            def _():
                self.pair_b().start()

        def pass_on(self):
            for j in (2, 3, 1):
                self.diag_b(j).wait_recv()
                block = self.p.at[member(self.g, j, 0), self.b]
                block[...] = (block[...].astype(F32) + self.ry[j].astype(F32)).astype(BF)
                self.ring_b(j).start()
            block = self.p.at[member(self.g, 0, 1), self.a]
            total = block[...].astype(F32)
            for j in (2, 3, 1):
                self.diag_a(j).wait_recv()
                total = total + self.ra[j - 1].astype(F32)
            block[...] = total.astype(BF)
            self.pair_a().start()

        def finish(self, own):
            for j in (1, 2, 3):
                self.ring_a(j).wait_recv()
            total = own[self.a, :]
            for j in (1, 2, 3):
                total = total + self.ra[2 + j].astype(F32)
            self.pair_b().wait_recv()
            rest = own[self.b, :] + self.ry[0].astype(F32)
            for j in (2, 3, 1):
                self.ring_b(j).wait_recv()
                rest = rest + self.rb[j - 1].astype(F32)
            own[self.b, :] = rest
            self.pair_a().wait_recv()
            own[self.a, :] = total + self.rp[...].astype(F32)

        def drain(self):
            for j in (1, 2, 3):
                self.diag_a(j).wait_send()
                self.diag_b(j).wait_send()
                self.ring_a(j).wait_send()
                self.ring_b(j).wait_send()
            self.pair_a().wait_send()
            self.pair_b().wait_send()

    class Weights(Gather):
        def __init__(self, full, ssem, rsem, xs, xr):
            super().__init__(full, shard_at, q, rows_dev, ssem, rsem, SH, SH_A)
            self.xs, self.xr = xs, xr

        def cross(self, dm, db):
            part = self.full.at[shard(member(q, 4 - dm, db), c)]
            return remote(part, part, self.xs.at[dm * 2 + db], self.xr.at[dm * 2 + db], sib)

        def crossed(self, dm, db):
            part = self.full.at[shard(member(q, 4 - dm, db), 1 - c)]
            return remote(part, part, self.xs.at[dm * 2 + db], self.xr.at[dm * 2 + db], sib)

        def cross_pair(self):
            self.take_pair()
            self.cross(0, 1).start()

        def cross_ring(self):
            for j in (1, 3, 2):
                self.take_ring(j)
                self.cross(j, 0).start()

        def settle(self):
            for j in (1, 3, 2):
                self.take_diag(j)
                self.cross(j, 1).start()
            for i in range(8):
                self.crossed(i // 2, i % 2).wait_recv()

        def drain(self):
            super().drain()
            for i in range(8):
                self.cross(i // 2, i % 2).wait_send()

    enc_g = Weights(encf, enc_s, enc_r, encx_s, encx_r)
    dec_g = Weights(decf, dec_s, dec_r, decx_s, decx_r)
    enc_cp.wait()
    enc_g.start()
    enc_g.cross(0, 0).start()

    next_cp.wait()
    lane48 = lax.broadcasted_iota(jnp.int32, (48, 48), 1)
    sub48 = lax.broadcasted_iota(jnp.int32, (48, 48), 0)
    mine = (r * 8 + l) * 48

    def find(j, dest):
        cols = pl.ds(pl.multiple_of(j * 512, 512), 512)
        ids = jnp.broadcast_to(source[:, cols], (48, 512))
        sub = lax.broadcasted_iota(jnp.int32, (48, 512), 0)
        lane = lax.broadcasted_iota(jnp.int32, (48, 512), 1)
        hit = jnp.where(ids == sub + mine, lane + j * 512, 0)
        return dest + jnp.sum(hit.astype(F32), axis=1, keepdims=True)

    dest = lax.fori_loop(0, 12, find, jnp.zeros((48, 1), F32))
    dest_row = jnp.sum(jnp.where(lane48 == sub48, dest, 0.0), axis=0, keepdims=True)
    slot = jnp.sum(jnp.where(dest < dest_row, 1.0, 0.0), axis=0, keepdims=True)
    pick = jnp.where(slot == sub48.astype(F32), 1.0, 0.0).astype(BF)
    tmp[...] = jnp.dot(pick, nacts[...], preferred_element_type=F32)
    for g in range(16):
        out3[g, 0:3, :] = tmp[3 * g : 3 * g + 3, :].astype(BF)

    def to_group(k):
        return remote(
            out3.at[(r + k) % 16], in3.at[r], a2a_s.at[k - 1], a2a_r.at[k - 1], ((r + k) % 16, l)
        )

    def from_group(k):
        part = in3.at[(r + 16 - k) % 16]
        return remote(part, part, a2a_s.at[k - 1], a2a_r.at[k - 1], (r, l))

    def send_group(k, _):
        to_group(k).start()
        return 0

    lax.fori_loop(1, 16, send_group, 0)
    in3[r] = out3[r]
    enc_g.forward_a()
    for j in (1, 3, 2):
        enc_g.forward_b(j)
    dec_cp.wait()
    dec_g.start()
    dec_g.cross(0, 0).start()
    enc_g.cross_pair()

    batch_cp.wait()

    def center(j, _):
        cols = pl.ds(pl.multiple_of(j * 128, 128), 128)
        x = batch[:, cols].astype(F32) - dec_bias[pl.ds(j, 1), :]
        cent[:, cols] = x.astype(BF)
        xt = x.T
        cent_t[pl.ds(pl.multiple_of(j * 128, 128), 128), :] = xt.astype(BF)
        for half in range(2):
            h = j * 2 + half

            @pl.when(h // 9 == l)
            def _():
                neg_t[pl.ds(pl.multiple_of((h % 9) * 64, 64), 64), :] = xt[64 * half : 64 * half + 64]

        return 0

    lax.fori_loop(0, 12, center, 0)
    dec_g.forward_a()
    lax.fori_loop(12, 24, center, 0)
    enc_g.cross_ring()
    dec_g.forward_b(1)
    lax.fori_loop(24, 36, center, 0)
    for j in (3, 2):
        dec_g.forward_b(j)

    def arrive(k, _):
        from_group(k).wait_recv()
        return 0

    lax.fori_loop(1, 16, arrive, 0)
    for g in range(16):
        tmp[3 * g : 3 * g + 3, :] = in3[g, 0:3, :].astype(F32)
    rows48[pl.ds(pl.multiple_of(l * 48, 16), 48), :] = tmp[...].astype(BF)

    def next_copy(g, slot, to):
        part = rows48.at[pl.ds(pl.multiple_of(g * 48, 16), 48)]
        return remote(part, part, n_s.at[slot], n_r.at[slot], lat_dev(to))

    def next_own(j):
        return next_copy(l, j, member(l, j, 0) if j else member(l, 0, 1))

    def next_came(j):
        return next_copy(member(l, 4 - j, 0) if j else member(l, 0, 1), j, l)

    def next_on(j):
        return next_copy(member(l, 0, 1), 3 + j, member(l, j, 0))

    def next_diag(j):
        return next_copy(member(l, 4 - j, 1), 3 + j, l)

    for j in range(4):
        next_own(j).start()

    enc_g.settle()
    pre[...] = jnp.broadcast_to(enc_bias[...], (ROWS, LAT))

    def encode(j, _):
        part = pl.ds(pl.multiple_of(j * 1152, 128), 1152)
        pre[...] += jnp.dot(cent[:, part], encf[part, :], preferred_element_type=F32)
        return 0

    lax.fori_loop(0, 4, encode, 0)
    codes[...] = jnp.maximum(pre[...], 0.0).astype(BF)
    dec_g.cross_pair()
    dec_g.cross_ring()

    dec_g.settle()

    lat_sum = Scatter(lpart, lrec_a, lrec_y, lrec_b, lrec_p, l, lat_dev, ls_s, ls_r, CH, CH_A)

    def order(g, i):
        return member(g, (i + 2) % 4, 1 - i // 4)

    def decode(i, _):
        p = order(l, i)
        part = lax.dot_general(decf[chunk(p), :], codes[...], NT, preferred_element_type=F32)
        lpart[p] = part.astype(BF)
        lat_sum.emit(p)

        @pl.when(i == 6)
        def _():
            recon[...] = part - neg_t[...]

        return 0

    lax.fori_loop(0, 8, decode, 0)
    lat_sum.pass_on()
    lat_sum.finish(recon)
    err[chunk(l), :] = recon[...].astype(BF)
    err_out[...] = err[chunk(l), :]

    err_g = Gather(err, chunk_at, l, lat_dev, err_s, err_r, CH, CH_A)
    err_g.start()
    gcodes[...] = jnp.full((ROWS, LAT), sparsity_weight, F32)

    def grad_begin(lhs, rhs, p, hold, scale, sib_r, xs, xr):
        other = jnp.dot(lhs[shard(p, 1 - c), :], rhs[...], preferred_element_type=F32)
        sib_s[p] = (other * scale).astype(BF)
        remote(sib_s.at[p], sib_r.at[p], xs.at[p], xr.at[p], sib).start()
        mine = jnp.dot(lhs[shard(p, c), :], rhs[...], preferred_element_type=F32)
        kept[hold] = mine * scale

    def grad_end(p, hold, sib_r, own, scatter, xs, xr):
        remote(sib_s.at[p], sib_r.at[p], xs.at[p], xr.at[p], sib).wait_recv()
        total = kept[hold] + sib_r[p].astype(F32)
        scatter.p[p] = total.astype(BF)
        scatter.emit(p)

        @pl.when(p == q)
        def _():
            own[...] = total

    dec_sum = Scatter(dpart, drec_a, drec_y, drec_b, drec_p, q, rows_dev, dg_s, dg_r, SH, SH_A)
    enc_sum = Scatter(epart, erec_a, erec_y, erec_b, erec_p, q, rows_dev, eg_s, eg_r, SH, SH_A)

    def error_begin(dm, db, hold):
        p = member(l, dm, db)
        gcodes[...] += lax.dot_general(
            err[chunk(p), :], decf[chunk(p), :], TN, preferred_element_type=F32
        )
        grad_begin(err, codes, p, hold, inv_tokens, dsib_r, dx_s, dx_r)

    def error_end(dm, db, hold):
        grad_end(member(l, dm, db), hold, dsib_r, down, dec_sum, dx_s, dx_r)

    error_begin(0, 0, 0)
    err_g.forward_a()
    err_g.forward_b(1)
    error_end(0, 0, 0)
    err_g.forward_b(3)
    err_g.take_pair()
    error_begin(0, 1, 1)
    err_g.forward_b(2)
    before = (0, 1)
    for i, (j, db) in enumerate(((1, 0), (3, 0), (2, 0), (1, 1), (3, 1), (2, 1))):
        if db:
            err_g.take_diag(j)
        else:
            err_g.take_ring(j)
        error_begin(4 - j, db, i % 2)
        error_end(*before, (i + 1) % 2)
        before = (4 - j, db)
    error_end(*before, 1)
    next_came(0).wait_recv()
    for j in (1, 3, 2):
        next_on(j).start()
    cgrad[...] = jnp.where(pre[...] > 0, gcodes[...] * inv_tokens, 0.0).astype(BF)

    def drain_cross(p, _):
        remote(sib_s.at[p], dsib_r.at[p], dx_s.at[p], dx_r.at[p], sib).wait_send()
        return 0

    lax.fori_loop(0, 8, drain_cross, 0)

    def enc_step(i, _):
        grad_begin(cent_t, cgrad, order(q, i), i % 2, 1.0, esib_r, ex_s, ex_r)

        @pl.when(i > 0)
        def _():
            grad_end(order(q, i - 1), (i + 1) % 2, esib_r, eown, enc_sum, ex_s, ex_r)

        return 0

    lax.fori_loop(0, 8, enc_step, 0)
    grad_end(order(q, 7), 1, esib_r, eown, enc_sum, ex_s, ex_r)
    dec_sum.pass_on()
    enc_sum.pass_on()

    place_l = lax.broadcasted_iota(jnp.int32, (ROWS, ROWS), 1)
    place_s = lax.broadcasted_iota(jnp.int32, (ROWS, ROWS), 0)
    wanted = source[:, pl.ds(pl.multiple_of(r * ROWS, 128), ROWS)]
    owner = jnp.right_shift(wanted * 43691, 21).astype(F32)
    owner_col = jnp.sum(jnp.where(place_l == place_s, owner, 0.0), axis=1, keepdims=True)
    earlier = jnp.logical_and(owner == owner_col, place_l < place_s)
    rank = jnp.sum(jnp.where(earlier, 1.0, 0.0), axis=1, keepdims=True)
    owner_i = owner_col.astype(jnp.int32)
    position = jnp.bitwise_and(owner_i, 7) * 48 + jnp.right_shift(owner_i, 3) * 3 + rank.astype(jnp.int32)
    put = jnp.where(position == place_l, 1.0, 0.0).astype(BF)
    for j in (1, 3, 2):
        next_came(j).wait_recv()
    for j in (1, 3, 2):
        next_diag(j).wait_recv()
    cgrad[:, 0:ROWS] = put

    def permute(j, _):
        cols = pl.ds(pl.multiple_of(j * 512, 512), 512)
        batch[:, cols] = jnp.dot(
            cgrad[:, 0:ROWS], rows48[:, cols], preferred_element_type=F32
        ).astype(BF)
        return 0

    lax.fori_loop(0, 9, permute, 0)
    out_cp = pltpu.make_async_copy(batch, next_out, loc.at[4])
    out_cp.start()

    def update(scatter, own, first, second, outs):
        scatter.finish(own)
        for out, value in zip(outs, adam_update(own[...], first[...], second[...])):
            out[...] = value

    update(dec_sum, down, df, ds, (ndf, nds, dup))
    update(enc_sum, eown, ef, es, (nef, nes, eup))

    enc_g.drain()
    dec_g.drain()
    err_g.drain()
    lat_sum.drain()
    dec_sum.drain()
    enc_sum.drain()

    def drain_group(k, _):
        to_group(k).wait_send()
        return 0

    lax.fori_loop(1, 16, drain_group, 0)
    for j in range(4):
        next_own(j).wait_send()
    for j in (1, 2, 3):
        next_on(j).wait_send()

    def drain_cross2(p, _):
        remote(sib_s.at[p], esib_r.at[p], ex_s.at[p], ex_r.at[p], sib).wait_send()
        return 0

    lax.fori_loop(0, 8, drain_cross2, 0)
    out_cp.wait()


def train_step(
    batch, next_acts, encw, decw_t, source, enc_bias, dec_bias, ef, es, df_t, ds_t, inv_tokens
):
    any_space = pl.BlockSpec(memory_space=pl.ANY)
    vmem = pl.BlockSpec(memory_space=pltpu.VMEM)
    dma = pltpu.SemaphoreType.DMA

    def received(size, size_a, width):
        return [
            pltpu.VMEM((8, size, width), BF),
            pltpu.VMEM((6, size_a, width), BF),
            pltpu.VMEM((4, size - size_a, width), BF),
            pltpu.VMEM((3, size - size_a, width), BF),
            pltpu.VMEM((size_a, width), BF),
        ]

    shard = jax.ShapeDtypeStruct((SH, LAT), BF)
    return pl.pallas_call(
        functools.partial(step_kernel, inv_tokens),
        out_shape=(
            jax.ShapeDtypeStruct((ROWS, D), BF),
            jax.ShapeDtypeStruct((ROWS, LAT), BF),
            jax.ShapeDtypeStruct((CH, ROWS), BF),
            *([shard] * 6),
        ),
        in_specs=[any_space] * 4 + [vmem] * 7,
        out_specs=[any_space] + [vmem] * 8,
        scratch_shapes=[
            pltpu.VMEM((ROWS, D), BF),
            pltpu.VMEM((ROWS, D), BF),
            pltpu.VMEM((D, ROWS), BF),
            pltpu.VMEM((CH, ROWS), F32),
            pltpu.VMEM((D, LAT), BF),
            pltpu.VMEM((D, LAT), BF),
            pltpu.VMEM((ROWS, LAT), F32),
            pltpu.VMEM((CH, ROWS), F32),
            pltpu.VMEM((D, ROWS), BF),
            pltpu.VMEM((ROWS, LAT), F32),
            pltpu.VMEM((ROWS, LAT), BF),
            *received(CH, CH_A, ROWS),
            *([pltpu.VMEM((8, SH, LAT), BF)] * 3),
            pltpu.VMEM((2, SH, LAT), F32),
            *received(SH, SH_A, LAT),
            pltpu.VMEM((SH, LAT), F32),
            *received(SH, SH_A, LAT),
            pltpu.VMEM((SH, LAT), F32),
            pltpu.VMEM((48, D), BF),
            pltpu.VMEM((48, D), F32),
            pltpu.VMEM((16, 4, D), BF),
            pltpu.VMEM((16, 4, D), BF),
            pltpu.VMEM((ROWS, D), BF),
            dma((5,)),
            dma((16,)), dma((16,)), dma((8,)), dma((8,)),
            dma((16,)), dma((16,)), dma((8,)), dma((8,)),
            dma((16,)), dma((16,)), dma((16,)), dma((16,)),
            dma((8,)), dma((8,)), dma((16,)), dma((16,)),
            dma((8,)), dma((8,)), dma((16,)), dma((16,)),
            dma((15,)), dma((15,)), dma((7,)), dma((7,)),
        ],
        compiler_params=pltpu.CompilerParams(
            collective_id=0, has_side_effects=True, vmem_limit_bytes=63 * 2**20
        ),
        cost_estimate=pl.CostEstimate(
            flops=5 * 2 * ROWS * LAT * D, bytes_accessed=16 * 2**20, transcendentals=0
        ),
    )(batch, next_acts, encw, decw_t, source, enc_bias, dec_bias, ef, es, df_t, ds_t)


def publish(*arrays):
    n = len(arrays)
    pieces = []
    for i, a in enumerate(arrays):
        step = a.shape[0] // 4 if a.size > 2**20 else a.shape[0]
        pieces += [(i, row, step) for row in range(0, a.shape[0], step)]

    def kernel(*refs):
        held, into, out_of = refs[2 * n : 3 * n], refs[3 * n], refs[3 * n + 1]

        def read(k):
            i, row, rows = pieces[k]
            part = pl.ds(row, rows)
            return pltpu.make_async_copy(refs[i].at[part], held[i].at[part], into.at[k])

        def write(k):
            i, row, rows = pieces[k]
            part = pl.ds(row, rows)
            return pltpu.make_async_copy(held[i].at[part], refs[n + i].at[part], out_of.at[k])

        for k in range(len(pieces)):
            read(k).start()
        for k in range(len(pieces)):
            read(k).wait()
            write(k).start()
        for k in range(len(pieces)):
            write(k).wait()

    any_space = pl.BlockSpec(memory_space=pl.ANY)
    return pl.pallas_call(
        kernel,
        out_shape=tuple(jax.ShapeDtypeStruct(a.shape, a.dtype) for a in arrays),
        in_specs=[any_space] * n,
        out_specs=[any_space] * n,
        scratch_shapes=[
            *[pltpu.VMEM(a.shape, a.dtype) for a in arrays],
            pltpu.SemaphoreType.DMA((len(pieces),)),
            pltpu.SemaphoreType.DMA((len(pieces),)),
        ],
        compiler_params=pltpu.CompilerParams(vmem_limit_bytes=63 * 2**20),
    )(*arrays)


def on_device(
    batch, next_acts, row_source, enc_weight, dec_weight, enc_bias, dec_bias,
    enc_first, enc_second, dec_first, dec_second,
):
    inv_tokens = 1.0 / (batch.shape[0] * 16)
    results = train_step(
        batch, next_acts, enc_weight, dec_weight.T, row_source.reshape(1, -1),
        enc_bias.reshape(1, LAT), dec_bias.reshape(D // 128, 128),
        enc_first, enc_second, dec_first.T, dec_second.T, inv_tokens,
    )
    next_batch, codes, err_t, nef, nes, eup, ndf, nds, dup = publish(*results)
    return next_batch, codes, err_t.T, nef, nes, eup, ndf.T, nds.T, dup.T


def solution(mesh):
    return jax.shard_map(
        on_device,
        mesh=mesh,
        in_specs=(
            P("rows", None),
            P(("rows", "lat"), None),
            P(),
            P("rows", "lat"),
            P("lat", "rows"),
            P("lat"),
            P(),
            P("rows", "lat"),
            P("rows", "lat"),
            P("lat", "rows"),
            P("lat", "rows"),
        ),
        out_specs=(
            P("rows", None),
            P("rows", "lat"),
            P("rows", "lat"),
            P("rows", "lat"),
            P("rows", "lat"),
            P("rows", "lat"),
            P("lat", "rows"),
            P("lat", "rows"),
            P("lat", "rows"),
        ),
        check_vma=False,
    )
```

```python
import functools

import jax
import jax.numpy as jnp
from jax import lax
from jax.experimental import pallas as pl
from jax.experimental.pallas import tpu as pltpu
from jax.sharding import PartitionSpec as P

beta_one = 0.9
beta_two = 0.999
correction_one = 1.0 - 0.9**3
correction_two = 1.0 - 0.999**3
eps_adam = 1e-08
sparsity_weight = 0.2

MESH = pl.DeviceIdType.MESH
BF = jnp.bfloat16
F32 = jnp.float32
D = 4608
ROWS = 384
LAT = 512
SH = 288
CH = 576
CH_A = 224
SH_A = 112
ERR_A = 320
ENC_A = 160
DEC_A = 160
NT = (((1,), (1,)), ((), ()))
TN = (((0,), (0,)), ((), ()))


def adam_update(gradient, first, second):
    first_new = beta_one * first.astype(F32) + (1.0 - beta_one) * gradient
    second_new = beta_two * second.astype(F32) + (1.0 - beta_two) * gradient * gradient
    direction = first_new / correction_one / (jnp.sqrt(second_new / correction_two) + eps_adam)
    return first_new.astype(BF), second_new.astype(BF), direction.astype(BF)


def step_kernel(
    inv_tokens,
    batch_h, next_h, encw, decw, source, enc_bias, dec_bias, ef, es, df, ds,
    next_out, codes, err_out, nef, nes, eup, ndf, nds, dup,
    batch, cent, cent_t, neg_t, encf, decf, pre, recon, err, gcodes, cgrad,
    lpart, lrec_a, lrec_y, lrec_b, lrec_p,
    sib_s, dsib_r, esib_r, kept,
    dpart, drec_a, drec_y, drec_b, drec_p, down,
    epart, erec_a, erec_y, erec_b, erec_p, eown,
    nacts, tmp, out3, in3, rows48,
    loc, enc_s, enc_r, encx_s, encx_r, dec_s, dec_r, decx_s, decx_r,
    ls_s, ls_r, err_s, err_r, dx_s, dx_r, dg_s, dg_r, ex_s, ex_r, eg_s, eg_r,
    a2a_s, a2a_r, n_s, n_r,
):
    r = lax.axis_index("rows")
    l = lax.axis_index("lat")
    c = r % 2
    q = r // 2
    sib = (q * 2 + 1 - c, l)

    def remote(src, dst, ssem, rsem, device):
        return pltpu.make_async_remote_copy(
            src_ref=src, dst_ref=dst, send_sem=ssem, recv_sem=rsem,
            device_id=device, device_id_type=MESH,
        )

    def member(g, dm, db):
        return (g // 2 + dm) % 4 * 2 + (g + db) % 2

    def rows_dev(g):
        return (g * 2 + c, l)

    def lat_dev(g):
        return (r, g)

    def shard_at(g):
        return pl.multiple_of((g * 2 + c) * SH, 32)

    def shard(g, core):
        return pl.ds(pl.multiple_of((g * 2 + core) * SH, 32), SH)

    def chunk_at(g):
        return pl.multiple_of(g * CH, 64)

    def chunk(g):
        return pl.ds(chunk_at(g), CH)

    barrier = pltpu.get_barrier_semaphore()
    for k in range(1, 16):
        pl.semaphore_signal(barrier, inc=1, device_id=((r + k) % 16, l), device_id_type=MESH)
    for dm, db in ((0, 1), (1, 0), (2, 0), (3, 0)):
        pl.semaphore_signal(barrier, inc=1, device_id=lat_dev(member(l, dm, db)), device_id_type=MESH)
    batch_cp = pltpu.make_async_copy(batch_h, batch, loc.at[0])
    enc_cp = pltpu.make_async_copy(encw, encf.at[shard(q, c)], loc.at[1])
    dec_cp = pltpu.make_async_copy(decw, decf.at[shard(q, c)], loc.at[2])
    next_cp = pltpu.make_async_copy(next_h, nacts, loc.at[3])
    next_cp.start()
    enc_cp.start()
    batch_cp.start()
    dec_cp.start()
    pl.semaphore_wait(barrier, 19)

    class Gather:
        def __init__(self, full, at, g, dev, ssem, rsem, size, size_a):
            self.full, self.at, self.g, self.dev, self.s, self.r = full, at, g, dev, ssem, rsem
            self.size, self.size_a = size, size_a

        def part(self, g, which):
            if which == "a":
                return self.full.at[pl.ds(self.at(g), self.size_a)]
            return self.full.at[pl.ds(self.at(g) + self.size_a, self.size - self.size_a)]

        def copy(self, g, which, slot, to):
            part = self.part(g, which)
            return remote(part, part, self.s.at[slot], self.r.at[slot], self.dev(to))

        def own(self, dm, db, which):
            slot = dm if which == "a" else 4 + dm
            return self.copy(self.g, which, slot, member(self.g, dm, db))

        def came(self, dm, db, which):
            slot = dm if which == "a" else 4 + dm
            return self.copy(member(self.g, 4 - dm, db), which, slot, self.g)

        def on_a(self, j):
            return self.copy(member(self.g, 0, 1), "a", 8 + j, member(self.g, j, 0))

        def on_b(self, j):
            return self.copy(member(self.g, 4 - j, 0), "b", 12 + j, member(self.g, 0, 1))

        def diag_a(self, j):
            return self.copy(member(self.g, 4 - j, 1), "a", 8 + j, self.g)

        def diag_b(self, j):
            return self.copy(member(self.g, 4 - j, 1), "b", 12 + j, self.g)

        def half(self, kind, g, second, slot, to):
            size = self.size - self.size_a if kind == "b" else self.size_a
            first = size // 32 * 16
            at = self.at(g) + (self.size_a if kind == "b" else 0)
            part = self.full.at[pl.ds(at + first, size - first) if second else pl.ds(at, first)]
            return remote(part, part, self.s.at[slot], self.r.at[slot], self.dev(to))

        def relay(self, kind, j):
            g = member(self.g, 4 - j, 1 if kind == "p" else 0)
            return self.half(kind, g, j == 3, 16 + 2 * "bap".index(kind) + j // 3, member(self.g, j, 0))

        def relayed(self, kind, j):
            g = member(self.g, 2, 1 if kind == "p" else 0)
            return self.half(kind, g, j == 3, 16 + 2 * "bap".index(kind) + j // 3, self.g)

        def start(self):
            self.own(0, 1, "a").start()
            for j in (1, 3):
                self.own(j, 0, "b").start()
            self.own(0, 1, "b").start()
            for j in (1, 3):
                self.own(j, 0, "a").start()

        def forward_a(self):
            self.came(0, 1, "a").wait_recv()
            for j in (1, 3):
                self.on_a(j).start()

        def forward_b(self, j):
            if j == 2:
                self.relayed("b", 1).wait_recv()
                self.relayed("b", 3).wait_recv()
            else:
                self.came(j, 0, "b").wait_recv()
                self.relay("b", j).start()
            self.on_b(j).start()

        def hear_ring(self, j):
            self.came(j, 0, "a").wait_recv()
            self.relay("a", j).start()

        def hear_diag(self, j):
            self.diag_a(j).wait_recv()
            self.relay("p", j).start()

        def take_pair(self):
            self.came(0, 1, "b").wait_recv()

        def take_ring(self, j):
            if j == 2:
                self.relayed("a", 1).wait_recv()
                self.relayed("a", 3).wait_recv()

        def take_diag(self, j):
            if j == 2:
                self.relayed("p", 1).wait_recv()
                self.relayed("p", 3).wait_recv()
            self.diag_b(j).wait_recv()

        def drain(self):
            for dm, db in ((0, 1), (1, 0), (3, 0)):
                self.own(dm, db, "a").wait_send()
                self.own(dm, db, "b").wait_send()
            for j in (1, 3):
                self.on_a(j).wait_send()
                for kind in "bap":
                    self.relay(kind, j).wait_send()
            for j in (1, 2, 3):
                self.on_b(j).wait_send()

    class Scatter:
        def __init__(self, part, rec_a, rec_y, rec_b, rec_p, g, dev, ssem, rsem, size, size_a):
            self.p, self.ra, self.ry, self.rb, self.rp = part, rec_a, rec_y, rec_b, rec_p
            self.g, self.dev, self.s, self.r = g, dev, ssem, rsem
            self.a, self.b = pl.ds(0, size_a), pl.ds(size_a, size - size_a)

        def copy(self, src, dst, slot, to):
            return remote(src, dst, self.s.at[slot], self.r.at[slot], self.dev(to))

        def diag_a(self, j):
            src = self.p.at[member(self.g, j, 1), self.a]
            return self.copy(src, self.ra.at[j - 1], j, member(self.g, j, 0))

        def diag_b(self, j):
            src = self.p.at[member(self.g, j, 1), self.b]
            return self.copy(src, self.ry.at[j], 4 + j, member(self.g, 0, 1))

        def ring_a(self, j):
            src = self.p.at[member(self.g, j, 0), self.a]
            return self.copy(src, self.ra.at[2 + j], 8 + j, member(self.g, j, 0))

        def ring_b(self, j):
            src = self.p.at[member(self.g, j, 0), self.b]
            return self.copy(src, self.rb.at[j - 1], 12 + j, member(self.g, j, 0))

        def pair_b(self):
            src = self.p.at[member(self.g, 0, 1), self.b]
            return self.copy(src, self.ry.at[0], 4, member(self.g, 0, 1))

        def pair_a(self):
            src = self.p.at[member(self.g, 0, 1), self.a]
            return self.copy(src, self.rp, 8, member(self.g, 0, 1))

        def emit(self, p):
            dm = (p // 2 + 4 - self.g // 2) % 4
            db = (p + self.g) % 2

            @pl.when(jnp.logical_and(db == 1, dm > 0))
            def _():
                self.diag_b(dm).start()
                self.diag_a(dm).start()

            @pl.when(jnp.logical_and(db == 0, dm > 0))
            def _():
                self.ring_a(dm).start()

            @pl.when(jnp.logical_and(db == 1, dm == 0))
            def _():
                self.pair_b().start()

        def pass_on(self):
            for j in (2, 3, 1):
                self.diag_b(j).wait_recv()
                block = self.p.at[member(self.g, j, 0), self.b]
                block[...] = (block[...].astype(F32) + self.ry[j].astype(F32)).astype(BF)
                self.ring_b(j).start()
            block = self.p.at[member(self.g, 0, 1), self.a]
            total = block[...].astype(F32)
            for j in (2, 3, 1):
                self.diag_a(j).wait_recv()
                total = total + self.ra[j - 1].astype(F32)
            block[...] = total.astype(BF)
            self.pair_a().start()

        def finish(self, own):
            for j in (1, 2, 3):
                self.ring_a(j).wait_recv()
            total = own[self.a, :]
            for j in (1, 2, 3):
                total = total + self.ra[2 + j].astype(F32)
            self.pair_b().wait_recv()
            rest = own[self.b, :] + self.ry[0].astype(F32)
            for j in (2, 3, 1):
                self.ring_b(j).wait_recv()
                rest = rest + self.rb[j - 1].astype(F32)
            own[self.b, :] = rest
            self.pair_a().wait_recv()
            own[self.a, :] = total + self.rp[...].astype(F32)

        def drain(self):
            for j in (1, 2, 3):
                self.diag_a(j).wait_send()
                self.diag_b(j).wait_send()
                self.ring_a(j).wait_send()
                self.ring_b(j).wait_send()
            self.pair_a().wait_send()
            self.pair_b().wait_send()

    class Weights(Gather):
        def __init__(self, full, ssem, rsem, xs, xr, size_a):
            super().__init__(full, shard_at, q, rows_dev, ssem, rsem, SH, size_a)
            self.xs, self.xr = xs, xr

        def cross(self, dm, db):
            part = self.full.at[shard(member(q, 4 - dm, db), c)]
            return remote(part, part, self.xs.at[dm * 2 + db], self.xr.at[dm * 2 + db], sib)

        def crossed(self, dm, db):
            part = self.full.at[shard(member(q, 4 - dm, db), 1 - c)]
            return remote(part, part, self.xs.at[dm * 2 + db], self.xr.at[dm * 2 + db], sib)

        def cross_pair(self):
            self.take_pair()
            self.cross(0, 1).start()

        def cross_ring(self, j):
            if j == 2:
                self.take_ring(2)
            else:
                self.hear_ring(j)
            self.cross(j, 0).start()

        def settle(self):
            for j in (1, 3, 2):
                self.take_diag(j)
                self.cross(j, 1).start()
            for i in range(8):
                self.crossed(i // 2, i % 2).wait_recv()

        def drain(self):
            super().drain()
            for i in range(8):
                self.cross(i // 2, i % 2).wait_send()

    enc_g = Weights(encf, enc_s, enc_r, encx_s, encx_r, ENC_A)
    dec_g = Weights(decf, dec_s, dec_r, decx_s, decx_r, DEC_A)
    enc_cp.wait()
    enc_g.start()
    enc_g.cross(0, 0).start()

    next_cp.wait()
    lane48 = lax.broadcasted_iota(jnp.int32, (48, 48), 1)
    sub48 = lax.broadcasted_iota(jnp.int32, (48, 48), 0)
    mine = (r * 8 + l) * 48

    def find(j, dest):
        cols = pl.ds(pl.multiple_of(j * 512, 512), 512)
        ids = jnp.broadcast_to(source[:, cols], (48, 512))
        sub = lax.broadcasted_iota(jnp.int32, (48, 512), 0)
        lane = lax.broadcasted_iota(jnp.int32, (48, 512), 1)
        hit = jnp.where(ids == sub + mine, lane + j * 512, 0)
        return dest + jnp.sum(hit.astype(F32), axis=1, keepdims=True)

    dest = lax.fori_loop(0, 12, find, jnp.zeros((48, 1), F32))
    dest_row = jnp.sum(jnp.where(lane48 == sub48, dest, 0.0), axis=0, keepdims=True)
    slot = jnp.sum(jnp.where(dest < dest_row, 1.0, 0.0), axis=0, keepdims=True)
    pick = jnp.where(slot == sub48.astype(F32), 1.0, 0.0).astype(BF)
    tmp[...] = jnp.dot(pick, nacts[...], preferred_element_type=F32)
    for g in range(16):
        out3[g, 0:3, :] = tmp[3 * g : 3 * g + 3, :].astype(BF)

    def to_group(k):
        return remote(
            out3.at[(r + k) % 16], in3.at[r], a2a_s.at[k - 1], a2a_r.at[k - 1], ((r + k) % 16, l)
        )

    def from_group(k):
        part = in3.at[(r + 16 - k) % 16]
        return remote(part, part, a2a_s.at[k - 1], a2a_r.at[k - 1], (r, l))

    def send_group(k, _):
        to_group(k).start()
        return 0

    lax.fori_loop(1, 16, send_group, 0)
    in3[r] = out3[r]
    enc_g.forward_a()
    for j in (1, 3):
        enc_g.forward_b(j)
    for j in (1, 3):
        enc_g.cross_ring(j)
    dec_cp.wait()
    dec_g.start()
    dec_g.cross(0, 0).start()
    enc_g.forward_b(2)
    enc_g.cross_pair()
    for j in (1, 3):
        enc_g.hear_diag(j)

    batch_cp.wait()

    def center(j, _):
        cols = pl.ds(pl.multiple_of(j * 128, 128), 128)
        x = batch[:, cols].astype(F32) - dec_bias[pl.ds(j, 1), :]
        cent[:, cols] = x.astype(BF)
        xt = x.T
        cent_t[pl.ds(pl.multiple_of(j * 128, 128), 128), :] = xt.astype(BF)
        for half in range(2):
            h = j * 2 + half

            @pl.when(h // 9 == l)
            def _():
                neg_t[pl.ds(pl.multiple_of((h % 9) * 64, 64), 64), :] = xt[64 * half : 64 * half + 64]

        return 0

    lax.fori_loop(0, 12, center, 0)
    dec_g.forward_a()
    for j in (1, 3):
        dec_g.forward_b(j)
    lax.fori_loop(12, 24, center, 0)
    enc_g.cross_ring(2)
    for j in (1, 3):
        dec_g.cross_ring(j)
    lax.fori_loop(24, 36, center, 0)
    dec_g.forward_b(2)

    def arrive(k, _):
        from_group(k).wait_recv()
        return 0

    lax.fori_loop(1, 16, arrive, 0)
    for g in range(16):
        tmp[3 * g : 3 * g + 3, :] = in3[g, 0:3, :].astype(F32)
    rows48[pl.ds(pl.multiple_of(l * 48, 16), 48), :] = tmp[...].astype(BF)

    def next_copy(g, slot, to):
        part = rows48.at[pl.ds(pl.multiple_of(g * 48, 16), 48)]
        return remote(part, part, n_s.at[slot], n_r.at[slot], lat_dev(to))

    def next_own(j):
        return next_copy(l, j, member(l, j, 0) if j else member(l, 0, 1))

    def next_came(j):
        return next_copy(member(l, 4 - j, 0) if j else member(l, 0, 1), j, l)

    def next_on(j):
        return next_copy(member(l, 0, 1), 3 + j, member(l, j, 0))

    def next_diag(j):
        return next_copy(member(l, 4 - j, 1), 3 + j, l)

    for j in range(4):
        next_own(j).start()

    enc_g.settle()
    pre[...] = jnp.broadcast_to(enc_bias[...], (ROWS, LAT))

    def encode(j, _):
        part = pl.ds(pl.multiple_of(j * 1152, 128), 1152)
        pre[...] += jnp.dot(cent[:, part], encf[part, :], preferred_element_type=F32)
        return 0

    lax.fori_loop(0, 4, encode, 0)
    codes[...] = jnp.maximum(pre[...], 0.0).astype(BF)
    for j in (1, 3):
        dec_g.hear_diag(j)
    dec_g.cross_pair()
    dec_g.cross_ring(2)

    dec_g.settle()

    lat_sum = Scatter(lpart, lrec_a, lrec_y, lrec_b, lrec_p, l, lat_dev, ls_s, ls_r, CH, CH_A)

    def order(g, i):
        return member(g, (i + 2) % 4, 1 - i // 4)

    def decode(i, _):
        p = order(l, i)
        part = lax.dot_general(decf[chunk(p), :], codes[...], NT, preferred_element_type=F32)
        lpart[p] = part.astype(BF)
        lat_sum.emit(p)

        @pl.when(i == 6)
        def _():
            recon[...] = part - neg_t[...]

        return 0

    lax.fori_loop(0, 8, decode, 0)
    lat_sum.pass_on()
    lat_sum.finish(recon)
    err[chunk(l), :] = recon[...].astype(BF)
    err_out[...] = err[chunk(l), :]

    err_g = Gather(err, chunk_at, l, lat_dev, err_s, err_r, CH, ERR_A)
    err_g.start()
    gcodes[...] = jnp.full((ROWS, LAT), sparsity_weight, F32)

    def grad_begin(lhs, rhs, p, hold, scale, sib_r, xs, xr):
        other = jnp.dot(lhs[shard(p, 1 - c), :], rhs[...], preferred_element_type=F32)
        sib_s[p] = (other * scale).astype(BF)
        remote(sib_s.at[p], sib_r.at[p], xs.at[p], xr.at[p], sib).start()
        mine = jnp.dot(lhs[shard(p, c), :], rhs[...], preferred_element_type=F32)
        kept[hold] = mine * scale

    def grad_end(p, hold, sib_r, own, scatter, xs, xr):
        remote(sib_s.at[p], sib_r.at[p], xs.at[p], xr.at[p], sib).wait_recv()
        total = kept[hold] + sib_r[p].astype(F32)
        scatter.p[p] = total.astype(BF)
        scatter.emit(p)

        @pl.when(p == q)
        def _():
            own[...] = total

    dec_sum = Scatter(dpart, drec_a, drec_y, drec_b, drec_p, q, rows_dev, dg_s, dg_r, SH, SH_A)
    enc_sum = Scatter(epart, erec_a, erec_y, erec_b, erec_p, q, rows_dev, eg_s, eg_r, SH, SH_A)

    def error_begin(dm, db, hold):
        p = member(l, dm, db)
        gcodes[...] += lax.dot_general(
            err[chunk(p), :], decf[chunk(p), :], TN, preferred_element_type=F32
        )
        grad_begin(err, codes, p, hold, inv_tokens, dsib_r, dx_s, dx_r)

    def error_end(dm, db, hold):
        grad_end(member(l, dm, db), hold, dsib_r, down, dec_sum, dx_s, dx_r)

    error_begin(0, 0, 0)
    err_g.forward_a()
    err_g.forward_b(1)
    error_end(0, 0, 0)
    err_g.forward_b(3)
    err_g.hear_ring(1)
    err_g.hear_ring(3)
    err_g.take_pair()
    error_begin(0, 1, 1)
    err_g.forward_b(2)
    before = (0, 1)
    for i, (j, db) in enumerate(((1, 0), (3, 0), (2, 0), (1, 1), (3, 1), (2, 1))):
        if db:
            err_g.take_diag(j)
        else:
            err_g.take_ring(j)
        error_begin(4 - j, db, i % 2)
        error_end(*before, (i + 1) % 2)
        before = (4 - j, db)
        if i in (0, 1):
            err_g.hear_diag((1, 3)[i])
    error_end(*before, 1)
    next_came(0).wait_recv()
    for j in (1, 3, 2):
        next_on(j).start()
    cgrad[...] = jnp.where(pre[...] > 0, gcodes[...] * inv_tokens, 0.0).astype(BF)

    def drain_cross(p, _):
        remote(sib_s.at[p], dsib_r.at[p], dx_s.at[p], dx_r.at[p], sib).wait_send()
        return 0

    lax.fori_loop(0, 8, drain_cross, 0)

    def enc_step(i, _):
        grad_begin(cent_t, cgrad, order(q, i), i % 2, 1.0, esib_r, ex_s, ex_r)

        @pl.when(i > 0)
        def _():
            grad_end(order(q, i - 1), (i + 1) % 2, esib_r, eown, enc_sum, ex_s, ex_r)

        return 0

    lax.fori_loop(0, 8, enc_step, 0)
    grad_end(order(q, 7), 1, esib_r, eown, enc_sum, ex_s, ex_r)
    dec_sum.pass_on()
    enc_sum.pass_on()

    place_l = lax.broadcasted_iota(jnp.int32, (ROWS, ROWS), 1)
    place_s = lax.broadcasted_iota(jnp.int32, (ROWS, ROWS), 0)
    wanted = source[:, pl.ds(pl.multiple_of(r * ROWS, 128), ROWS)]
    owner = jnp.right_shift(wanted * 43691, 21).astype(F32)
    owner_col = jnp.sum(jnp.where(place_l == place_s, owner, 0.0), axis=1, keepdims=True)
    earlier = jnp.logical_and(owner == owner_col, place_l < place_s)
    rank = jnp.sum(jnp.where(earlier, 1.0, 0.0), axis=1, keepdims=True)
    owner_i = owner_col.astype(jnp.int32)
    position = jnp.bitwise_and(owner_i, 7) * 48 + jnp.right_shift(owner_i, 3) * 3 + rank.astype(jnp.int32)
    put = jnp.where(position == place_l, 1.0, 0.0).astype(BF)
    for j in (1, 3, 2):
        next_came(j).wait_recv()
    for j in (1, 3, 2):
        next_diag(j).wait_recv()
    cgrad[:, 0:ROWS] = put

    def permute(j, _):
        cols = pl.ds(pl.multiple_of(j * 512, 512), 512)
        batch[:, cols] = jnp.dot(
            cgrad[:, 0:ROWS], rows48[:, cols], preferred_element_type=F32
        ).astype(BF)
        return 0

    lax.fori_loop(0, 9, permute, 0)
    out_cp = pltpu.make_async_copy(batch, next_out, loc.at[4])
    out_cp.start()

    def update(scatter, own, first, second, outs):
        scatter.finish(own)
        for out, value in zip(outs, adam_update(own[...], first[...], second[...])):
            out[...] = value

    update(dec_sum, down, df, ds, (ndf, nds, dup))
    update(enc_sum, eown, ef, es, (nef, nes, eup))

    enc_g.drain()
    dec_g.drain()
    err_g.drain()
    lat_sum.drain()
    dec_sum.drain()
    enc_sum.drain()

    def drain_group(k, _):
        to_group(k).wait_send()
        return 0

    lax.fori_loop(1, 16, drain_group, 0)
    for j in range(4):
        next_own(j).wait_send()
    for j in (1, 2, 3):
        next_on(j).wait_send()

    def drain_cross2(p, _):
        remote(sib_s.at[p], esib_r.at[p], ex_s.at[p], ex_r.at[p], sib).wait_send()
        return 0

    lax.fori_loop(0, 8, drain_cross2, 0)
    out_cp.wait()


def train_step(
    batch, next_acts, encw, decw_t, source, enc_bias, dec_bias, ef, es, df_t, ds_t, inv_tokens
):
    any_space = pl.BlockSpec(memory_space=pl.ANY)
    vmem = pl.BlockSpec(memory_space=pltpu.VMEM)
    dma = pltpu.SemaphoreType.DMA

    def received(size, size_a, width):
        return [
            pltpu.VMEM((8, size, width), BF),
            pltpu.VMEM((6, size_a, width), BF),
            pltpu.VMEM((4, size - size_a, width), BF),
            pltpu.VMEM((3, size - size_a, width), BF),
            pltpu.VMEM((size_a, width), BF),
        ]

    shard = jax.ShapeDtypeStruct((SH, LAT), BF)
    return pl.pallas_call(
        functools.partial(step_kernel, inv_tokens),
        out_shape=(
            jax.ShapeDtypeStruct((ROWS, D), BF),
            jax.ShapeDtypeStruct((ROWS, LAT), BF),
            jax.ShapeDtypeStruct((CH, ROWS), BF),
            *([shard] * 6),
        ),
        in_specs=[any_space] * 4 + [vmem] * 7,
        out_specs=[any_space] + [vmem] * 8,
        scratch_shapes=[
            pltpu.VMEM((ROWS, D), BF),
            pltpu.VMEM((ROWS, D), BF),
            pltpu.VMEM((D, ROWS), BF),
            pltpu.VMEM((CH, ROWS), F32),
            pltpu.VMEM((D, LAT), BF),
            pltpu.VMEM((D, LAT), BF),
            pltpu.VMEM((ROWS, LAT), F32),
            pltpu.VMEM((CH, ROWS), F32),
            pltpu.VMEM((D, ROWS), BF),
            pltpu.VMEM((ROWS, LAT), F32),
            pltpu.VMEM((ROWS, LAT), BF),
            *received(CH, CH_A, ROWS),
            *([pltpu.VMEM((8, SH, LAT), BF)] * 3),
            pltpu.VMEM((2, SH, LAT), F32),
            *received(SH, SH_A, LAT),
            pltpu.VMEM((SH, LAT), F32),
            *received(SH, SH_A, LAT),
            pltpu.VMEM((SH, LAT), F32),
            pltpu.VMEM((48, D), BF),
            pltpu.VMEM((48, D), F32),
            pltpu.VMEM((16, 4, D), BF),
            pltpu.VMEM((16, 4, D), BF),
            pltpu.VMEM((ROWS, D), BF),
            dma((5,)),
            dma((22,)), dma((22,)), dma((8,)), dma((8,)),
            dma((22,)), dma((22,)), dma((8,)), dma((8,)),
            dma((16,)), dma((16,)), dma((22,)), dma((22,)),
            dma((8,)), dma((8,)), dma((16,)), dma((16,)),
            dma((8,)), dma((8,)), dma((16,)), dma((16,)),
            dma((15,)), dma((15,)), dma((7,)), dma((7,)),
        ],
        compiler_params=pltpu.CompilerParams(
            collective_id=0, has_side_effects=True, vmem_limit_bytes=63 * 2**20
        ),
        cost_estimate=pl.CostEstimate(
            flops=5 * 2 * ROWS * LAT * D, bytes_accessed=16 * 2**20, transcendentals=0
        ),
    )(batch, next_acts, encw, decw_t, source, enc_bias, dec_bias, ef, es, df_t, ds_t)


def publish(*arrays):
    n = len(arrays)
    pieces = []
    for i, a in enumerate(arrays):
        step = a.shape[0] // 4 if a.size > 2**20 else a.shape[0]
        pieces += [(i, row, step) for row in range(0, a.shape[0], step)]

    def kernel(*refs):
        held, into, out_of = refs[2 * n : 3 * n], refs[3 * n], refs[3 * n + 1]

        def read(k):
            i, row, rows = pieces[k]
            part = pl.ds(row, rows)
            return pltpu.make_async_copy(refs[i].at[part], held[i].at[part], into.at[k])

        def write(k):
            i, row, rows = pieces[k]
            part = pl.ds(row, rows)
            return pltpu.make_async_copy(held[i].at[part], refs[n + i].at[part], out_of.at[k])

        for k in range(len(pieces)):
            read(k).start()
        for k in range(len(pieces)):
            read(k).wait()
            write(k).start()
        for k in range(len(pieces)):
            write(k).wait()

    any_space = pl.BlockSpec(memory_space=pl.ANY)
    return pl.pallas_call(
        kernel,
        out_shape=tuple(jax.ShapeDtypeStruct(a.shape, a.dtype) for a in arrays),
        in_specs=[any_space] * n,
        out_specs=[any_space] * n,
        scratch_shapes=[
            *[pltpu.VMEM(a.shape, a.dtype) for a in arrays],
            pltpu.SemaphoreType.DMA((len(pieces),)),
            pltpu.SemaphoreType.DMA((len(pieces),)),
        ],
        compiler_params=pltpu.CompilerParams(vmem_limit_bytes=63 * 2**20),
    )(*arrays)


def on_device(
    batch, next_acts, row_source, enc_weight, dec_weight, enc_bias, dec_bias,
    enc_first, enc_second, dec_first, dec_second,
):
    inv_tokens = 1.0 / (batch.shape[0] * 16)
    results = train_step(
        batch, next_acts, enc_weight, dec_weight.T, row_source.reshape(1, -1),
        enc_bias.reshape(1, LAT), dec_bias.reshape(D // 128, 128),
        enc_first, enc_second, dec_first.T, dec_second.T, inv_tokens,
    )
    next_batch, codes, err_t, nef, nes, eup, ndf, nds, dup = publish(*results)
    return next_batch, codes, err_t.T, nef, nes, eup, ndf.T, nds.T, dup.T


def solution(mesh):
    return jax.shard_map(
        on_device,
        mesh=mesh,
        in_specs=(
            P("rows", None),
            P(("rows", "lat"), None),
            P(),
            P("rows", "lat"),
            P("lat", "rows"),
            P("lat"),
            P(),
            P("rows", "lat"),
            P("rows", "lat"),
            P("lat", "rows"),
            P("lat", "rows"),
        ),
        out_specs=(
            P("rows", None),
            P("rows", "lat"),
            P("rows", "lat"),
            P("rows", "lat"),
            P("rows", "lat"),
            P("rows", "lat"),
            P("lat", "rows"),
            P("lat", "rows"),
            P("lat", "rows"),
        ),
        check_vma=False,
    )
```

```python
import functools

import jax
import jax.numpy as jnp
from jax import lax
from jax.experimental import pallas as pl
from jax.experimental.pallas import tpu as pltpu
from jax.sharding import PartitionSpec as P

beta_one = 0.9
beta_two = 0.999
correction_one = 1.0 - 0.9**3
correction_two = 1.0 - 0.999**3
eps_adam = 1e-08
sparsity_weight = 0.2

MESH = pl.DeviceIdType.MESH
BF = jnp.bfloat16
F32 = jnp.float32
D = 4608
ROWS = 384
LAT = 512
SH = 288
CH = 576
CH_A = 320
SH_A = 160
CH_SUM_A = 256
SH_SUM_A = 128
NT = (((1,), (1,)), ((), ()))
TN = (((0,), (0,)), ((), ()))


def adam_update(gradient, first, second):
    first_new = beta_one * first.astype(F32) + (1.0 - beta_one) * gradient
    second_new = beta_two * second.astype(F32) + (1.0 - beta_two) * gradient * gradient
    direction = first_new / correction_one / (jnp.sqrt(second_new / correction_two) + eps_adam)
    return first_new.astype(BF), second_new.astype(BF), direction.astype(BF)


def step_kernel(
    inv_tokens,
    batch_h, next_h, encw, decw, ef_h, es_h, df_h, ds_h, source, enc_bias, dec_bias,
    next_out, codes, err_out, nef, nes, eup, ndf, nds, dup,
    batch, cent, cent_t, neg_t, encf, decf, pre, recon, err, gcodes, cgrad,
    lpart, lrec_a, lrec_y, lrec_b, lrec_p, lrel_a, lrel_b,
    sib_s, dsib_r, esib_r, kept,
    dpart, drec_a, drec_y, drec_b, drec_p, drel_a, drel_b, down,
    epart, erec_a, erec_y, erec_b, erec_p, erel_a, erel_b, eown,
    nacts, tmp, out3, in3, rows48, put, ef, es, df, ds,
    loc, enc_s, enc_r, encx_s, encx_r, dec_s, dec_r, decx_s, decx_r,
    ls_s, ls_r, err_s, err_r, dx_s, dx_r, dg_s, dg_r, ex_s, ex_r, eg_s, eg_r,
    a2a_s, a2a_r, n_s, n_r,
):
    r = lax.axis_index("rows")
    l = lax.axis_index("lat")
    c = r % 2
    q = r // 2
    sib = (q * 2 + 1 - c, l)

    def remote(src, dst, ssem, rsem, device):
        return pltpu.make_async_remote_copy(
            src_ref=src, dst_ref=dst, send_sem=ssem, recv_sem=rsem,
            device_id=device, device_id_type=MESH,
        )

    def member(g, dm, db):
        return (g // 2 + dm) % 4 * 2 + (g + db) % 2

    def rows_dev(g):
        return (g * 2 + c, l)

    def lat_dev(g):
        return (r, g)

    def shard_at(g):
        return pl.multiple_of((g * 2 + c) * SH, 32)

    def shard(g, core):
        return pl.ds(pl.multiple_of((g * 2 + core) * SH, 32), SH)

    def chunk_at(g):
        return pl.multiple_of(g * CH, 64)

    def chunk(g):
        return pl.ds(chunk_at(g), CH)

    barrier = pltpu.get_barrier_semaphore()
    for k in range(1, 16):
        pl.semaphore_signal(barrier, inc=1, device_id=((r + k) % 16, l), device_id_type=MESH)
    for dm, db in ((0, 1), (1, 0), (2, 0), (3, 0)):
        pl.semaphore_signal(barrier, inc=1, device_id=lat_dev(member(l, dm, db)), device_id_type=MESH)
    batch_cp = pltpu.make_async_copy(batch_h, batch, loc.at[0])
    enc_cp = pltpu.make_async_copy(encw, encf.at[shard(q, c)], loc.at[1])
    dec_cp = pltpu.make_async_copy(decw, decf.at[shard(q, c)], loc.at[2])
    next_cp = pltpu.make_async_copy(next_h, nacts, loc.at[3])
    next_cp.start()
    enc_cp.start()
    batch_cp.start()
    dec_cp.start()
    moment_cps = [
        pltpu.make_async_copy(src, dst, loc.at[5 + i])
        for i, (src, dst) in enumerate(((ef_h, ef), (es_h, es), (df_h, df), (ds_h, ds)))
    ]
    pl.semaphore_wait(barrier, 19)

    class Gather:
        def __init__(self, full, at, g, dev, ssem, rsem, size, size_a):
            self.full, self.at, self.g, self.dev, self.s, self.r = full, at, g, dev, ssem, rsem
            self.size, self.size_a = size, size_a

        def part(self, g, which):
            if which == "a":
                return self.full.at[pl.ds(self.at(g), self.size_a)]
            return self.full.at[pl.ds(self.at(g) + self.size_a, self.size - self.size_a)]

        def copy(self, g, which, slot, to):
            part = self.part(g, which)
            return remote(part, part, self.s.at[slot], self.r.at[slot], self.dev(to))

        def own(self, dm, db, which):
            slot = dm if which == "a" else 4 + dm
            return self.copy(self.g, which, slot, member(self.g, dm, db))

        def came(self, dm, db, which):
            slot = dm if which == "a" else 4 + dm
            return self.copy(member(self.g, 4 - dm, db), which, slot, self.g)

        def on_a(self, j):
            return self.copy(member(self.g, 0, 1), "a", 8 + j, member(self.g, j, 0))

        def on_b(self, j):
            return self.copy(member(self.g, 4 - j, 0), "b", 12 + j, member(self.g, 0, 1))

        def diag_a(self, j):
            return self.copy(member(self.g, 4 - j, 1), "a", 8 + j, self.g)

        def diag_b(self, j):
            return self.copy(member(self.g, 4 - j, 1), "b", 12 + j, self.g)

        def half(self, kind, g, second, slot, to):
            size = self.size - self.size_a if kind == "b" else self.size_a
            first = size // 32 * 16
            at = self.at(g) + (self.size_a if kind == "b" else 0)
            part = self.full.at[pl.ds(at + first, size - first) if second else pl.ds(at, first)]
            return remote(part, part, self.s.at[slot], self.r.at[slot], self.dev(to))

        def relay(self, kind, j):
            g = member(self.g, 4 - j, 1 if kind == "p" else 0)
            return self.half(kind, g, j == 3, 16 + 2 * "bap".index(kind) + j // 3, member(self.g, j, 0))

        def relayed(self, kind, j):
            g = member(self.g, 2, 1 if kind == "p" else 0)
            return self.half(kind, g, j == 3, 16 + 2 * "bap".index(kind) + j // 3, self.g)

        def start(self):
            self.own(0, 1, "a").start()
            for j in (1, 3):
                self.own(j, 0, "b").start()
            self.own(0, 1, "b").start()
            for j in (1, 3):
                self.own(j, 0, "a").start()

        def forward_a(self):
            self.came(0, 1, "a").wait_recv()
            for j in (1, 3):
                self.on_a(j).start()

        def forward_b(self, j):
            if j == 2:
                self.relayed("b", 1).wait_recv()
                self.relayed("b", 3).wait_recv()
            else:
                self.came(j, 0, "b").wait_recv()
                self.relay("b", j).start()
            self.on_b(j).start()

        def hear_ring(self, j):
            self.came(j, 0, "a").wait_recv()
            self.relay("a", j).start()

        def hear_diag(self, j):
            self.diag_a(j).wait_recv()
            self.relay("p", j).start()

        def take_pair(self):
            self.came(0, 1, "b").wait_recv()

        def take_ring(self, j):
            if j == 2:
                self.relayed("a", 1).wait_recv()
                self.relayed("a", 3).wait_recv()

        def take_diag(self, j):
            if j == 2:
                self.relayed("p", 1).wait_recv()
                self.relayed("p", 3).wait_recv()
            self.diag_b(j).wait_recv()

        def drain(self):
            for dm, db in ((0, 1), (1, 0), (3, 0)):
                self.own(dm, db, "a").wait_send()
                self.own(dm, db, "b").wait_send()
            for j in (1, 3):
                self.on_a(j).wait_send()
                for kind in "bap":
                    self.relay(kind, j).wait_send()
            for j in (1, 2, 3):
                self.on_b(j).wait_send()

    class Scatter:
        def __init__(
            self, part, rec_a, rec_y, rec_b, rec_p, rel_a, rel_b, g, dev, ssem, rsem, size, size_a
        ):
            self.p, self.ra, self.ry, self.rb, self.rp = part, rec_a, rec_y, rec_b, rec_p
            self.la, self.lb = rel_a, rel_b
            self.g, self.dev, self.s, self.r = g, dev, ssem, rsem
            self.size, self.size_a = size, size_a
            self.a, self.b = pl.ds(0, size_a), pl.ds(size_a, size - size_a)

        def copy(self, src, dst, slot, to):
            return remote(src, dst, self.s.at[slot], self.r.at[slot], self.dev(to))

        def diag_a(self, j):
            src = self.p.at[member(self.g, j, 1), self.a]
            return self.copy(src, self.ra.at[j // 3], j, member(self.g, j, 0))

        def diag_b(self, j):
            src = self.p.at[member(self.g, j, 1), self.b]
            return self.copy(src, self.ry.at[j], 4 + j, member(self.g, 0, 1))

        def ring_a(self, j):
            src = self.p.at[member(self.g, j, 0), self.a]
            return self.copy(src, self.ra.at[2 + j // 3], 8 + j, member(self.g, j, 0))

        def ring_b(self, j):
            src = self.p.at[member(self.g, j, 0), self.b]
            return self.copy(src, self.rb.at[j // 3], 12 + j, member(self.g, j, 0))

        def pair_b(self):
            src = self.p.at[member(self.g, 0, 1), self.b]
            return self.copy(src, self.ry.at[0], 4, member(self.g, 0, 1))

        def pair_a(self):
            src = self.p.at[member(self.g, 0, 1), self.a]
            return self.copy(src, self.rp, 8, member(self.g, 0, 1))

        def half(self, kind, j):
            size_b = self.size - self.size_a
            if kind == "b":
                return pl.ds(self.size_a + j // 3 * (size_b // 2), size_b // 2)
            return pl.ds(j // 3 * (self.size_a // 2), self.size_a // 2)

        def held(self, kind, j):
            return self.lb.at[j // 3] if kind == "b" else self.la.at["dr".index(kind) * 2 + j // 3]

        def relay(self, kind, j):
            src = self.p.at[member(self.g, 2, 1 if kind == "d" else 0), self.half(kind, j)]
            slot = 16 + "drb".index(kind) * 2 + j // 3
            return self.copy(src, self.held(kind, j), slot, member(self.g, j, 0))

        def relays(self, kind):
            self.relay(kind, 1).start()
            self.relay(kind, 3).start()

        def add_relayed(self, kind, j):
            self.relay(kind, j).wait_recv()
            block = self.p.at[member(self.g, j, 1 if kind == "d" else 0), self.half(kind, j)]
            block[...] = (block[...].astype(F32) + self.held(kind, j)[...].astype(F32)).astype(BF)

        def emit(self, p):
            dm = (p // 2 + 4 - self.g // 2) % 4
            db = (p + self.g) % 2

            @pl.when(jnp.logical_and(db == 1, dm > 0))
            def _():
                self.diag_b(dm).start()

            @pl.when(jnp.logical_and(db == 1, dm == 2))
            def _():
                self.relays("d")

            @pl.when(jnp.logical_and(db == 0, dm == 2))
            def _():
                self.relays("r")

            @pl.when(jnp.logical_and(db == 1, dm == 0))
            def _():
                self.pair_b().start()

        def pass_diag(self):
            for j in (1, 3):
                self.add_relayed("d", j)
                self.diag_a(j).start()

        def pass_ring(self):
            for j in (1, 3):
                self.add_relayed("r", j)
                self.ring_a(j).start()

        def pass_on(self):
            for j in (2, 3, 1):
                self.diag_b(j).wait_recv()
                block = self.p.at[member(self.g, j, 0), self.b]
                block[...] = (block[...].astype(F32) + self.ry[j].astype(F32)).astype(BF)
                if j == 2:
                    self.relays("b")
            block = self.p.at[member(self.g, 0, 1), self.a]
            total = block[...].astype(F32)
            for j in (1, 3):
                self.diag_a(j).wait_recv()
                total = total + self.ra[j // 3].astype(F32)
            block[...] = total.astype(BF)
            self.pair_a().start()
            for j in (1, 3):
                self.add_relayed("b", j)
                self.ring_b(j).start()

        def finish(self, own):
            total = own[self.a, :]
            for j in (1, 3):
                self.ring_a(j).wait_recv()
                total = total + self.ra[2 + j // 3].astype(F32)
            self.pair_b().wait_recv()
            rest = own[self.b, :] + self.ry[0].astype(F32)
            self.pair_a().wait_recv()
            own[self.a, :] = total + self.rp[...].astype(F32)
            for j in (1, 3):
                self.ring_b(j).wait_recv()
                rest = rest + self.rb[j // 3].astype(F32)
            own[self.b, :] = rest

        def drain(self):
            for j in (1, 2, 3):
                self.diag_b(j).wait_send()
            for j in (1, 3):
                self.diag_a(j).wait_send()
                self.ring_a(j).wait_send()
                self.ring_b(j).wait_send()
                for kind in "drb":
                    self.relay(kind, j).wait_send()
            self.pair_a().wait_send()
            self.pair_b().wait_send()

    class Weights(Gather):
        def __init__(self, full, ssem, rsem, xs, xr, size_a):
            super().__init__(full, shard_at, q, rows_dev, ssem, rsem, SH, size_a)
            self.xs, self.xr = xs, xr

        def cross(self, dm, db):
            part = self.full.at[shard(member(q, 4 - dm, db), c)]
            return remote(part, part, self.xs.at[dm * 2 + db], self.xr.at[dm * 2 + db], sib)

        def crossed(self, dm, db):
            part = self.full.at[shard(member(q, 4 - dm, db), 1 - c)]
            return remote(part, part, self.xs.at[dm * 2 + db], self.xr.at[dm * 2 + db], sib)

        def cross_pair(self):
            self.take_pair()
            self.cross(0, 1).start()

        def cross_ring(self, j):
            if j == 2:
                self.take_ring(2)
            else:
                self.hear_ring(j)
            self.cross(j, 0).start()

        def settle(self):
            for j in (1, 3, 2):
                self.take_diag(j)
                self.cross(j, 1).start()
            for i in range(8):
                self.crossed(i // 2, i % 2).wait_recv()

        def drain(self):
            super().drain()
            for i in range(8):
                self.cross(i // 2, i % 2).wait_send()

    enc_g = Weights(encf, enc_s, enc_r, encx_s, encx_r, SH_A)
    dec_g = Weights(decf, dec_s, dec_r, decx_s, decx_r, SH_A)
    enc_cp.wait()
    enc_g.start()
    enc_g.cross(0, 0).start()

    next_cp.wait()
    lane48 = lax.broadcasted_iota(jnp.int32, (48, 48), 1)
    sub48 = lax.broadcasted_iota(jnp.int32, (48, 48), 0)
    mine = (r * 8 + l) * 48

    def find(j, dest):
        cols = pl.ds(pl.multiple_of(j * 512, 512), 512)
        ids = jnp.broadcast_to(source[:, cols], (48, 512))
        sub = lax.broadcasted_iota(jnp.int32, (48, 512), 0)
        lane = lax.broadcasted_iota(jnp.int32, (48, 512), 1)
        hit = jnp.where(ids == sub + mine, lane + j * 512, 0)
        return dest + jnp.sum(hit.astype(F32), axis=1, keepdims=True)

    dest = lax.fori_loop(0, 12, find, jnp.zeros((48, 1), F32))
    dest_row = jnp.sum(jnp.where(lane48 == sub48, dest, 0.0), axis=0, keepdims=True)
    slot = jnp.sum(jnp.where(dest < dest_row, 1.0, 0.0), axis=0, keepdims=True)
    pick = jnp.where(slot == sub48.astype(F32), 1.0, 0.0).astype(BF)
    tmp[...] = jnp.dot(pick, nacts[...], preferred_element_type=F32)
    for g in range(16):
        out3[g, 0:3, :] = tmp[3 * g : 3 * g + 3, :].astype(BF)

    def to_group(k):
        return remote(
            out3.at[(r + k) % 16], in3.at[r], a2a_s.at[k - 1], a2a_r.at[k - 1], ((r + k) % 16, l)
        )

    def from_group(k):
        part = in3.at[(r + 16 - k) % 16]
        return remote(part, part, a2a_s.at[k - 1], a2a_r.at[k - 1], (r, l))

    def send_group(k, _):
        to_group(k).start()
        return 0

    lax.fori_loop(1, 16, send_group, 0)
    in3[r] = out3[r]
    enc_g.forward_a()
    for j in (1, 3):
        enc_g.forward_b(j)
    for j in (1, 3):
        enc_g.cross_ring(j)
    dec_cp.wait()
    dec_g.start()
    dec_g.cross(0, 0).start()
    enc_g.forward_b(2)
    enc_g.cross_pair()
    for j in (1, 3):
        enc_g.hear_diag(j)

    for cp in moment_cps:
        cp.start()
    batch_cp.wait()

    def center(j, _):
        cols = pl.ds(pl.multiple_of(j * 128, 128), 128)
        x = batch[:, cols].astype(F32) - dec_bias[pl.ds(j, 1), :]
        cent[:, cols] = x.astype(BF)
        xt = x.T
        cent_t[pl.ds(pl.multiple_of(j * 128, 128), 128), :] = xt.astype(BF)
        for half in range(2):
            h = j * 2 + half

            @pl.when(h // 9 == l)
            def _():
                neg_t[pl.ds(pl.multiple_of((h % 9) * 64, 64), 64), :] = xt[64 * half : 64 * half + 64]

        return 0

    lax.fori_loop(0, 12, center, 0)
    dec_g.forward_a()
    for j in (1, 3):
        dec_g.forward_b(j)
    lax.fori_loop(12, 24, center, 0)
    enc_g.cross_ring(2)
    for j in (1, 3):
        dec_g.cross_ring(j)
    lax.fori_loop(24, 36, center, 0)
    dec_g.forward_b(2)

    def arrive(k, _):
        from_group(k).wait_recv()
        return 0

    lax.fori_loop(1, 16, arrive, 0)
    for g in range(16):
        tmp[3 * g : 3 * g + 3, :] = in3[g, 0:3, :].astype(F32)
    rows48[pl.ds(pl.multiple_of(l * 48, 16), 48), :] = tmp[...].astype(BF)

    def next_copy(g, slot, to):
        part = rows48.at[pl.ds(pl.multiple_of(g * 48, 16), 48)]
        return remote(part, part, n_s.at[slot], n_r.at[slot], lat_dev(to))

    def next_own(j):
        return next_copy(l, j, member(l, j, 0) if j else member(l, 0, 1))

    def next_came(j):
        return next_copy(member(l, 4 - j, 0) if j else member(l, 0, 1), j, l)

    def next_on(j):
        return next_copy(member(l, 0, 1), 3 + j, member(l, j, 0))

    def next_diag(j):
        return next_copy(member(l, 4 - j, 1), 3 + j, l)

    for j in range(4):
        next_own(j).start()

    place_l = lax.broadcasted_iota(jnp.int32, (ROWS, ROWS), 1)
    place_s = lax.broadcasted_iota(jnp.int32, (ROWS, ROWS), 0)
    wanted = source[:, pl.ds(pl.multiple_of(r * ROWS, 128), ROWS)]
    owner = jnp.right_shift(wanted * 43691, 21).astype(F32)
    owner_col = jnp.sum(jnp.where(place_l == place_s, owner, 0.0), axis=1, keepdims=True)
    earlier = jnp.logical_and(owner == owner_col, place_l < place_s)
    rank = jnp.sum(jnp.where(earlier, 1.0, 0.0), axis=1, keepdims=True)
    owner_i = owner_col.astype(jnp.int32)
    position = jnp.bitwise_and(owner_i, 7) * 48 + jnp.right_shift(owner_i, 3) * 3 + rank.astype(jnp.int32)
    put[...] = jnp.where(position == place_l, 1.0, 0.0).astype(BF)

    enc_g.settle()
    pre[...] = jnp.broadcast_to(enc_bias[...], (ROWS, LAT))

    def encode(j, _):
        part = pl.ds(pl.multiple_of(j * 1152, 128), 1152)
        pre[...] += jnp.dot(cent[:, part], encf[part, :], preferred_element_type=F32)
        return 0

    lax.fori_loop(0, 4, encode, 0)
    codes[...] = jnp.maximum(pre[...], 0.0).astype(BF)
    for j in (1, 3):
        dec_g.hear_diag(j)
    dec_g.cross_pair()
    dec_g.cross_ring(2)

    dec_g.settle()

    lat_sum = Scatter(lpart, lrec_a, lrec_y, lrec_b, lrec_p, lrel_a, lrel_b, l, lat_dev, ls_s, ls_r, CH, CH_SUM_A)

    def order(g, i):
        return member(g, (i + 2) % 4, 1 - i // 4)

    def decode(i, _):
        p = order(l, i)
        part = lax.dot_general(decf[chunk(p), :], codes[...], NT, preferred_element_type=F32)
        lpart[p] = part.astype(BF)
        lat_sum.emit(p)

        @pl.when(i == 6)
        def _():
            recon[...] = part - neg_t[...]

        return 0

    lax.fori_loop(0, 5, decode, 0)
    lat_sum.pass_diag()
    lax.fori_loop(5, 8, decode, 0)
    lat_sum.pass_ring()
    lat_sum.pass_on()
    lat_sum.finish(recon)
    err[chunk(l), :] = recon[...].astype(BF)
    err_out[...] = err[chunk(l), :]

    err_g = Gather(err, chunk_at, l, lat_dev, err_s, err_r, CH, CH_A)
    err_g.start()
    gcodes[...] = jnp.full((ROWS, LAT), sparsity_weight, F32)

    def grad_begin(lhs, rhs, p, hold, scale, sib_r, xs, xr):
        other = jnp.dot(lhs[shard(p, 1 - c), :], rhs[...], preferred_element_type=F32)
        sib_s[p] = (other * scale).astype(BF)
        remote(sib_s.at[p], sib_r.at[p], xs.at[p], xr.at[p], sib).start()
        mine = jnp.dot(lhs[shard(p, c), :], rhs[...], preferred_element_type=F32)
        kept[hold] = mine * scale

    def grad_end(p, hold, sib_r, own, scatter, xs, xr):
        remote(sib_s.at[p], sib_r.at[p], xs.at[p], xr.at[p], sib).wait_recv()
        total = kept[hold] + sib_r[p].astype(F32)
        scatter.p[p] = total.astype(BF)
        scatter.emit(p)

        @pl.when(p == q)
        def _():
            own[...] = total

    dec_sum = Scatter(dpart, drec_a, drec_y, drec_b, drec_p, drel_a, drel_b, q, rows_dev, dg_s, dg_r, SH, SH_SUM_A)
    enc_sum = Scatter(epart, erec_a, erec_y, erec_b, erec_p, erel_a, erel_b, q, rows_dev, eg_s, eg_r, SH, SH_SUM_A)

    def error_begin(dm, db, hold):
        p = member(l, dm, db)
        gcodes[...] += lax.dot_general(
            err[chunk(p), :], decf[chunk(p), :], TN, preferred_element_type=F32
        )
        grad_begin(err, codes, p, hold, inv_tokens, dsib_r, dx_s, dx_r)

    def error_end(dm, db, hold):
        grad_end(member(l, dm, db), hold, dsib_r, down, dec_sum, dx_s, dx_r)

    error_begin(0, 0, 0)
    err_g.forward_a()
    err_g.forward_b(1)
    error_end(0, 0, 0)
    err_g.forward_b(3)
    err_g.hear_ring(1)
    err_g.hear_ring(3)
    err_g.take_pair()
    error_begin(0, 1, 1)
    err_g.forward_b(2)
    before = (0, 1)
    for i, (j, db) in enumerate(((1, 0), (3, 0), (2, 0), (1, 1), (3, 1), (2, 1))):
        if db:
            err_g.take_diag(j)
        else:
            err_g.take_ring(j)
        error_begin(4 - j, db, i % 2)
        error_end(*before, (i + 1) % 2)
        before = (4 - j, db)
        if i in (0, 1):
            err_g.hear_diag((1, 3)[i])
    error_end(*before, 1)
    next_came(0).wait_recv()
    for j in (1, 3, 2):
        next_on(j).start()
    cgrad[...] = jnp.where(pre[...] > 0, gcodes[...] * inv_tokens, 0.0).astype(BF)

    def drain_cross(p, _):
        remote(sib_s.at[p], dsib_r.at[p], dx_s.at[p], dx_r.at[p], sib).wait_send()
        return 0

    lax.fori_loop(0, 8, drain_cross, 0)

    def enc_step(i, _):
        grad_begin(cent_t, cgrad, order(q, i), i % 2, 1.0, esib_r, ex_s, ex_r)

        @pl.when(i > 0)
        def _():
            grad_end(order(q, i - 1), (i + 1) % 2, esib_r, eown, enc_sum, ex_s, ex_r)

        return 0

    lax.fori_loop(0, 3, enc_step, 0)
    dec_sum.pass_diag()
    lax.fori_loop(3, 5, enc_step, 0)
    dec_sum.pass_ring()
    lax.fori_loop(5, 7, enc_step, 0)
    enc_sum.pass_diag()
    lax.fori_loop(7, 8, enc_step, 0)
    grad_end(order(q, 7), 1, esib_r, eown, enc_sum, ex_s, ex_r)
    enc_sum.pass_ring()
    dec_sum.pass_on()
    enc_sum.pass_on()

    for j in (1, 3, 2):
        next_came(j).wait_recv()
    for j in (1, 3, 2):
        next_diag(j).wait_recv()

    def permute(j, _):
        cols = pl.ds(pl.multiple_of(j * 512, 512), 512)
        batch[:, cols] = jnp.dot(
            put[...], rows48[:, cols], preferred_element_type=F32
        ).astype(BF)
        return 0

    lax.fori_loop(0, 9, permute, 0)
    out_cp = pltpu.make_async_copy(batch, next_out, loc.at[4])
    out_cp.start()

    def update(scatter, own, first, second, outs):
        scatter.finish(own)
        for out, value in zip(outs, adam_update(own[...], first[...], second[...])):
            out[...] = value

    for cp in moment_cps:
        cp.wait()
    update(dec_sum, down, df, ds, (ndf, nds, dup))
    update(enc_sum, eown, ef, es, (nef, nes, eup))

    enc_g.drain()
    dec_g.drain()
    err_g.drain()
    lat_sum.drain()
    dec_sum.drain()
    enc_sum.drain()

    def drain_group(k, _):
        to_group(k).wait_send()
        return 0

    lax.fori_loop(1, 16, drain_group, 0)
    for j in range(4):
        next_own(j).wait_send()
    for j in (1, 2, 3):
        next_on(j).wait_send()

    def drain_cross2(p, _):
        remote(sib_s.at[p], esib_r.at[p], ex_s.at[p], ex_r.at[p], sib).wait_send()
        return 0

    lax.fori_loop(0, 8, drain_cross2, 0)
    out_cp.wait()


def train_step(
    batch, next_acts, encw, decw_t, source, enc_bias, dec_bias, ef, es, df_t, ds_t, inv_tokens
):
    any_space = pl.BlockSpec(memory_space=pl.ANY)
    vmem = pl.BlockSpec(memory_space=pltpu.VMEM)
    dma = pltpu.SemaphoreType.DMA

    def received(size, size_a, width):
        return [
            pltpu.VMEM((8, size, width), BF),
            pltpu.VMEM((4, size_a, width), BF),
            pltpu.VMEM((4, size - size_a, width), BF),
            pltpu.VMEM((2, size - size_a, width), BF),
            pltpu.VMEM((size_a, width), BF),
            pltpu.VMEM((4, size_a // 2, width), BF),
            pltpu.VMEM((2, (size - size_a) // 2, width), BF),
        ]

    shard = jax.ShapeDtypeStruct((SH, LAT), BF)
    return pl.pallas_call(
        functools.partial(step_kernel, inv_tokens),
        out_shape=(
            jax.ShapeDtypeStruct((ROWS, D), BF),
            jax.ShapeDtypeStruct((ROWS, LAT), BF),
            jax.ShapeDtypeStruct((CH, ROWS), BF),
            *([shard] * 6),
        ),
        in_specs=[any_space] * 8 + [vmem] * 3,
        out_specs=[any_space] + [vmem] * 8,
        scratch_shapes=[
            pltpu.VMEM((ROWS, D), BF),
            pltpu.VMEM((ROWS, D), BF),
            pltpu.VMEM((D, ROWS), BF),
            pltpu.VMEM((CH, ROWS), F32),
            pltpu.VMEM((D, LAT), BF),
            pltpu.VMEM((D, LAT), BF),
            pltpu.VMEM((ROWS, LAT), F32),
            pltpu.VMEM((CH, ROWS), F32),
            pltpu.VMEM((D, ROWS), BF),
            pltpu.VMEM((ROWS, LAT), F32),
            pltpu.VMEM((ROWS, LAT), BF),
            *received(CH, CH_SUM_A, ROWS),
            *([pltpu.VMEM((8, SH, LAT), BF)] * 3),
            pltpu.VMEM((2, SH, LAT), F32),
            *received(SH, SH_SUM_A, LAT),
            pltpu.VMEM((SH, LAT), F32),
            *received(SH, SH_SUM_A, LAT),
            pltpu.VMEM((SH, LAT), F32),
            pltpu.VMEM((48, D), BF),
            pltpu.VMEM((48, D), F32),
            pltpu.VMEM((16, 4, D), BF),
            pltpu.VMEM((16, 4, D), BF),
            pltpu.VMEM((ROWS, D), BF),
            pltpu.VMEM((ROWS, ROWS), BF),
            *([pltpu.VMEM((SH, LAT), BF)] * 4),
            dma((9,)),
            dma((22,)), dma((22,)), dma((8,)), dma((8,)),
            dma((22,)), dma((22,)), dma((8,)), dma((8,)),
            dma((22,)), dma((22,)), dma((22,)), dma((22,)),
            dma((8,)), dma((8,)), dma((22,)), dma((22,)),
            dma((8,)), dma((8,)), dma((22,)), dma((22,)),
            dma((15,)), dma((15,)), dma((7,)), dma((7,)),
        ],
        compiler_params=pltpu.CompilerParams(
            collective_id=0, has_side_effects=True, vmem_limit_bytes=63 * 2**20
        ),
        cost_estimate=pl.CostEstimate(
            flops=5 * 2 * ROWS * LAT * D, bytes_accessed=16 * 2**20, transcendentals=0
        ),
    )(batch, next_acts, encw, decw_t, ef, es, df_t, ds_t, source, enc_bias, dec_bias)


def publish(*arrays):
    n = len(arrays)
    pieces = []
    for i, a in enumerate(arrays):
        step = a.shape[0] // 4 if a.size > 2**20 else a.shape[0]
        pieces += [(i, row, step) for row in range(0, a.shape[0], step)]

    def kernel(*refs):
        held, into, out_of = refs[2 * n : 3 * n], refs[3 * n], refs[3 * n + 1]

        def read(k):
            i, row, rows = pieces[k]
            part = pl.ds(row, rows)
            return pltpu.make_async_copy(refs[i].at[part], held[i].at[part], into.at[k])

        def write(k):
            i, row, rows = pieces[k]
            part = pl.ds(row, rows)
            return pltpu.make_async_copy(held[i].at[part], refs[n + i].at[part], out_of.at[k])

        for k in range(len(pieces)):
            read(k).start()
        for k in range(len(pieces)):
            read(k).wait()
            write(k).start()
        for k in range(len(pieces)):
            write(k).wait()

    any_space = pl.BlockSpec(memory_space=pl.ANY)
    return pl.pallas_call(
        kernel,
        out_shape=tuple(jax.ShapeDtypeStruct(a.shape, a.dtype) for a in arrays),
        in_specs=[any_space] * n,
        out_specs=[any_space] * n,
        scratch_shapes=[
            *[pltpu.VMEM(a.shape, a.dtype) for a in arrays],
            pltpu.SemaphoreType.DMA((len(pieces),)),
            pltpu.SemaphoreType.DMA((len(pieces),)),
        ],
        compiler_params=pltpu.CompilerParams(vmem_limit_bytes=63 * 2**20),
    )(*arrays)


def on_device(
    batch, next_acts, row_source, enc_weight, dec_weight, enc_bias, dec_bias,
    enc_first, enc_second, dec_first, dec_second,
):
    inv_tokens = 1.0 / (batch.shape[0] * 16)
    results = train_step(
        batch, next_acts, enc_weight, dec_weight.T, row_source.reshape(1, -1),
        enc_bias.reshape(1, LAT), dec_bias.reshape(D // 128, 128),
        enc_first, enc_second, dec_first.T, dec_second.T, inv_tokens,
    )
    next_batch, codes, err_t, nef, nes, eup, ndf, nds, dup = publish(*results)
    return next_batch, codes, err_t.T, nef, nes, eup, ndf.T, nds.T, dup.T


def solution(mesh):
    return jax.shard_map(
        on_device,
        mesh=mesh,
        in_specs=(
            P("rows", None),
            P(("rows", "lat"), None),
            P(),
            P("rows", "lat"),
            P("lat", "rows"),
            P("lat"),
            P(),
            P("rows", "lat"),
            P("rows", "lat"),
            P("lat", "rows"),
            P("lat", "rows"),
        ),
        out_specs=(
            P("rows", None),
            P("rows", "lat"),
            P("rows", "lat"),
            P("rows", "lat"),
            P("rows", "lat"),
            P("rows", "lat"),
            P("lat", "rows"),
            P("lat", "rows"),
            P("lat", "rows"),
        ),
        check_vma=False,
    )
```

```python
import functools

import jax
import jax.numpy as jnp
from jax import lax
from jax.experimental import pallas as pl
from jax.experimental.pallas import tpu as pltpu
from jax.sharding import PartitionSpec as P

beta_one = 0.9
beta_two = 0.999
correction_one = 1.0 - 0.9**3
correction_two = 1.0 - 0.999**3
eps_adam = 1e-08
sparsity_weight = 0.2

MESH = pl.DeviceIdType.MESH
BF = jnp.bfloat16
F32 = jnp.float32
D = 4608
ROWS = 384
LAT = 512
SH = 288
CH = 576
CH_A = 320
SH_A = 160
CH_SUM_A = 256
SH_SUM_A = 128
NT = (((1,), (1,)), ((), ()))
TN = (((0,), (0,)), ((), ()))


def adam_update(gradient, first, second):
    first_new = beta_one * first.astype(F32) + (1.0 - beta_one) * gradient
    second_new = beta_two * second.astype(F32) + (1.0 - beta_two) * gradient * gradient
    direction = first_new / correction_one / (jnp.sqrt(second_new / correction_two) + eps_adam)
    return first_new.astype(BF), second_new.astype(BF), direction.astype(BF)


def step_kernel(
    inv_tokens,
    batch_h, next_h, encw, decw, ef_h, es_h, df_h, ds_h, source, enc_bias, dec_bias,
    next_out, codes, err_out, nef, nes, eup, ndf, nds, dup,
    batch, cent, cent_t, neg_t, encf, decf, pre, recon, err, gcodes, cgrad,
    lpart, lrec_a, lrec_y, lrec_b, lrec_p, lrel_a, lrel_b,
    sib_s, dsib_r, esib_r, kept,
    dpart, drec_a, drec_y, drec_b, drec_p, drel_a, drel_b, down,
    epart, erec_a, erec_y, erec_b, erec_p, erel_a, erel_b, eown,
    nacts, tmp, out3, in3, rows48, put, ef, es, df, ds,
    loc, enc_s, enc_r, encx_s, encx_r, dec_s, dec_r, decx_s, decx_r,
    ls_s, ls_r, err_s, err_r, dx_s, dx_r, dg_s, dg_r, ex_s, ex_r, eg_s, eg_r,
    a2a_s, a2a_r, n_s, n_r,
):
    r = lax.axis_index("rows")
    l = lax.axis_index("lat")
    c = r % 2
    q = r // 2
    sib = (q * 2 + 1 - c, l)

    def remote(src, dst, ssem, rsem, device):
        return pltpu.make_async_remote_copy(
            src_ref=src, dst_ref=dst, send_sem=ssem, recv_sem=rsem,
            device_id=device, device_id_type=MESH,
        )

    def member(g, dm, db):
        return (g // 2 + dm) % 4 * 2 + (g + db) % 2

    def rows_dev(g):
        return (g * 2 + c, l)

    def lat_dev(g):
        return (r, g)

    def shard_at(g):
        return pl.multiple_of((g * 2 + c) * SH, 32)

    def shard(g, core):
        return pl.ds(pl.multiple_of((g * 2 + core) * SH, 32), SH)

    def chunk_at(g):
        return pl.multiple_of(g * CH, 64)

    def chunk(g):
        return pl.ds(chunk_at(g), CH)

    barrier = pltpu.get_barrier_semaphore()
    for k in range(1, 16):
        pl.semaphore_signal(barrier, inc=1, device_id=((r + k) % 16, l), device_id_type=MESH)
    for dm, db in ((0, 1), (1, 0), (2, 0), (3, 0)):
        pl.semaphore_signal(barrier, inc=1, device_id=lat_dev(member(l, dm, db)), device_id_type=MESH)
    batch_cp = pltpu.make_async_copy(batch_h, batch, loc.at[0])
    enc_cp = pltpu.make_async_copy(encw, encf.at[shard(q, c)], loc.at[1])
    dec_cp = pltpu.make_async_copy(decw, decf.at[shard(q, c)], loc.at[2])
    next_cp = pltpu.make_async_copy(next_h, nacts, loc.at[3])
    next_cp.start()
    enc_cp.start()
    batch_cp.start()
    dec_cp.start()
    moment_cps = [
        pltpu.make_async_copy(src, dst, loc.at[5 + i])
        for i, (src, dst) in enumerate(((ef_h, ef), (es_h, es), (df_h, df), (ds_h, ds)))
    ]
    pl.semaphore_wait(barrier, 19)

    class Gather:
        def __init__(self, full, at, g, dev, ssem, rsem, size, size_a):
            self.full, self.at, self.g, self.dev, self.s, self.r = full, at, g, dev, ssem, rsem
            self.size, self.size_a = size, size_a

        def part(self, g, which):
            if which == "a":
                return self.full.at[pl.ds(self.at(g), self.size_a)]
            return self.full.at[pl.ds(self.at(g) + self.size_a, self.size - self.size_a)]

        def copy(self, g, which, slot, to):
            part = self.part(g, which)
            return remote(part, part, self.s.at[slot], self.r.at[slot], self.dev(to))

        def own(self, dm, db, which):
            slot = dm if which == "a" else 4 + dm
            return self.copy(self.g, which, slot, member(self.g, dm, db))

        def came(self, dm, db, which):
            slot = dm if which == "a" else 4 + dm
            return self.copy(member(self.g, 4 - dm, db), which, slot, self.g)

        def on_a(self, j):
            return self.copy(member(self.g, 0, 1), "a", 8 + j, member(self.g, j, 0))

        def on_b(self, j):
            return self.copy(member(self.g, 4 - j, 0), "b", 12 + j, member(self.g, 0, 1))

        def diag_a(self, j):
            return self.copy(member(self.g, 4 - j, 1), "a", 8 + j, self.g)

        def diag_b(self, j):
            return self.copy(member(self.g, 4 - j, 1), "b", 12 + j, self.g)

        def half(self, kind, g, second, slot, to):
            size = self.size - self.size_a if kind == "b" else self.size_a
            first = size // 32 * 16
            at = self.at(g) + (self.size_a if kind == "b" else 0)
            part = self.full.at[pl.ds(at + first, size - first) if second else pl.ds(at, first)]
            return remote(part, part, self.s.at[slot], self.r.at[slot], self.dev(to))

        def relay(self, kind, j):
            g = member(self.g, 4 - j, 1 if kind == "p" else 0)
            return self.half(kind, g, j == 3, 16 + 2 * "bap".index(kind) + j // 3, member(self.g, j, 0))

        def relayed(self, kind, j):
            g = member(self.g, 2, 1 if kind == "p" else 0)
            return self.half(kind, g, j == 3, 16 + 2 * "bap".index(kind) + j // 3, self.g)

        def start(self):
            self.own(0, 1, "a").start()
            for j in (1, 3):
                self.own(j, 0, "b").start()
            self.own(0, 1, "b").start()
            for j in (1, 3):
                self.own(j, 0, "a").start()

        def forward_a(self):
            self.came(0, 1, "a").wait_recv()
            for j in (1, 3):
                self.on_a(j).start()

        def forward_b(self, j):
            if j == 2:
                self.relayed("b", 1).wait_recv()
                self.relayed("b", 3).wait_recv()
            else:
                self.came(j, 0, "b").wait_recv()
                self.relay("b", j).start()
            self.on_b(j).start()

        def hear_ring(self, j):
            self.came(j, 0, "a").wait_recv()
            self.relay("a", j).start()

        def hear_diag(self, j):
            self.diag_a(j).wait_recv()
            self.relay("p", j).start()

        def take_pair(self):
            self.came(0, 1, "b").wait_recv()

        def take_ring(self, j):
            if j == 2:
                self.relayed("a", 1).wait_recv()
                self.relayed("a", 3).wait_recv()

        def take_diag(self, j):
            if j == 2:
                self.relayed("p", 1).wait_recv()
                self.relayed("p", 3).wait_recv()
            self.diag_b(j).wait_recv()

        def drain(self):
            for dm, db in ((0, 1), (1, 0), (3, 0)):
                self.own(dm, db, "a").wait_send()
                self.own(dm, db, "b").wait_send()
            for j in (1, 3):
                self.on_a(j).wait_send()
                for kind in "bap":
                    self.relay(kind, j).wait_send()
            for j in (1, 2, 3):
                self.on_b(j).wait_send()

    class Scatter:
        def __init__(
            self, part, rec_a, rec_y, rec_b, rec_p, rel_a, rel_b, g, dev, ssem, rsem, size, size_a
        ):
            self.p, self.ra, self.ry, self.rb, self.rp = part, rec_a, rec_y, rec_b, rec_p
            self.la, self.lb = rel_a, rel_b
            self.g, self.dev, self.s, self.r = g, dev, ssem, rsem
            self.size, self.size_a = size, size_a
            self.a, self.b = pl.ds(0, size_a), pl.ds(size_a, size - size_a)

        def copy(self, src, dst, slot, to):
            return remote(src, dst, self.s.at[slot], self.r.at[slot], self.dev(to))

        def diag_a(self, j):
            src = self.p.at[member(self.g, j, 1), self.a]
            return self.copy(src, self.ra.at[j // 3], j, member(self.g, j, 0))

        def diag_b(self, j):
            src = self.p.at[member(self.g, j, 1), self.b]
            return self.copy(src, self.ry.at[j], 4 + j, member(self.g, 0, 1))

        def ring_a(self, j):
            src = self.p.at[member(self.g, j, 0), self.a]
            return self.copy(src, self.ra.at[2 + j // 3], 8 + j, member(self.g, j, 0))

        def ring_b(self, j):
            src = self.p.at[member(self.g, j, 0), self.b]
            return self.copy(src, self.rb.at[j // 3], 12 + j, member(self.g, j, 0))

        def pair_b(self):
            src = self.p.at[member(self.g, 0, 1), self.b]
            return self.copy(src, self.ry.at[0], 4, member(self.g, 0, 1))

        def pair_a(self):
            src = self.p.at[member(self.g, 0, 1), self.a]
            return self.copy(src, self.rp, 8, member(self.g, 0, 1))

        def half(self, kind, j):
            size_b = self.size - self.size_a
            if kind == "b":
                return pl.ds(self.size_a + j // 3 * (size_b // 2), size_b // 2)
            return pl.ds(j // 3 * (self.size_a // 2), self.size_a // 2)

        def held(self, kind, j):
            return self.lb.at[j // 3] if kind == "b" else self.la.at["dr".index(kind) * 2 + j // 3]

        def relay(self, kind, j):
            src = self.p.at[member(self.g, 2, 1 if kind == "d" else 0), self.half(kind, j)]
            slot = 16 + "drb".index(kind) * 2 + j // 3
            return self.copy(src, self.held(kind, j), slot, member(self.g, j, 0))

        def relays(self, kind):
            self.relay(kind, 1).start()
            self.relay(kind, 3).start()

        def add_relayed(self, kind, j):
            self.relay(kind, j).wait_recv()
            block = self.p.at[member(self.g, j, 1 if kind == "d" else 0), self.half(kind, j)]
            block[...] = (block[...].astype(F32) + self.held(kind, j)[...].astype(F32)).astype(BF)

        def emit(self, p):
            dm = (p // 2 + 4 - self.g // 2) % 4
            db = (p + self.g) % 2

            @pl.when(jnp.logical_and(db == 1, dm > 0))
            def _():
                self.diag_b(dm).start()

            @pl.when(jnp.logical_and(db == 1, dm == 2))
            def _():
                self.relays("d")

            @pl.when(jnp.logical_and(db == 0, dm == 2))
            def _():
                self.relays("r")

            @pl.when(jnp.logical_and(db == 1, dm == 0))
            def _():
                self.pair_b().start()

        def pass_diag(self):
            for j in (1, 3):
                self.add_relayed("d", j)
                self.diag_a(j).start()

        def pass_ring(self):
            for j in (1, 3):
                self.add_relayed("r", j)
                self.ring_a(j).start()

        def pass_on(self):
            for j in (2, 3, 1):
                self.diag_b(j).wait_recv()
                block = self.p.at[member(self.g, j, 0), self.b]
                block[...] = (block[...].astype(F32) + self.ry[j].astype(F32)).astype(BF)
                if j == 2:
                    self.relays("b")
            block = self.p.at[member(self.g, 0, 1), self.a]
            total = block[...].astype(F32)
            for j in (1, 3):
                self.diag_a(j).wait_recv()
                total = total + self.ra[j // 3].astype(F32)
            block[...] = total.astype(BF)
            self.pair_a().start()
            for j in (1, 3):
                self.add_relayed("b", j)
                self.ring_b(j).start()

        def finish(self, own):
            total = own[self.a, :]
            for j in (1, 3):
                self.ring_a(j).wait_recv()
                total = total + self.ra[2 + j // 3].astype(F32)
            self.pair_b().wait_recv()
            rest = own[self.b, :] + self.ry[0].astype(F32)
            self.pair_a().wait_recv()
            own[self.a, :] = total + self.rp[...].astype(F32)
            for j in (1, 3):
                self.ring_b(j).wait_recv()
                rest = rest + self.rb[j // 3].astype(F32)
            own[self.b, :] = rest

        def drain(self):
            for j in (1, 2, 3):
                self.diag_b(j).wait_send()
            for j in (1, 3):
                self.diag_a(j).wait_send()
                self.ring_a(j).wait_send()
                self.ring_b(j).wait_send()
                for kind in "drb":
                    self.relay(kind, j).wait_send()
            self.pair_a().wait_send()
            self.pair_b().wait_send()

    class Weights(Gather):
        def __init__(self, full, ssem, rsem, xs, xr, size_a):
            super().__init__(full, shard_at, q, rows_dev, ssem, rsem, SH, size_a)
            self.xs, self.xr = xs, xr

        def cross(self, dm, db):
            part = self.full.at[shard(member(q, 4 - dm, db), c)]
            return remote(part, part, self.xs.at[dm * 2 + db], self.xr.at[dm * 2 + db], sib)

        def crossed(self, dm, db):
            part = self.full.at[shard(member(q, 4 - dm, db), 1 - c)]
            return remote(part, part, self.xs.at[dm * 2 + db], self.xr.at[dm * 2 + db], sib)

        def cross_pair(self):
            self.take_pair()
            self.cross(0, 1).start()

        def cross_ring(self, j):
            if j == 2:
                self.take_ring(2)
            else:
                self.hear_ring(j)
            self.cross(j, 0).start()

        def settle(self):
            for j in (1, 3, 2):
                self.take_diag(j)
                self.cross(j, 1).start()
            for i in range(8):
                self.crossed(i // 2, i % 2).wait_recv()

        def drain(self):
            super().drain()
            for i in range(8):
                self.cross(i // 2, i % 2).wait_send()

    enc_g = Weights(encf, enc_s, enc_r, encx_s, encx_r, SH_A)
    dec_g = Weights(decf, dec_s, dec_r, decx_s, decx_r, SH_A)
    enc_cp.wait()
    enc_g.start()
    enc_g.cross(0, 0).start()

    next_cp.wait()
    lane48 = lax.broadcasted_iota(jnp.int32, (48, 48), 1)
    sub48 = lax.broadcasted_iota(jnp.int32, (48, 48), 0)
    mine = (r * 8 + l) * 48

    def find(j, dest):
        cols = pl.ds(pl.multiple_of(j * 512, 512), 512)
        ids = jnp.broadcast_to(source[:, cols], (48, 512))
        sub = lax.broadcasted_iota(jnp.int32, (48, 512), 0)
        lane = lax.broadcasted_iota(jnp.int32, (48, 512), 1)
        hit = jnp.where(ids == sub + mine, lane + j * 512, 0)
        return dest + jnp.sum(hit.astype(F32), axis=1, keepdims=True)

    dest = lax.fori_loop(0, 12, find, jnp.zeros((48, 1), F32))
    dest_row = jnp.sum(jnp.where(lane48 == sub48, dest, 0.0), axis=0, keepdims=True)
    slot = jnp.sum(jnp.where(dest < dest_row, 1.0, 0.0), axis=0, keepdims=True)
    pick = jnp.where(slot == sub48.astype(F32), 1.0, 0.0).astype(BF)
    tmp[...] = jnp.dot(pick, nacts[...], preferred_element_type=F32)
    for g in range(16):
        out3[g, 0:3, :] = tmp[3 * g : 3 * g + 3, :].astype(BF)

    def to_group(k):
        return remote(
            out3.at[(r + k) % 16], in3.at[r], a2a_s.at[k - 1], a2a_r.at[k - 1], ((r + k) % 16, l)
        )

    def from_group(k):
        part = in3.at[(r + 16 - k) % 16]
        return remote(part, part, a2a_s.at[k - 1], a2a_r.at[k - 1], (r, l))

    def send_group(k, _):
        to_group(k).start()
        return 0

    lax.fori_loop(1, 16, send_group, 0)
    in3[r] = out3[r]
    enc_g.forward_a()
    for j in (1, 3):
        enc_g.forward_b(j)
    for j in (1, 3):
        enc_g.cross_ring(j)
    dec_cp.wait()
    dec_g.start()
    dec_g.cross(0, 0).start()
    enc_g.forward_b(2)
    enc_g.cross_pair()
    for j in (1, 3):
        enc_g.hear_diag(j)

    for cp in moment_cps:
        cp.start()
    batch_cp.wait()

    def center(j, _):
        cols = pl.ds(pl.multiple_of(j * 128, 128), 128)
        x = batch[:, cols].astype(F32) - dec_bias[pl.ds(j, 1), :]
        cent[:, cols] = x.astype(BF)
        xt = x.T
        cent_t[pl.ds(pl.multiple_of(j * 128, 128), 128), :] = xt.astype(BF)
        for half in range(2):
            h = j * 2 + half

            @pl.when(h // 9 == l)
            def _():
                neg_t[pl.ds(pl.multiple_of((h % 9) * 64, 64), 64), :] = xt[64 * half : 64 * half + 64]

        return 0

    lax.fori_loop(0, 12, center, 0)
    dec_g.forward_a()
    for j in (1, 3):
        dec_g.forward_b(j)
    lax.fori_loop(12, 24, center, 0)
    enc_g.cross_ring(2)
    for j in (1, 3):
        dec_g.cross_ring(j)
    lax.fori_loop(24, 36, center, 0)
    dec_g.forward_b(2)
    for j in (1, 3):
        dec_g.hear_diag(j)

    def arrive(k, _):
        from_group(k).wait_recv()
        return 0

    lax.fori_loop(1, 16, arrive, 0)
    for g in range(16):
        tmp[3 * g : 3 * g + 3, :] = in3[g, 0:3, :].astype(F32)
    rows48[pl.ds(pl.multiple_of(l * 48, 16), 48), :] = tmp[...].astype(BF)

    def next_copy(g, slot, to):
        part = rows48.at[pl.ds(pl.multiple_of(g * 48, 16), 48)]
        return remote(part, part, n_s.at[slot], n_r.at[slot], lat_dev(to))

    def next_own(j):
        return next_copy(l, j, member(l, j, 0) if j else member(l, 0, 1))

    def next_came(j):
        return next_copy(member(l, 4 - j, 0) if j else member(l, 0, 1), j, l)

    def next_on(j):
        return next_copy(member(l, 0, 1), 3 + j, member(l, j, 0))

    def next_diag(j):
        return next_copy(member(l, 4 - j, 1), 3 + j, l)

    for j in range(4):
        next_own(j).start()

    place_l = lax.broadcasted_iota(jnp.int32, (ROWS, ROWS), 1)
    place_s = lax.broadcasted_iota(jnp.int32, (ROWS, ROWS), 0)
    wanted = source[:, pl.ds(pl.multiple_of(r * ROWS, 128), ROWS)]
    owner = jnp.right_shift(wanted * 43691, 21).astype(F32)
    owner_col = jnp.sum(jnp.where(place_l == place_s, owner, 0.0), axis=1, keepdims=True)
    earlier = jnp.logical_and(owner == owner_col, place_l < place_s)
    rank = jnp.sum(jnp.where(earlier, 1.0, 0.0), axis=1, keepdims=True)
    owner_i = owner_col.astype(jnp.int32)
    position = jnp.bitwise_and(owner_i, 7) * 48 + jnp.right_shift(owner_i, 3) * 3 + rank.astype(jnp.int32)
    put[...] = jnp.where(position == place_l, 1.0, 0.0).astype(BF)

    enc_g.settle()
    pre[...] = jnp.broadcast_to(enc_bias[...], (ROWS, LAT))

    def encode(j, _):
        part = pl.ds(pl.multiple_of(j * 1152, 128), 1152)
        pre[...] += jnp.dot(cent[:, part], encf[part, :], preferred_element_type=F32)
        return 0

    lax.fori_loop(0, 4, encode, 0)
    codes[...] = jnp.maximum(pre[...], 0.0).astype(BF)
    dec_g.cross_pair()
    dec_g.cross_ring(2)

    dec_g.settle()

    lat_sum = Scatter(lpart, lrec_a, lrec_y, lrec_b, lrec_p, lrel_a, lrel_b, l, lat_dev, ls_s, ls_r, CH, CH_SUM_A)

    def order(g, i):
        return member(g, (i + 2) % 4, 1 - i // 4)

    def decode(i, _):
        p = order(l, i)
        part = lax.dot_general(decf[chunk(p), :], codes[...], NT, preferred_element_type=F32)
        lpart[p] = part.astype(BF)
        lat_sum.emit(p)

        @pl.when(i == 6)
        def _():
            recon[...] = part - neg_t[...]

        return 0

    lax.fori_loop(0, 5, decode, 0)
    lat_sum.pass_diag()
    lax.fori_loop(5, 8, decode, 0)
    lat_sum.pass_ring()
    lat_sum.pass_on()
    lat_sum.finish(recon)
    err[chunk(l), :] = recon[...].astype(BF)
    err_out[...] = err[chunk(l), :]

    err_g = Gather(err, chunk_at, l, lat_dev, err_s, err_r, CH, CH_A)
    err_g.start()
    gcodes[...] = jnp.full((ROWS, LAT), sparsity_weight, F32)

    def grad_begin(lhs, rhs, p, hold, scale, sib_r, xs, xr):
        other = jnp.dot(lhs[shard(p, 1 - c), :], rhs[...], preferred_element_type=F32)
        sib_s[p] = (other * scale).astype(BF)
        remote(sib_s.at[p], sib_r.at[p], xs.at[p], xr.at[p], sib).start()
        mine = jnp.dot(lhs[shard(p, c), :], rhs[...], preferred_element_type=F32)
        kept[hold] = mine * scale

    def grad_end(p, hold, sib_r, own, scatter, xs, xr):
        remote(sib_s.at[p], sib_r.at[p], xs.at[p], xr.at[p], sib).wait_recv()
        total = kept[hold] + sib_r[p].astype(F32)
        scatter.p[p] = total.astype(BF)
        scatter.emit(p)

        @pl.when(p == q)
        def _():
            own[...] = total

    dec_sum = Scatter(dpart, drec_a, drec_y, drec_b, drec_p, drel_a, drel_b, q, rows_dev, dg_s, dg_r, SH, SH_SUM_A)
    enc_sum = Scatter(epart, erec_a, erec_y, erec_b, erec_p, erel_a, erel_b, q, rows_dev, eg_s, eg_r, SH, SH_SUM_A)

    def error_begin(dm, db, hold):
        p = member(l, dm, db)
        gcodes[...] += lax.dot_general(
            err[chunk(p), :], decf[chunk(p), :], TN, preferred_element_type=F32
        )
        grad_begin(err, codes, p, hold, inv_tokens, dsib_r, dx_s, dx_r)

    def error_end(dm, db, hold):
        grad_end(member(l, dm, db), hold, dsib_r, down, dec_sum, dx_s, dx_r)

    error_begin(0, 0, 0)
    err_g.forward_a()
    err_g.forward_b(1)
    error_end(0, 0, 0)
    err_g.forward_b(3)
    err_g.hear_ring(1)
    err_g.hear_ring(3)
    err_g.take_pair()
    error_begin(0, 1, 1)
    err_g.forward_b(2)
    before = (0, 1)
    for i, (j, db) in enumerate(((1, 0), (3, 0), (2, 0), (1, 1), (3, 1), (2, 1))):
        if db:
            err_g.take_diag(j)
        else:
            err_g.take_ring(j)
        error_begin(4 - j, db, i % 2)
        error_end(*before, (i + 1) % 2)
        before = (4 - j, db)
        if i in (0, 1):
            err_g.hear_diag((1, 3)[i])
    error_end(*before, 1)
    next_came(0).wait_recv()
    for j in (1, 3, 2):
        next_on(j).start()
    cgrad[...] = jnp.where(pre[...] > 0, gcodes[...] * inv_tokens, 0.0).astype(BF)

    def drain_cross(p, _):
        remote(sib_s.at[p], dsib_r.at[p], dx_s.at[p], dx_r.at[p], sib).wait_send()
        return 0

    lax.fori_loop(0, 8, drain_cross, 0)

    def enc_step(i, _):
        grad_begin(cent_t, cgrad, order(q, i), i % 2, 1.0, esib_r, ex_s, ex_r)

        @pl.when(i > 0)
        def _():
            grad_end(order(q, i - 1), (i + 1) % 2, esib_r, eown, enc_sum, ex_s, ex_r)

        return 0

    lax.fori_loop(0, 3, enc_step, 0)
    dec_sum.pass_diag()
    lax.fori_loop(3, 5, enc_step, 0)
    dec_sum.pass_ring()
    lax.fori_loop(5, 7, enc_step, 0)
    enc_sum.pass_diag()
    lax.fori_loop(7, 8, enc_step, 0)
    grad_end(order(q, 7), 1, esib_r, eown, enc_sum, ex_s, ex_r)
    enc_sum.pass_ring()
    dec_sum.pass_on()
    enc_sum.pass_on()

    for j in (1, 3, 2):
        next_came(j).wait_recv()
    for j in (1, 3, 2):
        next_diag(j).wait_recv()

    def permute(j, _):
        cols = pl.ds(pl.multiple_of(j * 512, 512), 512)
        batch[:, cols] = jnp.dot(
            put[...], rows48[:, cols], preferred_element_type=F32
        ).astype(BF)
        return 0

    lax.fori_loop(0, 9, permute, 0)
    out_cp = pltpu.make_async_copy(batch, next_out, loc.at[4])
    out_cp.start()

    def update(scatter, own, first, second, outs):
        scatter.finish(own)
        for out, value in zip(outs, adam_update(own[...], first[...], second[...])):
            out[...] = value

    for cp in moment_cps:
        cp.wait()
    update(dec_sum, down, df, ds, (ndf, nds, dup))
    update(enc_sum, eown, ef, es, (nef, nes, eup))

    enc_g.drain()
    dec_g.drain()
    err_g.drain()
    lat_sum.drain()
    dec_sum.drain()
    enc_sum.drain()

    def drain_group(k, _):
        to_group(k).wait_send()
        return 0

    lax.fori_loop(1, 16, drain_group, 0)
    for j in range(4):
        next_own(j).wait_send()
    for j in (1, 2, 3):
        next_on(j).wait_send()

    def drain_cross2(p, _):
        remote(sib_s.at[p], esib_r.at[p], ex_s.at[p], ex_r.at[p], sib).wait_send()
        return 0

    lax.fori_loop(0, 8, drain_cross2, 0)
    out_cp.wait()


def train_step(
    batch, next_acts, encw, decw_t, source, enc_bias, dec_bias, ef, es, df_t, ds_t, inv_tokens
):
    any_space = pl.BlockSpec(memory_space=pl.ANY)
    vmem = pl.BlockSpec(memory_space=pltpu.VMEM)
    dma = pltpu.SemaphoreType.DMA

    def received(size, size_a, width):
        return [
            pltpu.VMEM((8, size, width), BF),
            pltpu.VMEM((4, size_a, width), BF),
            pltpu.VMEM((4, size - size_a, width), BF),
            pltpu.VMEM((2, size - size_a, width), BF),
            pltpu.VMEM((size_a, width), BF),
            pltpu.VMEM((4, size_a // 2, width), BF),
            pltpu.VMEM((2, (size - size_a) // 2, width), BF),
        ]

    shard = jax.ShapeDtypeStruct((SH, LAT), BF)
    return pl.pallas_call(
        functools.partial(step_kernel, inv_tokens),
        out_shape=(
            jax.ShapeDtypeStruct((ROWS, D), BF),
            jax.ShapeDtypeStruct((ROWS, LAT), BF),
            jax.ShapeDtypeStruct((CH, ROWS), BF),
            *([shard] * 6),
        ),
        in_specs=[any_space] * 8 + [vmem] * 3,
        out_specs=[any_space] + [vmem] * 8,
        scratch_shapes=[
            pltpu.VMEM((ROWS, D), BF),
            pltpu.VMEM((ROWS, D), BF),
            pltpu.VMEM((D, ROWS), BF),
            pltpu.VMEM((CH, ROWS), F32),
            pltpu.VMEM((D, LAT), BF),
            pltpu.VMEM((D, LAT), BF),
            pltpu.VMEM((ROWS, LAT), F32),
            pltpu.VMEM((CH, ROWS), F32),
            pltpu.VMEM((D, ROWS), BF),
            pltpu.VMEM((ROWS, LAT), F32),
            pltpu.VMEM((ROWS, LAT), BF),
            *received(CH, CH_SUM_A, ROWS),
            *([pltpu.VMEM((8, SH, LAT), BF)] * 3),
            pltpu.VMEM((2, SH, LAT), F32),
            *received(SH, SH_SUM_A, LAT),
            pltpu.VMEM((SH, LAT), F32),
            *received(SH, SH_SUM_A, LAT),
            pltpu.VMEM((SH, LAT), F32),
            pltpu.VMEM((48, D), BF),
            pltpu.VMEM((48, D), F32),
            pltpu.VMEM((16, 4, D), BF),
            pltpu.VMEM((16, 4, D), BF),
            pltpu.VMEM((ROWS, D), BF),
            pltpu.VMEM((ROWS, ROWS), BF),
            *([pltpu.VMEM((SH, LAT), BF)] * 4),
            dma((9,)),
            dma((22,)), dma((22,)), dma((8,)), dma((8,)),
            dma((22,)), dma((22,)), dma((8,)), dma((8,)),
            dma((22,)), dma((22,)), dma((22,)), dma((22,)),
            dma((8,)), dma((8,)), dma((22,)), dma((22,)),
            dma((8,)), dma((8,)), dma((22,)), dma((22,)),
            dma((15,)), dma((15,)), dma((7,)), dma((7,)),
        ],
        compiler_params=pltpu.CompilerParams(
            collective_id=0, has_side_effects=True, vmem_limit_bytes=63 * 2**20
        ),
        cost_estimate=pl.CostEstimate(
            flops=5 * 2 * ROWS * LAT * D, bytes_accessed=16 * 2**20, transcendentals=0
        ),
    )(batch, next_acts, encw, decw_t, ef, es, df_t, ds_t, source, enc_bias, dec_bias)


def publish(*arrays):
    n = len(arrays)
    pieces = []
    for i, a in enumerate(arrays):
        step = a.shape[0] // 4 if a.size > 2**20 else a.shape[0]
        pieces += [(i, row, step) for row in range(0, a.shape[0], step)]

    def kernel(*refs):
        held, into, out_of = refs[2 * n : 3 * n], refs[3 * n], refs[3 * n + 1]

        def read(k):
            i, row, rows = pieces[k]
            part = pl.ds(row, rows)
            return pltpu.make_async_copy(refs[i].at[part], held[i].at[part], into.at[k])

        def write(k):
            i, row, rows = pieces[k]
            part = pl.ds(row, rows)
            return pltpu.make_async_copy(held[i].at[part], refs[n + i].at[part], out_of.at[k])

        for k in range(len(pieces)):
            read(k).start()
        for k in range(len(pieces)):
            read(k).wait()
            write(k).start()
        for k in range(len(pieces)):
            write(k).wait()

    any_space = pl.BlockSpec(memory_space=pl.ANY)
    return pl.pallas_call(
        kernel,
        out_shape=tuple(jax.ShapeDtypeStruct(a.shape, a.dtype) for a in arrays),
        in_specs=[any_space] * n,
        out_specs=[any_space] * n,
        scratch_shapes=[
            *[pltpu.VMEM(a.shape, a.dtype) for a in arrays],
            pltpu.SemaphoreType.DMA((len(pieces),)),
            pltpu.SemaphoreType.DMA((len(pieces),)),
        ],
        compiler_params=pltpu.CompilerParams(vmem_limit_bytes=63 * 2**20),
    )(*arrays)


def on_device(
    batch, next_acts, row_source, enc_weight, dec_weight, enc_bias, dec_bias,
    enc_first, enc_second, dec_first, dec_second,
):
    inv_tokens = 1.0 / (batch.shape[0] * 16)
    results = train_step(
        batch, next_acts, enc_weight, dec_weight.T, row_source.reshape(1, -1),
        enc_bias.reshape(1, LAT), dec_bias.reshape(D // 128, 128),
        enc_first, enc_second, dec_first.T, dec_second.T, inv_tokens,
    )
    next_batch, codes, err_t, nef, nes, eup, ndf, nds, dup = publish(*results)
    return next_batch, codes, err_t.T, nef, nes, eup, ndf.T, nds.T, dup.T


def solution(mesh):
    return jax.shard_map(
        on_device,
        mesh=mesh,
        in_specs=(
            P("rows", None),
            P(("rows", "lat"), None),
            P(),
            P("rows", "lat"),
            P("lat", "rows"),
            P("lat"),
            P(),
            P("rows", "lat"),
            P("rows", "lat"),
            P("lat", "rows"),
            P("lat", "rows"),
        ),
        out_specs=(
            P("rows", None),
            P("rows", "lat"),
            P("rows", "lat"),
            P("rows", "lat"),
            P("rows", "lat"),
            P("rows", "lat"),
            P("lat", "rows"),
            P("lat", "rows"),
            P("lat", "rows"),
        ),
        check_vma=False,
    )
```

```python
import functools

import jax
import jax.numpy as jnp
from jax import lax
from jax.experimental import pallas as pl
from jax.experimental.pallas import tpu as pltpu
from jax.sharding import PartitionSpec as P

beta_one = 0.9
beta_two = 0.999
correction_one = 1.0 - 0.9**3
correction_two = 1.0 - 0.999**3
eps_adam = 1e-08
sparsity_weight = 0.2

MESH = pl.DeviceIdType.MESH
BF = jnp.bfloat16
F32 = jnp.float32
D = 4608
ROWS = 384
LAT = 512
SH = 288
CH = 576
CH_A = 320
SH_A = 160
CH_SUM_A = 256
SH_SUM_A = 128
NT = (((1,), (1,)), ((), ()))
TN = (((0,), (0,)), ((), ()))


def adam_update(gradient, first, second):
    first_new = beta_one * first.astype(F32) + (1.0 - beta_one) * gradient
    second_new = beta_two * second.astype(F32) + (1.0 - beta_two) * gradient * gradient
    direction = first_new / correction_one / (jnp.sqrt(second_new / correction_two) + eps_adam)
    return first_new.astype(BF), second_new.astype(BF), direction.astype(BF)


def step_kernel(
    inv_tokens,
    batch_h, next_h, encw, decw, ef_h, es_h, df_h, ds_h, source, enc_bias, dec_bias,
    next_out, codes, err_out, nef, nes, eup, ndf, nds, dup,
    batch, cent, cent_t, neg_t, encf, decf, pre, recon, err, gcodes, cgrad,
    lpart, lrec_a, lrec_y, lrec_b, lrec_p, lrel_a, lrel_b,
    sib_s, dsib_r, esib_r, kept,
    dpart, drec_a, drec_y, drec_b, drec_p, drel_a, drel_b, down,
    epart, erec_a, erec_y, erec_b, erec_p, erel_a, erel_b, eown,
    nacts, tmp, out3, in3, rows48, put, ef, es, df, ds,
    loc, enc_s, enc_r, encx_s, encx_r, dec_s, dec_r, decx_s, decx_r,
    ls_s, ls_r, err_s, err_r, dx_s, dx_r, dg_s, dg_r, ex_s, ex_r, eg_s, eg_r,
    a2a_s, a2a_r, n_s, n_r,
):
    r = lax.axis_index("rows")
    l = lax.axis_index("lat")
    c = r % 2
    q = r // 2
    sib = (q * 2 + 1 - c, l)

    def remote(src, dst, ssem, rsem, device):
        return pltpu.make_async_remote_copy(
            src_ref=src, dst_ref=dst, send_sem=ssem, recv_sem=rsem,
            device_id=device, device_id_type=MESH,
        )

    def member(g, dm, db):
        return (g // 2 + dm) % 4 * 2 + (g + db) % 2

    def rows_dev(g):
        return (g * 2 + c, l)

    def lat_dev(g):
        return (r, g)

    def shard_at(g):
        return pl.multiple_of((g * 2 + c) * SH, 32)

    def shard(g, core):
        return pl.ds(pl.multiple_of((g * 2 + core) * SH, 32), SH)

    def chunk_at(g):
        return pl.multiple_of(g * CH, 64)

    def chunk(g):
        return pl.ds(chunk_at(g), CH)

    barrier = pltpu.get_barrier_semaphore()
    for k in range(1, 16):
        pl.semaphore_signal(barrier, inc=1, device_id=((r + k) % 16, l), device_id_type=MESH)
    for dm, db in ((0, 1), (1, 0), (2, 0), (3, 0)):
        pl.semaphore_signal(barrier, inc=1, device_id=lat_dev(member(l, dm, db)), device_id_type=MESH)
    batch_cp = pltpu.make_async_copy(batch_h, batch, loc.at[0])
    enc_cp = pltpu.make_async_copy(encw, encf.at[shard(q, c)], loc.at[1])
    dec_cp = pltpu.make_async_copy(decw, decf.at[shard(q, c)], loc.at[2])
    next_cp = pltpu.make_async_copy(next_h, nacts, loc.at[3])
    next_cp.start()
    enc_cp.start()
    batch_cp.start()
    dec_cp.start()
    moment_cps = [
        pltpu.make_async_copy(src, dst, loc.at[5 + i])
        for i, (src, dst) in enumerate(((ef_h, ef), (es_h, es), (df_h, df), (ds_h, ds)))
    ]
    pl.semaphore_wait(barrier, 19)

    class Gather:
        def __init__(self, full, at, g, dev, ssem, rsem, size, size_a):
            self.full, self.at, self.g, self.dev, self.s, self.r = full, at, g, dev, ssem, rsem
            self.size, self.size_a = size, size_a

        def part(self, g, which):
            if which == "a":
                return self.full.at[pl.ds(self.at(g), self.size_a)]
            return self.full.at[pl.ds(self.at(g) + self.size_a, self.size - self.size_a)]

        def copy(self, g, which, slot, to):
            part = self.part(g, which)
            return remote(part, part, self.s.at[slot], self.r.at[slot], self.dev(to))

        def own(self, dm, db, which):
            slot = dm if which == "a" else 4 + dm
            return self.copy(self.g, which, slot, member(self.g, dm, db))

        def came(self, dm, db, which):
            slot = dm if which == "a" else 4 + dm
            return self.copy(member(self.g, 4 - dm, db), which, slot, self.g)

        def on_a(self, j):
            return self.copy(member(self.g, 0, 1), "a", 8 + j, member(self.g, j, 0))

        def on_b(self, j):
            return self.copy(member(self.g, 4 - j, 0), "b", 12 + j, member(self.g, 0, 1))

        def diag_a(self, j):
            return self.copy(member(self.g, 4 - j, 1), "a", 8 + j, self.g)

        def diag_b(self, j):
            return self.copy(member(self.g, 4 - j, 1), "b", 12 + j, self.g)

        def half(self, kind, g, second, slot, to):
            size = self.size - self.size_a if kind == "b" else self.size_a
            first = size // 32 * 16
            at = self.at(g) + (self.size_a if kind == "b" else 0)
            part = self.full.at[pl.ds(at + first, size - first) if second else pl.ds(at, first)]
            return remote(part, part, self.s.at[slot], self.r.at[slot], self.dev(to))

        def relay(self, kind, j):
            g = member(self.g, 4 - j, 1 if kind == "p" else 0)
            return self.half(kind, g, j == 3, 16 + 2 * "bap".index(kind) + j // 3, member(self.g, j, 0))

        def relayed(self, kind, j):
            g = member(self.g, 2, 1 if kind == "p" else 0)
            return self.half(kind, g, j == 3, 16 + 2 * "bap".index(kind) + j // 3, self.g)

        def start(self):
            self.own(0, 1, "a").start()
            for j in (1, 3):
                self.own(j, 0, "b").start()
            self.own(0, 1, "b").start()
            for j in (1, 3):
                self.own(j, 0, "a").start()

        def forward_a(self):
            self.came(0, 1, "a").wait_recv()
            for j in (1, 3):
                self.on_a(j).start()

        def forward_b(self, j):
            if j == 2:
                self.relayed("b", 1).wait_recv()
                self.relayed("b", 3).wait_recv()
            else:
                self.came(j, 0, "b").wait_recv()
                self.relay("b", j).start()
            self.on_b(j).start()

        def hear_ring(self, j):
            self.came(j, 0, "a").wait_recv()
            self.relay("a", j).start()

        def hear_diag(self, j):
            self.diag_a(j).wait_recv()
            self.relay("p", j).start()

        def take_pair(self):
            self.came(0, 1, "b").wait_recv()

        def take_ring(self, j):
            if j == 2:
                self.relayed("a", 1).wait_recv()
                self.relayed("a", 3).wait_recv()

        def take_diag(self, j):
            if j == 2:
                self.relayed("p", 1).wait_recv()
                self.relayed("p", 3).wait_recv()
            self.diag_b(j).wait_recv()

        def drain(self):
            for dm, db in ((0, 1), (1, 0), (3, 0)):
                self.own(dm, db, "a").wait_send()
                self.own(dm, db, "b").wait_send()
            for j in (1, 3):
                self.on_a(j).wait_send()
                for kind in "bap":
                    self.relay(kind, j).wait_send()
            for j in (1, 2, 3):
                self.on_b(j).wait_send()

    class Scatter:
        def __init__(
            self, part, rec_a, rec_y, rec_b, rec_p, rel_a, rel_b, g, dev, ssem, rsem, size, size_a
        ):
            self.p, self.ra, self.ry, self.rb, self.rp = part, rec_a, rec_y, rec_b, rec_p
            self.la, self.lb = rel_a, rel_b
            self.g, self.dev, self.s, self.r = g, dev, ssem, rsem
            self.size, self.size_a = size, size_a
            self.a, self.b = pl.ds(0, size_a), pl.ds(size_a, size - size_a)

        def copy(self, src, dst, slot, to):
            return remote(src, dst, self.s.at[slot], self.r.at[slot], self.dev(to))

        def diag_a(self, j):
            src = self.p.at[member(self.g, j, 1), self.a]
            return self.copy(src, self.ra.at[j // 3], j, member(self.g, j, 0))

        def diag_b(self, j):
            src = self.p.at[member(self.g, j, 1), self.b]
            return self.copy(src, self.ry.at[j], 4 + j, member(self.g, 0, 1))

        def ring_a(self, j):
            src = self.p.at[member(self.g, j, 0), self.a]
            return self.copy(src, self.ra.at[2 + j // 3], 8 + j, member(self.g, j, 0))

        def ring_b(self, j):
            src = self.p.at[member(self.g, j, 0), self.b]
            return self.copy(src, self.rb.at[j // 3], 12 + j, member(self.g, j, 0))

        def pair_b(self):
            src = self.p.at[member(self.g, 0, 1), self.b]
            return self.copy(src, self.ry.at[0], 4, member(self.g, 0, 1))

        def pair_a(self):
            src = self.p.at[member(self.g, 0, 1), self.a]
            return self.copy(src, self.rp, 8, member(self.g, 0, 1))

        def half(self, kind, j):
            size_b = self.size - self.size_a
            if kind == "b":
                return pl.ds(self.size_a + j // 3 * (size_b // 2), size_b // 2)
            return pl.ds(j // 3 * (self.size_a // 2), self.size_a // 2)

        def held(self, kind, j):
            return self.lb.at[j // 3] if kind == "b" else self.la.at["dr".index(kind) * 2 + j // 3]

        def relay(self, kind, j):
            src = self.p.at[member(self.g, 2, 1 if kind == "d" else 0), self.half(kind, j)]
            slot = 16 + "drb".index(kind) * 2 + j // 3
            return self.copy(src, self.held(kind, j), slot, member(self.g, j, 0))

        def relays(self, kind):
            self.relay(kind, 1).start()
            self.relay(kind, 3).start()

        def add_relayed(self, kind, j):
            self.relay(kind, j).wait_recv()
            block = self.p.at[member(self.g, j, 1 if kind == "d" else 0), self.half(kind, j)]
            block[...] = (block[...].astype(F32) + self.held(kind, j)[...].astype(F32)).astype(BF)

        def emit(self, p):
            dm = (p // 2 + 4 - self.g // 2) % 4
            db = (p + self.g) % 2

            @pl.when(jnp.logical_and(db == 1, dm > 0))
            def _():
                self.diag_b(dm).start()

            @pl.when(jnp.logical_and(db == 1, dm == 2))
            def _():
                self.relays("d")

            @pl.when(jnp.logical_and(db == 0, dm == 2))
            def _():
                self.relays("r")

            @pl.when(jnp.logical_and(db == 1, dm == 0))
            def _():
                self.pair_b().start()

        def pass_diag(self):
            for j in (1, 3):
                self.add_relayed("d", j)
                self.diag_a(j).start()

        def pass_ring(self):
            for j in (1, 3):
                self.add_relayed("r", j)
                self.ring_a(j).start()

        def pass_on(self):
            for j in (2, 3, 1):
                self.diag_b(j).wait_recv()
                block = self.p.at[member(self.g, j, 0), self.b]
                block[...] = (block[...].astype(F32) + self.ry[j].astype(F32)).astype(BF)
                if j == 2:
                    self.relays("b")
            block = self.p.at[member(self.g, 0, 1), self.a]
            total = block[...].astype(F32)
            for j in (1, 3):
                self.diag_a(j).wait_recv()
                total = total + self.ra[j // 3].astype(F32)
            block[...] = total.astype(BF)
            self.pair_a().start()
            for j in (1, 3):
                self.add_relayed("b", j)
                self.ring_b(j).start()

        def finish(self, own):
            total = own[self.a, :]
            for j in (1, 3):
                self.ring_a(j).wait_recv()
                total = total + self.ra[2 + j // 3].astype(F32)
            self.pair_b().wait_recv()
            rest = own[self.b, :] + self.ry[0].astype(F32)
            self.pair_a().wait_recv()
            own[self.a, :] = total + self.rp[...].astype(F32)
            for j in (1, 3):
                self.ring_b(j).wait_recv()
                rest = rest + self.rb[j // 3].astype(F32)
            own[self.b, :] = rest

        def drain(self):
            for j in (1, 2, 3):
                self.diag_b(j).wait_send()
            for j in (1, 3):
                self.diag_a(j).wait_send()
                self.ring_a(j).wait_send()
                self.ring_b(j).wait_send()
                for kind in "drb":
                    self.relay(kind, j).wait_send()
            self.pair_a().wait_send()
            self.pair_b().wait_send()

    class Weights(Gather):
        def __init__(self, full, ssem, rsem, xs, xr, size_a):
            super().__init__(full, shard_at, q, rows_dev, ssem, rsem, SH, size_a)
            self.xs, self.xr = xs, xr

        def cross(self, dm, db):
            part = self.full.at[shard(member(q, 4 - dm, db), c)]
            return remote(part, part, self.xs.at[dm * 2 + db], self.xr.at[dm * 2 + db], sib)

        def crossed(self, dm, db):
            part = self.full.at[shard(member(q, 4 - dm, db), 1 - c)]
            return remote(part, part, self.xs.at[dm * 2 + db], self.xr.at[dm * 2 + db], sib)

        def cross_pair(self):
            self.take_pair()
            self.cross(0, 1).start()

        def cross_ring(self, j):
            if j == 2:
                self.take_ring(2)
            else:
                self.hear_ring(j)
            self.cross(j, 0).start()

        def settle(self):
            for j in (1, 3, 2):
                self.take_diag(j)
                self.cross(j, 1).start()
            for i in range(8):
                self.crossed(i // 2, i % 2).wait_recv()

        def drain(self):
            super().drain()
            for i in range(8):
                self.cross(i // 2, i % 2).wait_send()

    enc_g = Weights(encf, enc_s, enc_r, encx_s, encx_r, SH_A)
    dec_g = Weights(decf, dec_s, dec_r, decx_s, decx_r, SH_A)
    enc_cp.wait()
    enc_g.start()
    enc_g.cross(0, 0).start()

    next_cp.wait()
    lane48 = lax.broadcasted_iota(jnp.int32, (48, 48), 1)
    sub48 = lax.broadcasted_iota(jnp.int32, (48, 48), 0)
    mine = (r * 8 + l) * 48

    def find(j, dest):
        cols = pl.ds(pl.multiple_of(j * 512, 512), 512)
        ids = jnp.broadcast_to(source[:, cols], (48, 512))
        sub = lax.broadcasted_iota(jnp.int32, (48, 512), 0)
        lane = lax.broadcasted_iota(jnp.int32, (48, 512), 1)
        hit = jnp.where(ids == sub + mine, lane + j * 512, 0)
        return dest + jnp.sum(hit.astype(F32), axis=1, keepdims=True)

    dest = lax.fori_loop(0, 12, find, jnp.zeros((48, 1), F32))
    dest_row = jnp.sum(jnp.where(lane48 == sub48, dest, 0.0), axis=0, keepdims=True)
    slot = jnp.sum(jnp.where(dest < dest_row, 1.0, 0.0), axis=0, keepdims=True)
    pick = jnp.where(slot == sub48.astype(F32), 1.0, 0.0).astype(BF)
    tmp[...] = jnp.dot(pick, nacts[...], preferred_element_type=F32)
    for g in range(16):
        out3[g, 0:3, :] = tmp[3 * g : 3 * g + 3, :].astype(BF)

    def to_group(k):
        return remote(
            out3.at[(r + k) % 16], in3.at[r], a2a_s.at[k - 1], a2a_r.at[k - 1], ((r + k) % 16, l)
        )

    def from_group(k):
        part = in3.at[(r + 16 - k) % 16]
        return remote(part, part, a2a_s.at[k - 1], a2a_r.at[k - 1], (r, l))

    def send_group(k, _):
        to_group(k).start()
        return 0

    lax.fori_loop(1, 16, send_group, 0)
    in3[r] = out3[r]
    enc_g.forward_a()
    for j in (1, 3):
        enc_g.forward_b(j)
    for j in (1, 3):
        enc_g.cross_ring(j)
    dec_cp.wait()
    dec_g.start()
    dec_g.cross(0, 0).start()
    enc_g.forward_b(2)
    enc_g.cross_pair()
    for j in (1, 3):
        enc_g.hear_diag(j)

    for cp in moment_cps:
        cp.start()
    batch_cp.wait()

    def center(j, _):
        cols = pl.ds(pl.multiple_of(j * 128, 128), 128)
        x = batch[:, cols].astype(F32) - dec_bias[pl.ds(j, 1), :]
        cent[:, cols] = x.astype(BF)
        xt = x.T
        cent_t[pl.ds(pl.multiple_of(j * 128, 128), 128), :] = xt.astype(BF)
        for half in range(2):
            h = j * 2 + half

            @pl.when(h // 9 == l)
            def _():
                neg_t[pl.ds(pl.multiple_of((h % 9) * 64, 64), 64), :] = xt[64 * half : 64 * half + 64]

        return 0

    lax.fori_loop(0, 12, center, 0)
    dec_g.forward_a()
    for j in (1, 3):
        dec_g.forward_b(j)
    lax.fori_loop(12, 24, center, 0)
    enc_g.cross_ring(2)
    for j in (1, 3):
        dec_g.cross_ring(j)
    lax.fori_loop(24, 36, center, 0)
    dec_g.forward_b(2)
    for j in (1, 3):
        dec_g.hear_diag(j)

    def arrive(k, _):
        from_group(k).wait_recv()
        return 0

    lax.fori_loop(1, 16, arrive, 0)
    for g in range(16):
        tmp[3 * g : 3 * g + 3, :] = in3[g, 0:3, :].astype(F32)
    rows48[pl.ds(pl.multiple_of(l * 48, 16), 48), :] = tmp[...].astype(BF)

    def next_copy(g, slot, to):
        part = rows48.at[pl.ds(pl.multiple_of(g * 48, 16), 48)]
        return remote(part, part, n_s.at[slot], n_r.at[slot], lat_dev(to))

    def next_own(j):
        return next_copy(l, j, member(l, j, 0) if j else member(l, 0, 1))

    def next_came(j):
        return next_copy(member(l, 4 - j, 0) if j else member(l, 0, 1), j, l)

    def next_on(j):
        return next_copy(member(l, 0, 1), 3 + j, member(l, j, 0))

    def next_diag(j):
        return next_copy(member(l, 4 - j, 1), 3 + j, l)

    for j in range(4):
        next_own(j).start()

    place_l = lax.broadcasted_iota(jnp.int32, (ROWS, ROWS), 1)
    place_s = lax.broadcasted_iota(jnp.int32, (ROWS, ROWS), 0)
    wanted = source[:, pl.ds(pl.multiple_of(r * ROWS, 128), ROWS)]
    owner = jnp.right_shift(wanted * 43691, 21).astype(F32)
    owner_col = jnp.sum(jnp.where(place_l == place_s, owner, 0.0), axis=1, keepdims=True)
    earlier = jnp.logical_and(owner == owner_col, place_l < place_s)
    rank = jnp.sum(jnp.where(earlier, 1.0, 0.0), axis=1, keepdims=True)
    owner_i = owner_col.astype(jnp.int32)
    position = jnp.bitwise_and(owner_i, 7) * 48 + jnp.right_shift(owner_i, 3) * 3 + rank.astype(jnp.int32)
    put[...] = jnp.where(position == place_l, 1.0, 0.0).astype(BF)

    enc_g.settle()
    pre[...] = jnp.broadcast_to(enc_bias[...], (ROWS, LAT))

    def encode(j, _):
        part = pl.ds(pl.multiple_of(j * 1152, 128), 1152)
        pre[...] += jnp.dot(cent[:, part], encf[part, :], preferred_element_type=F32)
        return 0

    lax.fori_loop(0, 4, encode, 0)
    codes[...] = jnp.maximum(pre[...], 0.0).astype(BF)
    dec_g.cross_pair()
    dec_g.cross_ring(2)

    dec_g.settle()

    lat_sum = Scatter(lpart, lrec_a, lrec_y, lrec_b, lrec_p, lrel_a, lrel_b, l, lat_dev, ls_s, ls_r, CH, CH_SUM_A)

    def order(g, i):
        return member(g, (i + 2) % 4, 1 - i // 4)

    def decode(i, _):
        p = order(l, i)
        part = lax.dot_general(decf[chunk(p), :], codes[...], NT, preferred_element_type=F32)
        lpart[p] = part.astype(BF)
        lat_sum.emit(p)

        @pl.when(i == 6)
        def _():
            recon[...] = part - neg_t[...]

        return 0

    lax.fori_loop(0, 5, decode, 0)
    lat_sum.pass_diag()
    lax.fori_loop(5, 8, decode, 0)
    lat_sum.pass_ring()
    lat_sum.pass_on()
    lat_sum.finish(recon)
    err[chunk(l), :] = recon[...].astype(BF)
    err_out[...] = err[chunk(l), :]

    err_g = Gather(err, chunk_at, l, lat_dev, err_s, err_r, CH, CH_A)
    err_g.start()
    gcodes[...] = jnp.full((ROWS, LAT), sparsity_weight, F32)

    def grad_begin(lhs, rhs, p, hold, scale, sib_r, xs, xr):
        other = jnp.dot(lhs[shard(p, 1 - c), :], rhs[...], preferred_element_type=F32)
        sib_s[p] = (other * scale).astype(BF)
        remote(sib_s.at[p], sib_r.at[p], xs.at[p], xr.at[p], sib).start()
        mine = jnp.dot(lhs[shard(p, c), :], rhs[...], preferred_element_type=F32)
        kept[hold] = mine * scale

    def grad_end(p, hold, sib_r, own, scatter, xs, xr):
        remote(sib_s.at[p], sib_r.at[p], xs.at[p], xr.at[p], sib).wait_recv()
        total = kept[hold] + sib_r[p].astype(F32)
        scatter.p[p] = total.astype(BF)
        scatter.emit(p)

        @pl.when(p == q)
        def _():
            own[...] = total

    dec_sum = Scatter(dpart, drec_a, drec_y, drec_b, drec_p, drel_a, drel_b, q, rows_dev, dg_s, dg_r, SH, SH_SUM_A)
    enc_sum = Scatter(epart, erec_a, erec_y, erec_b, erec_p, erel_a, erel_b, q, rows_dev, eg_s, eg_r, SH, SH_SUM_A)

    def error_begin(dm, db, hold):
        p = member(l, dm, db)
        gcodes[...] += lax.dot_general(
            err[chunk(p), :], decf[chunk(p), :], TN, preferred_element_type=F32
        )
        grad_begin(err, codes, p, hold, inv_tokens, dsib_r, dx_s, dx_r)

    def error_end(dm, db, hold):
        grad_end(member(l, dm, db), hold, dsib_r, down, dec_sum, dx_s, dx_r)

    error_begin(0, 0, 0)
    err_g.forward_a()
    err_g.forward_b(1)
    error_end(0, 0, 0)
    err_g.forward_b(3)
    err_g.hear_ring(1)
    err_g.hear_ring(3)
    err_g.take_pair()
    error_begin(0, 1, 1)
    err_g.forward_b(2)
    before = (0, 1)
    for i, (j, db) in enumerate(((1, 0), (3, 0), (2, 0), (1, 1), (3, 1), (2, 1))):
        if db:
            err_g.take_diag(j)
        else:
            err_g.take_ring(j)
        error_begin(4 - j, db, i % 2)
        error_end(*before, (i + 1) % 2)
        before = (4 - j, db)
        if i == 0:
            err_g.hear_diag(1)
            err_g.hear_diag(3)
    error_end(*before, 1)
    next_came(0).wait_recv()
    for j in (1, 3, 2):
        next_on(j).start()
    cgrad[...] = jnp.where(pre[...] > 0, gcodes[...] * inv_tokens, 0.0).astype(BF)

    def drain_cross(p, _):
        remote(sib_s.at[p], dsib_r.at[p], dx_s.at[p], dx_r.at[p], sib).wait_send()
        return 0

    lax.fori_loop(0, 8, drain_cross, 0)

    def enc_step(i, _):
        grad_begin(cent_t, cgrad, order(q, i), i % 2, 1.0, esib_r, ex_s, ex_r)

        @pl.when(i > 0)
        def _():
            grad_end(order(q, i - 1), (i + 1) % 2, esib_r, eown, enc_sum, ex_s, ex_r)

        return 0

    lax.fori_loop(0, 3, enc_step, 0)
    dec_sum.pass_diag()
    lax.fori_loop(3, 5, enc_step, 0)
    dec_sum.pass_ring()
    lax.fori_loop(5, 7, enc_step, 0)
    enc_sum.pass_diag()
    lax.fori_loop(7, 8, enc_step, 0)
    grad_end(order(q, 7), 1, esib_r, eown, enc_sum, ex_s, ex_r)
    enc_sum.pass_ring()
    dec_sum.pass_on()
    enc_sum.pass_on()

    for j in (1, 3, 2):
        next_came(j).wait_recv()
    for j in (1, 3, 2):
        next_diag(j).wait_recv()

    def permute(j, _):
        cols = pl.ds(pl.multiple_of(j * 512, 512), 512)
        batch[:, cols] = jnp.dot(
            put[...], rows48[:, cols], preferred_element_type=F32
        ).astype(BF)
        return 0

    lax.fori_loop(0, 9, permute, 0)
    out_cp = pltpu.make_async_copy(batch, next_out, loc.at[4])
    out_cp.start()

    def update(scatter, own, first, second, outs):
        scatter.finish(own)
        for out, value in zip(outs, adam_update(own[...], first[...], second[...])):
            out[...] = value

    for cp in moment_cps:
        cp.wait()
    update(dec_sum, down, df, ds, (ndf, nds, dup))
    update(enc_sum, eown, ef, es, (nef, nes, eup))

    enc_g.drain()
    dec_g.drain()
    err_g.drain()
    lat_sum.drain()
    dec_sum.drain()
    enc_sum.drain()

    def drain_group(k, _):
        to_group(k).wait_send()
        return 0

    lax.fori_loop(1, 16, drain_group, 0)
    for j in range(4):
        next_own(j).wait_send()
    for j in (1, 2, 3):
        next_on(j).wait_send()

    def drain_cross2(p, _):
        remote(sib_s.at[p], esib_r.at[p], ex_s.at[p], ex_r.at[p], sib).wait_send()
        return 0

    lax.fori_loop(0, 8, drain_cross2, 0)
    out_cp.wait()


def train_step(
    batch, next_acts, encw, decw_t, source, enc_bias, dec_bias, ef, es, df_t, ds_t, inv_tokens
):
    any_space = pl.BlockSpec(memory_space=pl.ANY)
    vmem = pl.BlockSpec(memory_space=pltpu.VMEM)
    dma = pltpu.SemaphoreType.DMA

    def received(size, size_a, width):
        return [
            pltpu.VMEM((8, size, width), BF),
            pltpu.VMEM((4, size_a, width), BF),
            pltpu.VMEM((4, size - size_a, width), BF),
            pltpu.VMEM((2, size - size_a, width), BF),
            pltpu.VMEM((size_a, width), BF),
            pltpu.VMEM((4, size_a // 2, width), BF),
            pltpu.VMEM((2, (size - size_a) // 2, width), BF),
        ]

    shard = jax.ShapeDtypeStruct((SH, LAT), BF)
    return pl.pallas_call(
        functools.partial(step_kernel, inv_tokens),
        out_shape=(
            jax.ShapeDtypeStruct((ROWS, D), BF),
            jax.ShapeDtypeStruct((ROWS, LAT), BF),
            jax.ShapeDtypeStruct((CH, ROWS), BF),
            *([shard] * 6),
        ),
        in_specs=[any_space] * 8 + [vmem] * 3,
        out_specs=[any_space] + [vmem] * 8,
        scratch_shapes=[
            pltpu.VMEM((ROWS, D), BF),
            pltpu.VMEM((ROWS, D), BF),
            pltpu.VMEM((D, ROWS), BF),
            pltpu.VMEM((CH, ROWS), F32),
            pltpu.VMEM((D, LAT), BF),
            pltpu.VMEM((D, LAT), BF),
            pltpu.VMEM((ROWS, LAT), F32),
            pltpu.VMEM((CH, ROWS), F32),
            pltpu.VMEM((D, ROWS), BF),
            pltpu.VMEM((ROWS, LAT), F32),
            pltpu.VMEM((ROWS, LAT), BF),
            *received(CH, CH_SUM_A, ROWS),
            *([pltpu.VMEM((8, SH, LAT), BF)] * 3),
            pltpu.VMEM((2, SH, LAT), F32),
            *received(SH, SH_SUM_A, LAT),
            pltpu.VMEM((SH, LAT), F32),
            *received(SH, SH_SUM_A, LAT),
            pltpu.VMEM((SH, LAT), F32),
            pltpu.VMEM((48, D), BF),
            pltpu.VMEM((48, D), F32),
            pltpu.VMEM((16, 4, D), BF),
            pltpu.VMEM((16, 4, D), BF),
            pltpu.VMEM((ROWS, D), BF),
            pltpu.VMEM((ROWS, ROWS), BF),
            *([pltpu.VMEM((SH, LAT), BF)] * 4),
            dma((9,)),
            dma((22,)), dma((22,)), dma((8,)), dma((8,)),
            dma((22,)), dma((22,)), dma((8,)), dma((8,)),
            dma((22,)), dma((22,)), dma((22,)), dma((22,)),
            dma((8,)), dma((8,)), dma((22,)), dma((22,)),
            dma((8,)), dma((8,)), dma((22,)), dma((22,)),
            dma((15,)), dma((15,)), dma((7,)), dma((7,)),
        ],
        compiler_params=pltpu.CompilerParams(
            collective_id=0, has_side_effects=True, vmem_limit_bytes=63 * 2**20
        ),
        cost_estimate=pl.CostEstimate(
            flops=5 * 2 * ROWS * LAT * D, bytes_accessed=16 * 2**20, transcendentals=0
        ),
    )(batch, next_acts, encw, decw_t, ef, es, df_t, ds_t, source, enc_bias, dec_bias)


def publish(*arrays):
    n = len(arrays)
    pieces = []
    for i, a in enumerate(arrays):
        step = a.shape[0] // 4 if a.size > 2**20 else a.shape[0]
        pieces += [(i, row, step) for row in range(0, a.shape[0], step)]

    def kernel(*refs):
        held, into, out_of = refs[2 * n : 3 * n], refs[3 * n], refs[3 * n + 1]

        def read(k):
            i, row, rows = pieces[k]
            part = pl.ds(row, rows)
            return pltpu.make_async_copy(refs[i].at[part], held[i].at[part], into.at[k])

        def write(k):
            i, row, rows = pieces[k]
            part = pl.ds(row, rows)
            return pltpu.make_async_copy(held[i].at[part], refs[n + i].at[part], out_of.at[k])

        for k in range(len(pieces)):
            read(k).start()
        for k in range(len(pieces)):
            read(k).wait()
            write(k).start()
        for k in range(len(pieces)):
            write(k).wait()

    any_space = pl.BlockSpec(memory_space=pl.ANY)
    return pl.pallas_call(
        kernel,
        out_shape=tuple(jax.ShapeDtypeStruct(a.shape, a.dtype) for a in arrays),
        in_specs=[any_space] * n,
        out_specs=[any_space] * n,
        scratch_shapes=[
            *[pltpu.VMEM(a.shape, a.dtype) for a in arrays],
            pltpu.SemaphoreType.DMA((len(pieces),)),
            pltpu.SemaphoreType.DMA((len(pieces),)),
        ],
        compiler_params=pltpu.CompilerParams(vmem_limit_bytes=63 * 2**20),
    )(*arrays)


def on_device(
    batch, next_acts, row_source, enc_weight, dec_weight, enc_bias, dec_bias,
    enc_first, enc_second, dec_first, dec_second,
):
    inv_tokens = 1.0 / (batch.shape[0] * 16)
    results = train_step(
        batch, next_acts, enc_weight, dec_weight.T, row_source.reshape(1, -1),
        enc_bias.reshape(1, LAT), dec_bias.reshape(D // 128, 128),
        enc_first, enc_second, dec_first.T, dec_second.T, inv_tokens,
    )
    next_batch, codes, err_t, nef, nes, eup, ndf, nds, dup = publish(*results)
    return next_batch, codes, err_t.T, nef, nes, eup, ndf.T, nds.T, dup.T


def solution(mesh):
    return jax.shard_map(
        on_device,
        mesh=mesh,
        in_specs=(
            P("rows", None),
            P(("rows", "lat"), None),
            P(),
            P("rows", "lat"),
            P("lat", "rows"),
            P("lat"),
            P(),
            P("rows", "lat"),
            P("rows", "lat"),
            P("lat", "rows"),
            P("lat", "rows"),
        ),
        out_specs=(
            P("rows", None),
            P("rows", "lat"),
            P("rows", "lat"),
            P("rows", "lat"),
            P("rows", "lat"),
            P("rows", "lat"),
            P("lat", "rows"),
            P("lat", "rows"),
            P("lat", "rows"),
        ),
        check_vma=False,
    )
```
